32 devices in a mesh: seq: 8 (over z, x), head: 4 (over y, core).
Axes of the slice: x: 2, y: 2, z: 4, core: 2. Of those that a mesh axis runs over, the one named last changes fastest.
Arguments:
- block_in: bfloat16 [12288, 1024], P(('seq', 'head')), may hold values from -6 to 6
- out_grad: bfloat16 [12288, 1024], P(('seq', 'head')), may hold values from -6 to 6
- utt_ends: int32 [27], replicated, may hold values from 1 to 12288, as said below
- valid_ends: int32 [27], replicated, may hold values from 1 to 12288, as said below
- ffn1_in: bfloat16 [1024, 4096], P('seq', 'head'), may hold values from -0.1875 to 0.1875
- ffn1_out: bfloat16 [4096, 1024], P('head', 'seq'), may hold values from -0.09375 to 0.09375
- att_qkv: bfloat16 [1024, 3072], P(('seq', 'head')), may hold values from -0.1875 to 0.1875
- att_out: bfloat16 [1024, 1024], P(('seq', 'head')), may hold values from -0.5 to 0.5
- content_bias: bfloat16 [1024], P(('seq', 'head')), may hold values from -3 to 3
- conv_in: bfloat16 [1024, 2048], P(('seq', 'head')), may hold values from -0.1875 to 0.1875
- conv_out: bfloat16 [1024, 1024], P(('seq', 'head')), may hold values from -0.1875 to 0.1875
- ffn2_in: bfloat16 [1024, 4096], P('seq', 'head'), may hold values from -0.1875 to 0.1875
- ffn2_out: bfloat16 [4096, 1024], P('head', 'seq'), may hold values from -0.09375 to 0.09375
- conv_depth: bfloat16 [5, 1024], P(None, ('seq', 'head')), may hold values from -3 to 3
- norm_gain: bfloat16 [6, 1024], P(None, ('seq', 'head')), may hold values from 0.5 to 1.5
- norm_bias: bfloat16 [6, 1024], P(None, ('seq', 'head')), may hold values from -1.75 to 1.75
Outputs:
- block_out: bfloat16 [12288, 1024], P(('seq', 'head'))
- grad_in: bfloat16 [12288, 1024], P(('seq', 'head'))
- grad_ffn1_in: float32 [1024, 4096], P('seq', 'head')
- grad_ffn1_out: float32 [4096, 1024], P('head', 'seq')
- grad_att_qkv: float32 [1024, 3072], P(('seq', 'head'))
- grad_att_out: float32 [1024, 1024], P(('seq', 'head'))
- grad_content_bias: float32 [1024], P(('seq', 'head'))
- grad_conv_in: float32 [1024, 2048], P(('seq', 'head'))
- grad_conv_out: float32 [1024, 1024], P(('seq', 'head'))
- grad_ffn2_in: float32 [1024, 4096], P('seq', 'head')
- grad_ffn2_out: float32 [4096, 1024], P('head', 'seq')
- grad_conv_depth: float32 [5, 1024], P(None, ('seq', 'head'))
- grad_norm_gain: float32 [6, 1024], P(None, ('seq', 'head'))
- grad_norm_bias: float32 [6, 1024], P(None, ('seq', 'head'))
The draws below stay inside these ranges and needn't reach their ends.
Inputs may be any that keep to these rules, and one draw needn't show every extreme that they name: `utt_ends`: Non-decreasing; the utterance u spans frames from the previous entry (0 for the first) to this one; every utterance is shorter than 1536 frames; the final entries equal 12288, the last ones as empty utterances. `valid_ends`: for each utterance, a frame between its start plus one and its end; frames from there to its end are padding.
All inputs are finite; a program needn't handle non-finite values.
Results may differ from the reference program's by a relative error of at most 0.019.
Values may be sent and summed in bfloat16 or wider, within the bound.
No kernel may reach another device: no remote copies, remote signals or barrier semaphores. Data moves between devices by JAX's collectives and lax.ppermute only.
A program may use at most 320 MiB of HBM per device.

```python
import jax
import jax.numpy as jnp
from jax import lax

D = 1024
FF = 4096
HEADS = 8
DH = 128
KSIZE = 5
TOK_DEV = 384
SPAN = 1536
TOKENS = 12288
NUTT = 27


def utterance_bounds(base_key):
    shortest = SPAN * 5 // 16
    longest = SPAN * 25 // 32 + 1
    lengths = jax.random.randint(jax.random.fold_in(base_key, 101), (NUTT,), shortest, longest, dtype=jnp.int32)
    end_frames = jnp.cumsum(lengths).astype(jnp.int32)
    remainder = end_frames % TOK_DEV
    nudge = jnp.where((remainder < 2) | (remainder > TOK_DEV - 2), TOK_DEV // 2, 0).astype(jnp.int32)
    end_frames = jnp.minimum(end_frames + nudge, TOKENS).astype(jnp.int32)
    start_frames = jnp.concatenate([jnp.zeros((1,), jnp.int32), end_frames[:-1]])
    padding = jax.random.randint(jax.random.fold_in(base_key, 102), (NUTT,), 0, (end_frames - start_frames) // 8 + 1, dtype=jnp.int32)
    return (end_frames, (end_frames - padding).astype(jnp.int32))


def draw_utt_ends(key, part):
    return utterance_bounds(key)[0]


def draw_valid_ends(key, part):
    return utterance_bounds(key)[1]


def levels(own_key, extent, split, smallest, largest):
    level = 1.0
    for axis_at, blocks in split:
        heights = jax.random.uniform(jax.random.fold_in(jax.random.fold_in(own_key, 6), axis_at), (blocks,), jnp.float32, smallest / len(split), largest / len(split))
        level = level * jnp.repeat(jnp.exp(heights), extent[axis_at] // blocks).reshape((-1,) + (1,) * (len(extent) - 1 - axis_at))
    return level


def bell_draw(key, dims, scale, limit, pieces=(), kind=jnp.bfloat16):
    array = scale * jax.random.normal(key, dims, jnp.float32)
    if pieces:
        array = array * levels(key, dims, pieces, -0.22, 0.18)
    return jnp.clip(array, -limit, limit).astype(kind)


def setup_inputs(seed: int = 0) -> dict:
    splits = jax.random.split(jax.random.key(seed), 17)
    return {
        "block_in": bell_draw(splits[0], (TOKENS, D), 1.0, 6.0, ((0, 32),)),
        "out_grad": bell_draw(splits[1], (TOKENS, D), 1.0, 6.0, ((0, 32),)),
        "utt_ends": draw_utt_ends(jax.random.fold_in(splits[16], 71), 0),
        "valid_ends": draw_valid_ends(jax.random.fold_in(splits[16], 71), 0),
        "ffn1_in": bell_draw(splits[4], (D, FF), D ** -0.5, 0.1875, ((0, 8), (1, 4))),
        "ffn1_out": bell_draw(splits[5], (FF, D), FF ** -0.5, 0.09375, ((0, 4), (1, 8))),
        "att_qkv": bell_draw(splits[6], (D, 3 * D), D ** -0.5, 0.1875, ((0, 32),)),
        "att_out": bell_draw(splits[7], (D, D), (D // 8) ** -0.5, 0.5, ((0, 32),)),
        "content_bias": bell_draw(splits[8], (D,), 0.5, 3.0, ((0, 32),)),
        "conv_in": bell_draw(splits[9], (D, 2 * D), D ** -0.5, 0.1875, ((0, 32),)),
        "conv_out": bell_draw(splits[10], (D, D), D ** -0.5, 0.1875, ((0, 32),)),
        "ffn2_in": bell_draw(splits[11], (D, FF), D ** -0.5, 0.1875, ((0, 8), (1, 4))),
        "ffn2_out": bell_draw(splits[12], (FF, D), FF ** -0.5, 0.09375, ((0, 4), (1, 8))),
        "conv_depth": bell_draw(splits[13], (KSIZE, D), 0.5, 3.0, ((1, 32),)),
        "norm_gain": jnp.clip(1.0 + 0.1 * jax.random.normal(splits[14], (6, D), jnp.float32), 0.5, 1.5).astype(jnp.bfloat16),
        "norm_bias": bell_draw(splits[15], (6, D), 0.3, 1.75, ((1, 32),)),
    }


@jax.custom_vjp
def low(v):
    return lax.optimization_barrier(v.astype(jnp.bfloat16)).astype(jnp.float32)

@jax.custom_vjp
def low_back(v):
    return v

def low_keep(v):
    return (low(v), None)

def low_pass(kept, grad):
    return (grad,)

def back_keep(v):
    return (v, None)

def back_low(kept, grad):
    return (low(grad),)
low.defvjp(low_keep, low_pass)
low_back.defvjp(back_keep, back_low)
EPSILON = 1e-05
MASKED = -1e+30
HIGHEST = lax.Precision.HIGHEST

def matmul(left_side, right_side):
    return jnp.dot(left_side, right_side, precision=HIGHEST)

def layer_norm(values, norm_gains, shifts):
    centred = values - lax.optimization_barrier(jnp.mean(values, axis=-1, keepdims=True))
    variance = lax.optimization_barrier(jnp.mean(centred * centred, axis=-1, keepdims=True))
    return centred * lax.rsqrt(variance + EPSILON) * norm_gains + shifts

def frame_segments(end_frames, valid_frames):
    positions = jnp.arange(TOKENS, dtype=jnp.int32)
    segment = jnp.searchsorted(end_frames, positions, side='right').astype(jnp.int32)
    valid_seg = jnp.searchsorted(valid_frames, positions, side='right').astype(jnp.int32)
    return (segment, segment == valid_seg)

def feed_forward(values, w_in, w_out, norm_gains, shifts):
    normed = layer_norm(values, norm_gains, shifts)
    hidden = low_back(matmul(low(normed), w_in))
    return low_back(matmul(low(jax.nn.silu(hidden)), w_out))

def attention(queries, key_vals, value_vals, segment, valid):
    all_frames = queries.shape[0]
    block_rows = min(512, SPAN)
    window = block_rows + 2 * SPAN
    keys_pad = jnp.pad(key_vals, ((SPAN, SPAN), (0, 0)))
    values_pad = jnp.pad(value_vals, ((SPAN, SPAN), (0, 0)))
    seg_pad = jnp.pad(segment, (SPAN, SPAN), constant_values=-1)
    valid_pad = jnp.pad(valid, (SPAN, SPAN), constant_values=False)
    slopes = 32.0 * jnp.exp2(-jnp.arange(HEADS).astype(jnp.float32))
    score_scale = DH ** (-0.5)

    def one_block(row_start):
        q_rows = lax.dynamic_slice_in_dim(queries, row_start, block_rows, 0).reshape(block_rows, HEADS, DH)
        k_rows = lax.dynamic_slice_in_dim(keys_pad, row_start, window, 0).reshape(window, HEADS, DH)
        v_rows = lax.dynamic_slice_in_dim(values_pad, row_start, window, 0).reshape(window, HEADS, DH)
        q_seg = lax.dynamic_slice_in_dim(segment, row_start, block_rows, 0)
        k_seg = lax.dynamic_slice_in_dim(seg_pad, row_start, window, 0)
        k_valid = lax.dynamic_slice_in_dim(valid_pad, row_start, window, 0)
        raw = low_back(jnp.einsum('qhd,khd->hqk', q_rows, k_rows, precision=HIGHEST) * score_scale)
        q_pos = row_start + jnp.arange(block_rows, dtype=jnp.int32)
        k_pos = row_start - SPAN + jnp.arange(window, dtype=jnp.int32)
        distance = jnp.abs(q_pos[:, None] - k_pos[None, :]).astype(jnp.float32)
        allowed = (q_seg[:, None] == k_seg[None, :]) & k_valid[None, :]
        scores = jnp.where(allowed[None], raw - slopes[:, None, None] * distance[None] / SPAN, MASKED)
        probabilities = jax.nn.softmax(scores, axis=-1)
        mixed = jnp.einsum('hqk,khd->qhd', low(probabilities), v_rows, precision=HIGHEST)
        return mixed.reshape(block_rows, D)
    row_starts = jnp.arange(all_frames // block_rows, dtype=jnp.int32) * block_rows
    return lax.map(jax.checkpoint(one_block), row_starts).reshape(all_frames, D)

def forward(params, inputs, segment, valid, valid_count):
    w_f1i, w_f1o, w_qkv, w_att, u_bias, w_cin, w_cout, w_f2i, w_f2o, w_depth, norm_gains, shifts = params
    all_frames = inputs.shape[0]
    after_ffn1 = inputs + 0.5 * feed_forward(inputs, w_f1i, w_f1o, norm_gains[0], shifts[0])
    attn_normed = layer_norm(after_ffn1, norm_gains[1], shifts[1])
    projected = low_back(matmul(low(attn_normed), w_qkv))
    queries = low(projected[:, :D] + u_bias)
    key_vals = low(projected[:, D:2 * D])
    value_vals = low(projected[:, 2 * D:])
    mixed = attention(queries, key_vals, value_vals, segment, valid)
    after_attn = after_ffn1 + low_back(matmul(low(low_back(mixed)), w_att))
    conv_normed = layer_norm(after_attn, norm_gains[2], shifts[2])
    pointwise = low_back(matmul(low(conv_normed), w_cin))
    valid_col = valid.astype(jnp.float32)[:, None]
    gated = low(pointwise[:, :D] * jax.nn.sigmoid(pointwise[:, D:]) * valid_col)
    conv_reach = (KSIZE - 1) // 2
    gated_pad = jnp.pad(gated, ((conv_reach, conv_reach), (0, 0)))
    seg_pad = jnp.pad(segment, (conv_reach, conv_reach), constant_values=-1)
    conv_sum = jnp.zeros_like(gated)
    for offset in range(KSIZE):
        same_seg = (seg_pad[offset:offset + all_frames] == segment).astype(jnp.float32)
        conv_sum = conv_sum + w_depth[offset] * gated_pad[offset:offset + all_frames] * same_seg[:, None]
    conv_sum = low_back(conv_sum)
    mean_c = lax.optimization_barrier(jnp.sum(valid_col * conv_sum, axis=0)) / valid_count
    variance_c = lax.optimization_barrier(jnp.sum(valid_col * conv_sum * conv_sum, axis=0)) / valid_count - mean_c * mean_c
    batch_out = (conv_sum - mean_c) * lax.rsqrt(variance_c + EPSILON) * norm_gains[3] + shifts[3]
    after_conv = after_attn + low_back(matmul(low(jax.nn.silu(batch_out)), w_cout))
    after_ffn2 = after_conv + 0.5 * feed_forward(after_conv, w_f2i, w_f2o, norm_gains[4], shifts[4])
    return layer_norm(after_ffn2, norm_gains[5], shifts[5])

def reference(block_in, out_grad, utt_ends, valid_ends, ffn1_in, ffn1_out, att_qkv, att_out, content_bias, conv_in, conv_out, ffn2_in, ffn2_out, conv_depth, norm_gain, norm_bias):
    segment, valid = frame_segments(utt_ends, valid_ends)
    valid_count = jnp.sum(valid.astype(jnp.float32))
    params = (ffn1_in.astype(jnp.float32), ffn1_out.astype(jnp.float32), att_qkv.astype(jnp.float32), att_out.astype(jnp.float32), content_bias.astype(jnp.float32), conv_in.astype(jnp.float32), conv_out.astype(jnp.float32), ffn2_in.astype(jnp.float32), ffn2_out.astype(jnp.float32), conv_depth.astype(jnp.float32), norm_gain.astype(jnp.float32), norm_bias.astype(jnp.float32))

    def layer(weights, inputs):
        return forward(weights, inputs, segment, valid, valid_count)
    output, pullback = jax.vjp(layer, params, block_in.astype(jnp.float32))
    grad_params, grad_input = pullback(out_grad.astype(jnp.float32))
    return (output.astype(jnp.bfloat16), grad_input.astype(jnp.bfloat16), grad_params[0], grad_params[1], grad_params[2], grad_params[3], grad_params[4], grad_params[5], grad_params[6], grad_params[7], grad_params[8], grad_params[9], grad_params[10], grad_params[11])
```

```python
import math

import jax
import jax.numpy as jnp
from jax import lax
from jax.experimental import pallas as pl
from jax.experimental.pallas import tpu as pltpu
from jax.sharding import Mesh
from jax.sharding import PartitionSpec as P

DH = 128
KSIZE = 5
REACH = (KSIZE - 1) // 2
EPSILON = 1e-05
MASKED = -1e30
LOG2E = math.log2(math.e)
DEV = ("z", "x", "y", "c")
LAYER = ("x", "y", "c")
WIDE = ("y", "c", "z", "x")
BQ = 256
BK = 512
BF = jnp.bfloat16
F32 = jnp.float32
VMEM_BYTES = 56 * 1024 * 1024


def pick(cells, index, dim):
    return lax.dynamic_index_in_dim(cells, index, dim, keepdims=False)


def xor_send(cells, axis, bit):
    count = lax.axis_size(axis)
    return lax.ppermute(cells, axis, [(i, i ^ bit) for i in range(count)])


def neighbour_rows(cells):
    count = 1
    for axis in DEV:
        count *= lax.axis_size(axis)
    before = lax.ppermute(cells[-REACH:], DEV, [(i, i + 1) for i in range(count - 1)])
    after = lax.ppermute(cells[:REACH], DEV, [(i + 1, i) for i in range(count - 1)])
    return jnp.concatenate([before, cells, after], axis=0)


def sum_everywhere(rows):
    count = 1
    for axis in DEV:
        count *= lax.axis_size(axis)
    spread = jnp.broadcast_to(rows[None], (count,) + rows.shape)
    return jnp.sum(lax.all_to_all(spread, DEV, split_axis=0, concat_axis=0, tiled=True), axis=0)


def dot_nn(a, b):
    return lax.dot_general(a, b, (((1,), (0,)), ((), ())), preferred_element_type=F32)


def dot_nt(a, b):
    return lax.dot_general(a, b, (((1,), (1,)), ((), ())), preferred_element_type=F32)


def dot_tn(a, b):
    return lax.dot_general(a, b, (((0,), (0,)), ((), ())), preferred_element_type=F32)


def norm_stats(values):
    centred = values - jnp.mean(values, axis=-1, keepdims=True)
    inv_std = lax.rsqrt(jnp.mean(centred * centred, axis=-1, keepdims=True) + EPSILON)
    return centred * inv_std, inv_std


def norm_back(upstream, normed, inv_std, gain):
    scaled = upstream * gain
    inner = (
        scaled
        - jnp.mean(scaled, axis=-1, keepdims=True)
        - normed * jnp.mean(scaled * normed, axis=-1, keepdims=True)
    )
    return inv_std * inner


def ffn_fwd_kernel(x_ref, w_ref, vec_ref, x1_ref, n_ref, s_ref, d_ref, n2_ref, acc_ref):
    step = pl.program_id(0)
    width = x_ref.shape[1]

    @pl.when(step == 0)
    def _():
        normed, _ = norm_stats(x_ref[...].astype(F32))
        n_ref[...] = (normed * vec_ref[0:1, :] + vec_ref[1:2, :]).astype(BF)
        acc_ref[...] = jnp.zeros_like(acc_ref)

    chunk = 256
    for at in range(0, width, chunk):
        a = dot_nn(n_ref[...], w_ref[0, :, at : at + chunk])
        sig = jax.nn.sigmoid(a)
        s_ref[0, :, at : at + chunk] = (a * sig).astype(BF)
        d_ref[0, :, at : at + chunk] = (sig * (1.0 + a * (1.0 - sig))).astype(BF)
    acc_ref[...] += dot_nt(s_ref[0], w_ref[0, :, width:])

    @pl.when(step == pl.num_programs(0) - 1)
    def _():
        x1 = x_ref[...].astype(F32) + 0.5 * acc_ref[...]
        x1_ref[...] = x1
        normed, _ = norm_stats(x1)
        n2_ref[...] = (normed * vec_ref[2:3, :] + vec_ref[3:4, :]).astype(BF)


def ffn_fwd(x, w, vectors):
    frames, width = x.shape
    blocks = w.shape[0]
    whole = lambda j: (0, 0)
    slab = lambda j: (j, 0, 0)
    return pl.pallas_call(
        ffn_fwd_kernel,
        grid=(blocks,),
        in_specs=[
            pl.BlockSpec((frames, width), whole),
            pl.BlockSpec((1, width, 2 * width), slab),
            pl.BlockSpec(vectors.shape, whole),
        ],
        out_specs=[
            pl.BlockSpec((frames, width), whole),
            pl.BlockSpec((frames, width), whole),
            pl.BlockSpec((1, frames, width), slab),
            pl.BlockSpec((1, frames, width), slab),
            pl.BlockSpec((frames, width), whole),
        ],
        out_shape=[
            jax.ShapeDtypeStruct((frames, width), F32),
            jax.ShapeDtypeStruct((frames, width), BF),
            jax.ShapeDtypeStruct((blocks, frames, width), BF),
            jax.ShapeDtypeStruct((blocks, frames, width), BF),
            jax.ShapeDtypeStruct((frames, width), BF),
        ],
        scratch_shapes=[pltpu.VMEM((frames, width), F32)],
        compiler_params=pltpu.CompilerParams(vmem_limit_bytes=VMEM_BYTES),
        cost_estimate=pl.CostEstimate(
            flops=4 * frames * width * width * blocks,
            bytes_accessed=4 * width * width * blocks + 8 * frames * width * blocks,
            transcendentals=frames * width * blocks,
        ),
        name="ffn_forward",
    )(x, w, vectors)


def ffn_last_kernel(
    x_ref, w_ref, vec_ref, og_ref, out_ref, n_ref, s_ref, d_ref, dx_ref, sums_ref, acc_ref
):
    step = pl.program_id(0)
    width = x_ref.shape[1]

    @pl.when(step == 0)
    def _():
        normed, _ = norm_stats(x_ref[...])
        n_ref[...] = (normed * vec_ref[0:1, :] + vec_ref[1:2, :]).astype(BF)
        acc_ref[...] = jnp.zeros_like(acc_ref)

    chunk = 256
    for at in range(0, width, chunk):
        a = dot_nn(n_ref[...], w_ref[0, :, at : at + chunk])
        sig = jax.nn.sigmoid(a)
        s_ref[0, :, at : at + chunk] = (a * sig).astype(BF)
        d_ref[0, :, at : at + chunk] = (sig * (1.0 + a * (1.0 - sig))).astype(BF)
    acc_ref[...] += dot_nt(s_ref[0], w_ref[0, :, width:])

    @pl.when(step == pl.num_programs(0) - 1)
    def _():
        x4 = x_ref[...] + 0.5 * acc_ref[...]
        normed, inv_std = norm_stats(x4)
        gain = vec_ref[2:3, :]
        out_ref[...] = (normed * gain + vec_ref[3:4, :]).astype(BF)
        upstream = og_ref[...].astype(F32)
        dx_ref[...] = norm_back(upstream, normed, inv_std, gain)
        sums_ref[0:1, :] = jnp.sum(upstream * normed, axis=0, keepdims=True)
        sums_ref[1:2, :] = jnp.sum(upstream, axis=0, keepdims=True)


def ffn_last(x, w, vectors, out_grad):
    frames, width = x.shape
    blocks = w.shape[0]
    whole = lambda j: (0, 0)
    slab = lambda j: (j, 0, 0)
    return pl.pallas_call(
        ffn_last_kernel,
        grid=(blocks,),
        in_specs=[
            pl.BlockSpec((frames, width), whole),
            pl.BlockSpec((1, width, 2 * width), slab),
            pl.BlockSpec(vectors.shape, whole),
            pl.BlockSpec((frames, width), whole),
        ],
        out_specs=[
            pl.BlockSpec((frames, width), whole),
            pl.BlockSpec((frames, width), whole),
            pl.BlockSpec((1, frames, width), slab),
            pl.BlockSpec((1, frames, width), slab),
            pl.BlockSpec((frames, width), whole),
            pl.BlockSpec((2, width), whole),
        ],
        out_shape=[
            jax.ShapeDtypeStruct((frames, width), BF),
            jax.ShapeDtypeStruct((frames, width), BF),
            jax.ShapeDtypeStruct((blocks, frames, width), BF),
            jax.ShapeDtypeStruct((blocks, frames, width), BF),
            jax.ShapeDtypeStruct((frames, width), F32),
            jax.ShapeDtypeStruct((2, width), F32),
        ],
        scratch_shapes=[pltpu.VMEM((frames, width), F32)],
        compiler_params=pltpu.CompilerParams(vmem_limit_bytes=VMEM_BYTES),
        cost_estimate=pl.CostEstimate(
            flops=4 * frames * width * width * blocks,
            bytes_accessed=4 * width * width * blocks + 8 * frames * width * blocks,
            transcendentals=frames * width * blocks,
        ),
        name="ffn_last",
    )(x, w, vectors, out_grad)


def ffn_bwd_kernel(up_ref, x_ref, w_ref, d_ref, vec_ref, ef_ref, da_ref, dx_ref, sums_ref, acc_ref):
    step = pl.program_id(0)
    width = up_ref.shape[1]

    @pl.when(step == 0)
    def _():
        ef_ref[...] = (0.5 * up_ref[...]).astype(BF)
        acc_ref[...] = jnp.zeros_like(acc_ref)

    chunk = 256
    for at in range(0, width, chunk):
        ds = dot_nn(ef_ref[...], w_ref[0, :, width + at : width + at + chunk])
        da_ref[0, :, at : at + chunk] = (ds * d_ref[0, :, at : at + chunk].astype(F32)).astype(BF)
    acc_ref[...] += dot_nt(da_ref[0], w_ref[0, :, :width])

    @pl.when(step == pl.num_programs(0) - 1)
    def _():
        normed, inv_std = norm_stats(x_ref[...].astype(F32))
        dn = acc_ref[...]
        dx = up_ref[...] + norm_back(dn, normed, inv_std, vec_ref[0:1, :])
        dx_ref[...] = dx.astype(dx_ref.dtype)
        sums_ref[0:1, :] = jnp.sum(dn * normed, axis=0, keepdims=True)
        sums_ref[1:2, :] = jnp.sum(dn, axis=0, keepdims=True)


def ffn_bwd(upstream, x, w, slope, vectors, out_type):
    frames, width = upstream.shape
    blocks = w.shape[0]
    whole = lambda j: (0, 0)
    slab = lambda j: (j, 0, 0)
    return pl.pallas_call(
        ffn_bwd_kernel,
        grid=(blocks,),
        in_specs=[
            pl.BlockSpec((frames, width), whole),
            pl.BlockSpec((frames, width), whole),
            pl.BlockSpec((1, width, 2 * width), slab),
            pl.BlockSpec((1, frames, width), slab),
            pl.BlockSpec(vectors.shape, whole),
        ],
        out_specs=[
            pl.BlockSpec((frames, width), whole),
            pl.BlockSpec((1, frames, width), slab),
            pl.BlockSpec((frames, width), whole),
            pl.BlockSpec((2, width), whole),
        ],
        out_shape=[
            jax.ShapeDtypeStruct((frames, width), BF),
            jax.ShapeDtypeStruct((blocks, frames, width), BF),
            jax.ShapeDtypeStruct((frames, width), out_type),
            jax.ShapeDtypeStruct((2, width), F32),
        ],
        scratch_shapes=[pltpu.VMEM((frames, width), F32)],
        compiler_params=pltpu.CompilerParams(vmem_limit_bytes=VMEM_BYTES),
        cost_estimate=pl.CostEstimate(
            flops=4 * frames * width * width * blocks,
            bytes_accessed=4 * width * width * blocks + 4 * frames * width * blocks,
            transcendentals=0,
        ),
        name="ffn_backward",
    )(upstream, x, w, slope, vectors)


def attn_fwd_kernel(origin, low_ref, high_ref, c2_ref, q_ref, kv_ref, lo_ref, hi_ref, o_ref, lse_ref):
    block = pl.program_id(0)
    rows = q_ref.shape[0]
    q = q_ref[...]
    c1 = LOG2E * DH**-0.5
    c2 = c2_ref[0]
    at = lax.broadcasted_iota(jnp.int32, (1, rows), 1) + (origin + block * rows)
    q_pos = at.astype(F32)
    lo_q, hi_q = lo_ref[...], hi_ref[...]
    first = low_ref[block]
    steps = (high_ref[block] - first + (BK - 1)) // BK

    def step(t, carry):
        top, total, mixed = carry
        start = pl.multiple_of(first + t * BK, 128)
        k = kv_ref[pl.ds(start, BK), :DH]
        v = kv_ref[pl.ds(start, BK), DH:]
        k_pos = (lax.broadcasted_iota(jnp.int32, (BK, 1), 0) + start).astype(F32)
        scores = dot_nt(k, q) * c1 - jnp.abs(k_pos - q_pos) * c2
        scores = jnp.where((k_pos >= lo_q) & (k_pos < hi_q), scores, MASKED)
        new_top = jnp.maximum(top, jnp.max(scores, axis=0, keepdims=True))
        expo = jnp.exp2(scores - new_top)
        keep = jnp.exp2(top - new_top)
        total = total * keep + jnp.sum(expo, axis=0, keepdims=True)
        mixed = mixed * keep + dot_tn(v, expo.astype(BF))
        return new_top, total, mixed

    top, total, mixed = lax.fori_loop(
        0,
        steps,
        step,
        (
            jnp.full((1, rows), MASKED, F32),
            jnp.zeros((1, rows), F32),
            jnp.zeros((DH, rows), F32),
        ),
    )
    o_ref[...] = (mixed / total).T.astype(BF)
    lse_ref[...] = top + jnp.log2(total)


def attn_fwd(q, kv, low, high, c2, lo_q, hi_q, origin):
    frames = q.shape[0]
    blocks = frames // BQ
    pairs = frames * 1024 * DH
    grid_spec = pltpu.PrefetchScalarGridSpec(
        num_scalar_prefetch=3,
        grid=(blocks,),
        in_specs=[
            pl.BlockSpec((BQ, DH), lambda i, *_: (i, 0)),
            pl.BlockSpec(kv.shape, lambda i, *_: (0, 0)),
            pl.BlockSpec((1, BQ), lambda i, *_: (0, i)),
            pl.BlockSpec((1, BQ), lambda i, *_: (0, i)),
        ],
        out_specs=[
            pl.BlockSpec((BQ, DH), lambda i, *_: (i, 0)),
            pl.BlockSpec((1, BQ), lambda i, *_: (0, i)),
        ],
    )

    def kernel(*refs):
        attn_fwd_kernel(origin, *refs)

    return pl.pallas_call(
        kernel,
        grid_spec=grid_spec,
        out_shape=[
            jax.ShapeDtypeStruct((frames, DH), BF),
            jax.ShapeDtypeStruct((1, frames), F32),
        ],
        compiler_params=pltpu.CompilerParams(vmem_limit_bytes=VMEM_BYTES),
        cost_estimate=pl.CostEstimate(
            flops=4 * pairs, bytes_accessed=4 * kv.size, transcendentals=frames * 1024
        ),
        name="attention_forward",
    )(low, high, c2, q, kv, lo_q, hi_q)


def attn_bwd_kernel(
    origin,
    low_ref,
    high_ref,
    c2_ref,
    q_ref,
    o_ref,
    do_ref,
    lse_ref,
    lo_ref,
    hi_ref,
    kv_ref,
    dq_ref,
    prev_ref,
    own_ref,
    next_ref,
    dk_acc,
    dv_acc,
):
    block = pl.program_id(0)
    rows = q_ref.shape[0]
    frames = own_ref.shape[0]
    scale = DH**-0.5
    c1 = LOG2E * scale

    @pl.when(block == 0)
    def _():
        dk_acc[...] = jnp.zeros_like(dk_acc)
        dv_acc[...] = jnp.zeros_like(dv_acc)

    q = q_ref[...]
    do = do_ref[...]
    c2 = c2_ref[0]
    delta = jnp.sum((o_ref[...].astype(F32) * do.astype(F32)).T, axis=0, keepdims=True)
    lse = lse_ref[...]
    at = lax.broadcasted_iota(jnp.int32, (1, rows), 1) + (origin + block * rows)
    q_pos = at.astype(F32)
    lo_q, hi_q = lo_ref[...], hi_ref[...]
    first = low_ref[block]
    steps = (high_ref[block] - first + (BK - 1)) // BK

    def step(t, dq):
        start = pl.multiple_of(first + t * BK, 128)
        here = pl.ds(start, BK)
        k = kv_ref[here, :DH]
        v = kv_ref[here, DH:]
        k_pos = (lax.broadcasted_iota(jnp.int32, (BK, 1), 0) + start).astype(F32)
        scores = dot_nt(k, q) * c1 - jnp.abs(k_pos - q_pos) * c2 - lse
        scores = jnp.where((k_pos >= lo_q) & (k_pos < hi_q), scores, MASKED)
        probs = jnp.exp2(scores)
        grads = (probs * (dot_nt(v, do) - delta)).astype(BF)
        dv_acc[here, :] += dot_nn(probs.astype(BF), do)
        dk_acc[here, :] += dot_nn(grads, q)
        return dq + dot_tn(k, grads)

    dq = lax.fori_loop(0, steps, step, jnp.zeros((DH, rows), F32))
    dq_ref[...] = (dq * scale).T.astype(BF)

    @pl.when(block == pl.num_programs(0) - 1)
    def _():
        prev_ref[:, :DH] = (dk_acc[:origin, :] * scale).astype(BF)
        prev_ref[:, DH:] = dv_acc[:origin, :].astype(BF)
        own_ref[:, :DH] = dk_acc[origin : origin + frames, :] * scale
        own_ref[:, DH:] = dv_acc[origin : origin + frames, :]
        next_ref[:, :DH] = (dk_acc[origin + frames : 2 * origin + frames, :] * scale).astype(BF)
        next_ref[:, DH:] = dv_acc[origin + frames : 2 * origin + frames, :].astype(BF)


def attn_bwd(q, o, do, lse, kv, low, high, c2, lo_q, hi_q, origin):
    frames = q.shape[0]
    blocks = frames // BQ
    pairs = frames * 1024 * DH
    tile = pl.BlockSpec((BQ, DH), lambda i, *_: (i, 0))
    row = pl.BlockSpec((1, BQ), lambda i, *_: (0, i))
    grid_spec = pltpu.PrefetchScalarGridSpec(
        num_scalar_prefetch=3,
        grid=(blocks,),
        in_specs=[
            tile,
            tile,
            tile,
            row,
            row,
            row,
            pl.BlockSpec(kv.shape, lambda i, *_: (0, 0)),
        ],
        out_specs=[
            tile,
            pl.BlockSpec((origin, 2 * DH), lambda i, *_: (0, 0)),
            pl.BlockSpec((frames, 2 * DH), lambda i, *_: (0, 0)),
            pl.BlockSpec((origin, 2 * DH), lambda i, *_: (0, 0)),
        ],
        scratch_shapes=[
            pltpu.VMEM((kv.shape[0], DH), F32),
            pltpu.VMEM((kv.shape[0], DH), F32),
        ],
    )

    def kernel(*refs):
        attn_bwd_kernel(origin, *refs)

    return pl.pallas_call(
        kernel,
        grid_spec=grid_spec,
        out_shape=[
            jax.ShapeDtypeStruct((frames, DH), BF),
            jax.ShapeDtypeStruct((origin, 2 * DH), BF),
            jax.ShapeDtypeStruct((frames, 2 * DH), F32),
            jax.ShapeDtypeStruct((origin, 2 * DH), BF),
        ],
        compiler_params=pltpu.CompilerParams(vmem_limit_bytes=VMEM_BYTES),
        cost_estimate=pl.CostEstimate(
            flops=10 * pairs, bytes_accessed=8 * kv.size, transcendentals=frames * 1024
        ),
        name="attention_backward",
    )(low, high, c2, q, o, do, lse, lo_q, hi_q, kv)


def halve(send, keep, axis, bit):
    return keep.astype(F32) + xor_send(send, axis, bit).astype(F32)


def finish_over_z(part):
    place = lax.axis_index("z")
    bit = 1
    while part.shape[0] > 1:
        pairs = part.reshape((part.shape[0] // 2, 2) + part.shape[1:])
        mine = (place // bit) % 2
        send = pick(pairs, 1 - mine, 1).astype(BF)
        part = halve(send, pick(pairs, mine, 1), "z", bit)
        bit *= 2
    return part[0]


def pair_up(cells):
    return xor_send(cells, "c", 1)


def ffn_grads(left, right, first):
    zs, xs = lax.axis_size("z"), lax.axis_size("x")
    width = left.shape[-1]
    rows = width // (zs * xs)
    x, y = lax.axis_index("x"), lax.axis_index("y")
    hidden = right.shape[-1]

    def product(one_x, one_y):
        lhs = left if one_x is None else pick(left.reshape(2, -1, zs, xs, rows), one_x, 3)
        lhs = lhs.reshape(2, lhs.shape[1], -1)
        out = [
            dot_tn(lhs[0], right[0, j]) + dot_tn(lhs[1], right[1, j])
            for j in range(right.shape[1])
        ] if one_y is None else None
        if one_y is not None:
            rhs = pick(right, one_y, 1)
            return dot_tn(lhs[0], rhs[0]) + dot_tn(lhs[1], rhs[1])
        return jnp.stack(out)

    if first == "x":
        part = halve(product(1 - x, None).astype(BF), product(x, None), "x", 1)
        part = halve(pick(part, 1 - y, 0).astype(BF), pick(part, y, 0), "y", 1)
    else:
        part = halve(product(None, 1 - y).astype(BF), product(None, y), "y", 1)
        part = part.reshape(zs, xs, rows, hidden)
        part = halve(pick(part, 1 - x, 1).astype(BF), pick(part, x, 1), "x", 1)
    return finish_over_z(part.reshape(zs, rows, hidden))


def row_grads(whole):
    zs = lax.axis_size("z")
    x, y, c = lax.axis_index("x"), lax.axis_index("y"), lax.axis_index("c")
    rows = whole.shape[0] // (8 * zs)
    part = whole.reshape(zs, 2, 2, 2, rows, whole.shape[1])
    part = halve(pick(part, 1 - c, 3).astype(BF), pick(part, c, 3), "c", 1)
    part = halve(pick(part, 1 - x, 1).astype(BF), pick(part, x, 1), "x", 1)
    part = halve(pick(part, 1 - y, 1).astype(BF), pick(part, y, 1), "y", 1)
    return finish_over_z(part)


def body(
    block_in,
    out_grad,
    utt_ends,
    valid_ends,
    ffn1_in,
    ffn1_out,
    att_qkv,
    att_out,
    content_bias,
    conv_in,
    conv_out,
    ffn2_in,
    ffn2_out,
    conv_depth,
    norm_gain,
    norm_bias,
):
    zs = lax.axis_size("z")
    devices = 8 * zs
    frames, width = block_in.shape
    heads = width // DH
    z, x, y, c = (lax.axis_index(axis) for axis in DEV)
    place = ((z * 2 + x) * 2 + y) * 2 + c
    head = (x * 2 + y) * 2 + c

    small = jnp.concatenate([norm_gain, norm_bias, conv_depth, content_bias[None]], axis=0)
    small = jnp.broadcast_to(small[None], (devices,) + small.shape)
    small = lax.all_to_all(small, DEV, split_axis=0, concat_axis=0, tiled=True)
    small = small.transpose(1, 0, 2).reshape(small.shape[1], width).astype(F32)
    gains, shifts, taps, q_bias = small[:6], small[6:12], small[12 : 12 + KSIZE], small[12 + KSIZE]

    def gather_ffn(w_in, w_out):
        both = jnp.concatenate([w_in, w_out.T], axis=1)
        return lax.all_gather(both, WIDE, axis=0, tiled=True).reshape(4, width, 2 * width)

    w_f1 = gather_ffn(ffn1_in, ffn1_out)
    w_qkv = lax.all_gather(att_qkv, DEV, axis=0, tiled=True)
    w_mid = lax.all_gather(jnp.concatenate([att_out, conv_in, conv_out], axis=1), DEV, axis=0, tiled=True)
    w_f2 = gather_ffn(ffn2_in, ffn2_out)
    w_att, w_cin, w_cout = w_mid[:, :width], w_mid[:, width : 3 * width], w_mid[:, 3 * width :]

    all_frames = frames * devices
    first_frame = place * frames
    span = 4 * frames
    group = 8 * frames
    origin = span
    group_first = z * group
    starts = jnp.concatenate([jnp.zeros((1,), jnp.int32), utt_ends[:-1]])
    valid_count = jnp.sum((valid_ends - starts).astype(F32))

    def segments(positions):
        seg = jnp.sum((utt_ends[None, :] <= positions[:, None]).astype(jnp.int32), axis=1)
        valid_seg = jnp.sum((valid_ends[None, :] <= positions[:, None]).astype(jnp.int32), axis=1)
        valid = seg == valid_seg
        return jnp.where(positions < 0, -1, jnp.where(positions >= all_frames, -2, seg)), valid

    ext_seg, ext_valid = segments(
        first_frame - REACH + jnp.arange(frames + 2 * REACH, dtype=jnp.int32)
    )
    own_seg = ext_seg[REACH : REACH + frames]
    valid_col = ext_valid[REACH : REACH + frames].astype(F32)[:, None]
    masks = [
        (ext_seg[m : m + frames] == own_seg).astype(F32)[:, None] for m in range(KSIZE)
    ]
    group_pos = group_first + jnp.arange(group, dtype=jnp.int32)
    ended = utt_ends[None, :] <= group_pos[:, None]
    group_seg = jnp.sum(ended.astype(jnp.int32), axis=1)
    group_lo = jnp.max(jnp.where(ended, utt_ends[None, :], 0), axis=1)
    slots = jnp.arange(utt_ends.shape[0], dtype=jnp.int32)
    group_hi = jnp.sum(
        jnp.where(group_seg[:, None] == slots[None, :], valid_ends[None, :], 0), axis=1
    )
    window_first = group_first - origin
    lo_q = group_lo - window_first
    hi_q = group_hi - window_first
    low = (lo_q[::BQ] // 128) * 128
    high = hi_q[BQ - 1 :: BQ]
    lo_q = lo_q.astype(F32)[None, :]
    hi_q = hi_q.astype(F32)[None, :]
    c2 = (32.0 * jnp.exp2(-head.astype(F32)) * (LOG2E / span))[None]

    def vectors(*rows):
        rows = jnp.stack(rows)
        return jnp.concatenate([rows, jnp.zeros((8 - rows.shape[0], width), F32)], axis=0)

    x1, n0, s1, d1, n2 = ffn_fwd(
        block_in, w_f1, vectors(gains[0], shifts[0], gains[1], shifts[1])
    )

    def for_sibling(first, slabs):
        theirs = pick(slabs.reshape((2, 2) + slabs.shape[1:]), 1 - c, 1)
        got = pair_up(jnp.concatenate([first[None], theirs], axis=0))
        own = pick(slabs.reshape((2, 2) + slabs.shape[1:]), c, 1)
        return jnp.stack([first, got[0]]), jnp.stack([own, got[1:]])

    n0_pair, s1_pair = for_sibling(n0, s1)

    projected = dot_nn(n2, w_qkv)
    queries = (projected[:, :width] + q_bias).astype(BF)
    key_vals = projected[:, width:].astype(BF).reshape(frames, 2, heads, DH)
    key_vals = key_vals.transpose(0, 2, 1, 3).reshape(frames, 2 * width)
    kv_own = lax.all_to_all(key_vals, LAYER, split_axis=1, concat_axis=0, tiled=True)
    up = [(i, i + 1) for i in range(zs - 1)]
    down = [(i + 1, i) for i in range(zs - 1)]
    kv_prev = lax.ppermute(kv_own[-span:], "z", up)
    kv_next = lax.ppermute(kv_own[:span], "z", down)
    q_own = lax.all_to_all(queries, LAYER, split_axis=1, concat_axis=0, tiled=True)
    kv = jnp.concatenate([kv_prev, kv_own, kv_next, jnp.zeros((BK, 2 * DH), BF)], axis=0)
    o_own, lse = attn_fwd(q_own, kv, low, high, c2, lo_q, hi_q, origin)
    mixed = lax.all_to_all(o_own, LAYER, split_axis=0, concat_axis=1, tiled=True)
    x2 = x1 + dot_nn(mixed, w_att)

    hat2, inv2 = norm_stats(x2)
    n3 = (hat2 * gains[2] + shifts[2]).astype(BF)
    pointwise = dot_nn(n3, w_cin)
    linear_half = pointwise[:, :width]
    gate = jax.nn.sigmoid(pointwise[:, width:])
    gated = neighbour_rows((linear_half * gate * valid_col).astype(BF))
    conv = jnp.zeros((frames, width), F32)
    for m in range(KSIZE):
        conv = conv + taps[m] * gated[m : m + frames].astype(F32) * masks[m]
    moments = sum_everywhere(
        jnp.stack([jnp.sum(valid_col * conv, axis=0), jnp.sum(valid_col * conv * conv, axis=0)])
    )
    mean_c = moments[0] / valid_count
    inv_batch = lax.rsqrt(moments[1] / valid_count - mean_c * mean_c + EPSILON)
    conv_hat = (conv - mean_c) * inv_batch
    batch_out = conv_hat * gains[3] + shifts[3]
    sig_bn = jax.nn.sigmoid(batch_out)
    swished = (batch_out * sig_bn).astype(BF)
    x3 = x2 + dot_nn(swished, w_cout)

    final_out, n4, s2, d2, dx4, sums5 = ffn_last(
        x3, w_f2, vectors(gains[4], shifts[4], gains[5], shifts[5]), out_grad
    )
    n4_pair, s2_pair = for_sibling(n4, s2)
    ef2, da2, dx3, sums4 = ffn_bwd(dx4, x3, w_f2, d2, vectors(gains[4]), F32)
    ef2_pair, da2_pair = for_sibling(ef2, da2)
    grad_f2i = ffn_grads(n4_pair, da2_pair, "x")
    grad_f2o = ffn_grads(ef2_pair, s2_pair, "y")

    ew = dx3.astype(BF)
    grad_cout = dot_tn(swished, ew)
    batch_grad = dot_nt(ew, w_cout) * (sig_bn * (1.0 + batch_out * (1.0 - sig_bn)))
    sums3 = jnp.stack([jnp.sum(batch_grad * conv_hat, axis=0), jnp.sum(batch_grad, axis=0)])
    totals = sum_everywhere(sums3 * gains[3])
    conv_grad = (
        inv_batch
        * (
            batch_grad * gains[3]
            - valid_col * (totals[1] + conv_hat * totals[0]) / valid_count
        )
    ).astype(BF)
    grad_ext = neighbour_rows(conv_grad)
    conv_grad_f = conv_grad.astype(F32)
    gated_grad = jnp.zeros((frames, width), F32)
    depth_rows = []
    for m in range(KSIZE):
        back = 2 * REACH - m
        gated_grad = gated_grad + taps[m] * grad_ext[back : back + frames].astype(F32) * masks[back]
        depth_rows.append(
            jnp.sum(conv_grad_f * gated[m : m + frames].astype(F32) * masks[m], axis=0)
        )
    glu_grad = gated_grad * valid_col
    point_grad = jnp.concatenate(
        [glu_grad * gate, glu_grad * linear_half * gate * (1.0 - gate)], axis=1
    ).astype(BF)
    grad_cin = dot_tn(n3, point_grad)
    dn3 = dot_nt(point_grad, w_cin)
    sums2 = jnp.stack([jnp.sum(dn3 * hat2, axis=0), jnp.sum(dn3, axis=0)])
    dx2 = dx3 + norm_back(dn3, hat2, inv2, gains[2])
    ey = dx2.astype(BF)
    grad_att = dot_tn(mixed, ey)
    mixed_grad = dot_nt(ey, w_att).astype(BF)
    do_own = lax.all_to_all(mixed_grad, LAYER, split_axis=1, concat_axis=0, tiled=True)
    mid = row_grads(jnp.concatenate([grad_att, grad_cin, grad_cout], axis=1))
    out_att, out_cin, out_cout = mid[:, :width], mid[:, width : 3 * width], mid[:, 3 * width :]

    dq, dkv_prev, dkv, dkv_next = attn_bwd(
        q_own, o_own, do_own, lse, kv, low, high, c2, lo_q, hi_q, origin
    )
    from_next = lax.ppermute(dkv_prev, "z", down).astype(F32)
    from_prev = lax.ppermute(dkv_next, "z", up).astype(F32)
    grad_query = lax.all_to_all(dq, LAYER, split_axis=0, concat_axis=1, tiled=True)
    dkv = jnp.concatenate(
        [dkv[:span] + from_prev, dkv[span:-span], dkv[-span:] + from_next], axis=0
    ).astype(BF)
    grad_kv = lax.all_to_all(dkv, LAYER, split_axis=0, concat_axis=1, tiled=True)
    grad_kv = grad_kv.reshape(frames, heads, 2, DH).transpose(0, 2, 1, 3).reshape(frames, 2 * width)
    proj_grad = jnp.concatenate([grad_query, grad_kv], axis=1)
    bias_grad = jnp.sum(grad_query.astype(F32), axis=0)

    dn2 = dot_nt(proj_grad, w_qkv)
    hat1, inv1 = norm_stats(x1)
    sums1 = jnp.stack([jnp.sum(dn2 * hat1, axis=0), jnp.sum(dn2, axis=0)])
    dx1 = dx2 + norm_back(dn2, hat1, inv1, gains[1])
    ef1, da1, grad_input, sums0 = ffn_bwd(dx1, block_in, w_f1, d1, vectors(gains[0]), BF)
    ef1_pair, da1_pair = for_sibling(ef1, da1)
    grad_f1o = ffn_grads(ef1_pair, s1_pair, "y")
    grad_f1i = ffn_grads(n0_pair, da1_pair, "x")
    out_qkv = row_grads(dot_tn(n2, proj_grad))

    rows = [sums0, sums1, sums2, sums3, sums4, sums5]
    rows = jnp.concatenate(
        [r[:1] for r in rows] + [r[1:] for r in rows] + [jnp.stack(depth_rows), bias_grad[None]],
        axis=0,
    )
    rows = rows.reshape(rows.shape[0], devices, width // devices).transpose(1, 0, 2)
    rows = jnp.sum(lax.all_to_all(rows, DEV, split_axis=0, concat_axis=0, tiled=True), axis=0)

    return (
        final_out,
        grad_input,
        grad_f1i,
        grad_f1o.T,
        out_qkv,
        out_att,
        rows[12 + KSIZE],
        out_cin,
        out_cout,
        grad_f2i,
        grad_f2o.T,
        rows[12 : 12 + KSIZE],
        rows[:6],
        rows[6:12],
    )


def solution(mesh):
    seq, heads = mesh.shape["seq"], mesh.shape["head"]
    grid = Mesh(mesh.devices.reshape(seq // 2, 2, heads // 2, 2), DEV)
    both = P(DEV, None)
    inward = P(("z", "x"), ("y", "c"))
    outward = P(("y", "c"), ("z", "x"))
    columns = P(None, DEV)
    return jax.shard_map(
        body,
        mesh=grid,
        in_specs=(
            both,
            both,
            P(),
            P(),
            inward,
            outward,
            both,
            both,
            P(DEV),
            both,
            both,
            inward,
            outward,
            columns,
            columns,
            columns,
        ),
        out_specs=(
            both,
            both,
            inward,
            outward,
            both,
            both,
            P(DEV),
            both,
            both,
            inward,
            outward,
            columns,
            columns,
            columns,
        ),
        check_vma=False,
    )
```

```python
import functools
import math

import jax
import jax.numpy as jnp
from jax import lax
from jax.experimental import pallas as pl
from jax.experimental.pallas import tpu as pltpu
from jax.sharding import Mesh
from jax.sharding import PartitionSpec as P

DH = 128
KSIZE = 5
REACH = (KSIZE - 1) // 2
EPSILON = 1e-05
MASKED = -1e30
LOG2E = math.log2(math.e)
DEV = ("z", "x", "y", "c")
LAYER = ("x", "y", "c")
BQ = 256
BK = 512
BF = jnp.bfloat16
F32 = jnp.float32
VMEM_BYTES = 56 * 1024 * 1024


def pick(cells, index, dim):
    return lax.dynamic_index_in_dim(cells, index, dim, keepdims=False)


def xor_send(cells, axis, bit):
    count = lax.axis_size(axis)
    return lax.ppermute(cells, axis, [(i, i ^ bit) for i in range(count)])


def neighbour_rows(tail, head=None):
    if head is None:
        tail, head = tail[-REACH:], tail[:REACH]
    count = 1
    for axis in DEV:
        count *= lax.axis_size(axis)
    before = lax.ppermute(tail, DEV, [(i, i + 1) for i in range(count - 1)])
    after = lax.ppermute(head, DEV, [(i + 1, i) for i in range(count - 1)])
    return before, after


def dot_nn(a, b):
    return lax.dot_general(a, b, (((1,), (0,)), ((), ())), preferred_element_type=F32)


def dot_nt(a, b):
    return lax.dot_general(a, b, (((1,), (1,)), ((), ())), preferred_element_type=F32)


def dot_tn(a, b):
    return lax.dot_general(a, b, (((0,), (0,)), ((), ())), preferred_element_type=F32)


def norm_stats(values):
    centred = values - jnp.mean(values, axis=-1, keepdims=True)
    inv_std = lax.rsqrt(jnp.mean(centred * centred, axis=-1, keepdims=True) + EPSILON)
    return centred * inv_std, inv_std


def norm_back(upstream, normed, inv_std, gain):
    scaled = upstream * gain
    inner = (
        scaled
        - jnp.mean(scaled, axis=-1, keepdims=True)
        - normed * jnp.mean(scaled * normed, axis=-1, keepdims=True)
    )
    return inv_std * inner


def pack_kernel(extra, in_ref, out_ref, *refs):
    rows = in_ref.shape[0]
    refs[extra][:rows] = in_ref[...]
    refs[extra][rows:] = out_ref[...].T


def pack_ffn(w_in, w_out, order=()):
    rows, width = w_in.shape
    whole = lambda v: pl.BlockSpec(v.shape, lambda: (0, 0))
    if rows % 128:
        return jnp.concatenate([w_in, w_out.T], axis=0)
    return pl.pallas_call(
        functools.partial(pack_kernel, len(order)),
        in_specs=[whole(w_in), whole(w_out)] + [pl.BlockSpec(memory_space=pl.ANY)] * len(order),
        out_specs=pl.BlockSpec((2 * rows, width), lambda: (0, 0)),
        out_shape=jax.ShapeDtypeStruct((2 * rows, width), BF),
        name="pack_ffn",
    )(w_in, w_out, *order)


class Rows:
    def __init__(self, gathered, first, count):
        self.stepped = count % 16 == 0 and first % count == 0
        devices, _, width = gathered.shape
        self.count = count
        if self.stepped:
            self.at = first // count
            self.array = gathered
            self.block = (devices, count, width)
        else:
            self.first = first
            self.gathered = gathered
            self.width = width

    def blocks(self, pick_block, total):
        if self.stepped:
            at = self.at
            return self.array, pl.BlockSpec(self.block, lambda j, *_: (0, at + pick_block(j), 0))
        cut = [
            self.gathered[:, self.first + i * self.count : self.first + (i + 1) * self.count]
            for i in range(total)
        ]
        cut = jnp.stack([v.reshape(-1, self.width) for v in cut])
        return cut, pl.BlockSpec((1,) + cut.shape[1:], lambda j, *_: (pick_block(j), 0, 0))


def square(ref):
    return ref[...].reshape(-1, ref.shape[-1])


def slab_of(step, core):
    return (step % 2) * 2 + jnp.where(step < 2, 1 - core, core)


def slab_specs(gathered, rows, step_of):
    devices, total, width = gathered.shape
    array = gathered.reshape(devices // 4, 4, total, width)
    block = (devices // 4, 1, rows, width)
    specs = [
        pl.BlockSpec(block, lambda j, c, i=i: (0, slab_of(step_of(j), c[0]), i, 0)) for i in (0, 1)
    ]
    return [array, array], specs


def heads_of(ref, lo, hi):
    return jnp.concatenate([ref[h, :, lo:hi] for h in range(ref.shape[0])], axis=1)


def forward_slab(n, w1_ref, w2_ref, s_ref, d_out):
    width = n.shape[1]
    w1 = square(w1_ref)
    chunk = 256
    for at in range(0, width, chunk):
        a = dot_nn(n, w1[:, at : at + chunk])
        sig = jax.nn.sigmoid(a)
        s_ref[:, at : at + chunk] = (a * sig).astype(BF)
        d_out[:, at : at + chunk] = (sig * (1.0 + a * (1.0 - sig))).astype(BF)
    return dot_nt(s_ref[...], square(w2_ref))


def backward_slab(ef, w1_ref, w2_ref, d_in, da_ref):
    width = ef.shape[1]
    w2 = square(w2_ref)
    chunk = 256
    for at in range(0, width, chunk):
        ds = dot_nn(ef, w2[:, at : at + chunk])
        da_ref[:, at : at + chunk] = (ds * d_in[:, at : at + chunk].astype(F32)).astype(BF)
    return dot_nt(da_ref[...], square(w1_ref))


def keep_slab(step, cells, pack_ref, pack_at, own_ref):
    @pl.when(step < 2)
    def _():
        pack_ref[pack_at + step] = cells

    @pl.when(step >= 2)
    def _():
        own_ref[0] = cells


def first_kernel(
    core_ref,
    x_ref,
    w1_ref,
    w2_ref,
    wp_ref,
    vec_ref,
    x1_ref,
    n2_ref,
    pack_ref,
    own_ref,
    d_ref,
    q_ref,
    k_ref,
    v_ref,
    acc_ref,
    s_ref,
):
    step = pl.program_id(0)

    @pl.when(step == 0)
    def _():
        normed, _ = norm_stats(x_ref[...].astype(F32))
        pack_ref[0] = (normed * vec_ref[0:1, :] + vec_ref[1:2, :]).astype(BF)
        acc_ref[...] = jnp.zeros_like(acc_ref)

    @pl.when(step < 4)
    def _():
        acc_ref[...] += forward_slab(pack_ref[0], w1_ref, w2_ref, s_ref, d_ref.at[0])
        keep_slab(step, s_ref[...], pack_ref, 1, own_ref)

    @pl.when(step == 3)
    def _():
        x1 = x_ref[...].astype(F32) + 0.5 * acc_ref[...]
        x1_ref[...] = x1
        normed, _ = norm_stats(x1)
        n2_ref[...] = (normed * vec_ref[2:3, :] + vec_ref[3:4, :]).astype(BF)

    for part, ref in enumerate((q_ref, k_ref, v_ref)):

        @pl.when(step == 4 + part)
        def _():
            projected = dot_nn(n2_ref[...], square(wp_ref))
            if part == 0:
                projected = projected + vec_ref[4:5, :]
            projected = projected.astype(BF)
            for h in range(ref.shape[0]):
                ref[h] = projected[:, h * DH : (h + 1) * DH]


def first_call(core, x, gathered, rows, proj, vectors):
    frames, width = x.shape
    heads = width // DH
    fixed = lambda *shape: pl.BlockSpec(shape, lambda j, c: (0,) * len(shape))
    slabs, slab_blocks = slab_specs(gathered, rows, lambda j: jnp.minimum(j, 3))
    proj_array, proj_block = proj.blocks(lambda j: jnp.clip(j - 4, 0, 2), 3)
    return pl.pallas_call(
        first_kernel,
        grid_spec=pltpu.PrefetchScalarGridSpec(
            num_scalar_prefetch=1,
            grid=(7,),
            in_specs=[fixed(frames, width)] + slab_blocks + [proj_block, fixed(*vectors.shape)],
            out_specs=[
                fixed(frames, width),
                fixed(frames, width),
                fixed(3, frames, width),
                pl.BlockSpec((1, frames, width), lambda j, c: (jnp.clip(j - 2, 0, 1), 0, 0)),
                pl.BlockSpec((1, frames, width), lambda j, c: (jnp.minimum(j, 3), 0, 0)),
                fixed(heads, frames, DH),
                fixed(heads, frames, DH),
                fixed(heads, frames, DH),
            ],
            scratch_shapes=[pltpu.VMEM((frames, width), F32), pltpu.VMEM((frames, width), BF)],
        ),
        out_shape=[
            jax.ShapeDtypeStruct((frames, width), F32),
            jax.ShapeDtypeStruct((frames, width), BF),
            jax.ShapeDtypeStruct((3, frames, width), BF),
            jax.ShapeDtypeStruct((2, frames, width), BF),
            jax.ShapeDtypeStruct((4, frames, width), BF),
            jax.ShapeDtypeStruct((heads, frames, DH), BF),
            jax.ShapeDtypeStruct((heads, frames, DH), BF),
            jax.ShapeDtypeStruct((heads, frames, DH), BF),
        ],
        compiler_params=pltpu.CompilerParams(vmem_limit_bytes=VMEM_BYTES),
        cost_estimate=pl.CostEstimate(
            flops=22 * frames * width * width,
            bytes_accessed=22 * width * width + 40 * frames * width,
            transcendentals=4 * frames * width,
        ),
        name="first_part",
    )(core, x, *slabs, proj_array, vectors)


def gate_kernel(
    mh_ref,
    x1_ref,
    w_ref,
    vec_ref,
    cols_ref,
    mixed_ref,
    x2_ref,
    n3_ref,
    lin_ref,
    sig_ref,
    g_ref,
):
    step = pl.program_id(0)

    @pl.when(step == 0)
    def _():
        mixed = heads_of(mh_ref, 0, DH)
        mixed_ref[...] = mixed
        x2 = x1_ref[...] + dot_nn(mixed, square(w_ref))
        x2_ref[...] = x2
        normed, _ = norm_stats(x2)
        n3_ref[...] = (normed * vec_ref[0:1, :] + vec_ref[1:2, :]).astype(BF)

    @pl.when(step == 1)
    def _():
        lin_ref[...] = dot_nn(n3_ref[...], square(w_ref))

    @pl.when(step == 2)
    def _():
        sig = jax.nn.sigmoid(dot_nn(n3_ref[...], square(w_ref)))
        sig_ref[...] = sig
        g_ref[...] = (lin_ref[...] * sig * cols_ref[:, KSIZE : KSIZE + 1]).astype(BF)


def gate_call(mixed_heads, x1, weights, vectors, columns):
    frames, width = x1.shape
    fixed = lambda *shape: pl.BlockSpec(shape, lambda j: (0,) * len(shape))
    array, block = weights.blocks(lambda j: j, 3)
    return pl.pallas_call(
        gate_kernel,
        grid=(3,),
        in_specs=[
            fixed(*mixed_heads.shape),
            fixed(frames, width),
            block,
            fixed(*vectors.shape),
            fixed(*columns.shape),
        ],
        out_specs=[fixed(frames, width)] * 6,
        out_shape=[jax.ShapeDtypeStruct((frames, width), t) for t in (BF, F32, BF, F32, F32, BF)],
        compiler_params=pltpu.CompilerParams(vmem_limit_bytes=VMEM_BYTES),
        cost_estimate=pl.CostEstimate(
            flops=6 * frames * width * width,
            bytes_accessed=6 * width * width + 24 * frames * width,
            transcendentals=frames * width,
        ),
        name="attention_out_and_gate",
    )(mixed_heads, x1, array, vectors, columns)


PAD = 8


def lay_out(scratch, before, cells, after):
    frames = cells.shape[0]
    scratch[PAD - REACH : PAD, :] = before
    scratch[PAD : PAD + frames, :] = cells
    scratch[PAD + frames : PAD + frames + REACH, :] = after


def conv_kernel(g_ref, before_ref, after_ref, vec_ref, cols_ref, conv_ref, sums_ref, ext):
    frames = g_ref.shape[0]
    lay_out(
        ext, before_ref[...].astype(F32), g_ref[...].astype(F32), after_ref[...].astype(F32)
    )
    conv = jnp.zeros(g_ref.shape, F32)
    for m in range(KSIZE):
        rows = ext[PAD - REACH + m : PAD - REACH + m + frames, :]
        conv = conv + vec_ref[m : m + 1, :] * rows * cols_ref[:, m : m + 1]
    conv_ref[...] = conv
    counted = conv * cols_ref[:, KSIZE : KSIZE + 1]
    sums = jnp.concatenate(
        [jnp.sum(counted, axis=0, keepdims=True), jnp.sum(counted * conv, axis=0, keepdims=True)]
    )
    sums_ref[...] = jnp.broadcast_to(sums[None], sums_ref.shape)


def conv_call(g, before, after, taps, columns, devices):
    frames, width = g.shape
    return pl.pallas_call(
        conv_kernel,
        out_shape=[
            jax.ShapeDtypeStruct((frames, width), F32),
            jax.ShapeDtypeStruct((devices, 2, width), F32),
        ],
        scratch_shapes=[pltpu.VMEM((frames + 2 * PAD, width), F32)],
        compiler_params=pltpu.CompilerParams(vmem_limit_bytes=VMEM_BYTES),
        cost_estimate=pl.CostEstimate(
            flops=20 * frames * width, bytes_accessed=8 * frames * width, transcendentals=0
        ),
        name="depthwise",
    )(g, before, after, taps, columns)


def batch_stats(moments_ref, count):
    sums = jnp.sum(moments_ref[...], axis=0)
    mean = sums[0:1, :] / count
    return mean, lax.rsqrt(sums[1:2, :] / count - mean * mean + EPSILON)


def second_kernel(
    core_ref,
    x2_ref,
    conv_ref,
    mom_ref,
    wc_ref,
    w1_ref,
    w2_ref,
    vec_ref,
    og_ref,
    out_ref,
    swish_ref,
    dx_ref,
    ew_ref,
    dz_ref,
    sums_ref,
    spread_ref,
    pack_ref,
    s_own_ref,
    da_own_ref,
    x3_ref,
    acc_ref,
    d_ref,
    dsilu_ref,
    s_ref,
    dx4_ref,
):
    step = pl.program_id(0)
    count = vec_ref[6:7, :]

    @pl.when(step == 0)
    def _():
        mean, inv = batch_stats(mom_ref, count)
        z = (conv_ref[...] - mean) * inv * vec_ref[0:1, :] + vec_ref[1:2, :]
        sig = jax.nn.sigmoid(z)
        swish = (z * sig).astype(BF)
        swish_ref[...] = swish
        dsilu_ref[...] = sig * (1.0 + z * (1.0 - sig))
        x3 = x2_ref[...] + dot_nn(swish, square(wc_ref))
        x3_ref[...] = x3
        normed, _ = norm_stats(x3)
        pack_ref[0] = (normed * vec_ref[2:3, :] + vec_ref[3:4, :]).astype(BF)
        acc_ref[...] = jnp.zeros_like(acc_ref)

    @pl.when(step < 4)
    def _():
        acc_ref[...] += forward_slab(pack_ref[0], w1_ref, w2_ref, s_ref, d_ref.at[step])
        keep_slab(step, s_ref[...], pack_ref, 1, s_own_ref)

    @pl.when(step == 3)
    def _():
        normed, inv_std = norm_stats(x3_ref[...] + 0.5 * acc_ref[...])
        gain = vec_ref[4:5, :]
        out_ref[...] = (normed * gain + vec_ref[5:6, :]).astype(BF)
        upstream = og_ref[...].astype(F32)
        dx4 = norm_back(upstream, normed, inv_std, gain)
        dx4_ref[...] = dx4
        pack_ref[3] = (0.5 * dx4).astype(BF)
        sums_ref[0:1, :] = jnp.sum(upstream * normed, axis=0, keepdims=True)
        sums_ref[1:2, :] = jnp.sum(upstream, axis=0, keepdims=True)
        acc_ref[...] = jnp.zeros_like(acc_ref)

    @pl.when(step >= 4)
    def _():
        acc_ref[...] += backward_slab(pack_ref[3], w1_ref, w2_ref, d_ref.at[step - 4], s_ref)
        keep_slab(step - 4, s_ref[...], pack_ref, 4, da_own_ref)

    @pl.when(step == 7)
    def _():
        normed, inv_std = norm_stats(x3_ref[...])
        dn = acc_ref[...]
        dx3 = dx4_ref[...] + norm_back(dn, normed, inv_std, vec_ref[2:3, :])
        dx_ref[...] = dx3
        sums_ref[2:3, :] = jnp.sum(dn * normed, axis=0, keepdims=True)
        sums_ref[3:4, :] = jnp.sum(dn, axis=0, keepdims=True)
        ew = dx3.astype(BF)
        ew_ref[...] = ew
        dz = dot_nt(ew, square(wc_ref)) * dsilu_ref[...]
        dz_ref[...] = dz
        mean, inv = batch_stats(mom_ref, count)
        zhat = (conv_ref[...] - mean) * inv
        totals = jnp.concatenate(
            [jnp.sum(dz * zhat, axis=0, keepdims=True), jnp.sum(dz, axis=0, keepdims=True)]
        )
        sums_ref[4:6, :] = totals
        sums_ref[6:8, :] = jnp.zeros((2, dz.shape[1]), F32)
        spread_ref[...] = jnp.broadcast_to(totals[None], spread_ref.shape)


def second_call(core, x2, conv, moments, weights, gathered, rows, vectors, out_grad):
    frames, width = x2.shape
    fixed = lambda *shape: pl.BlockSpec(shape, lambda j, c: (0,) * len(shape))
    slabs, slab_blocks = slab_specs(gathered, rows, lambda j: j % 4)
    array, block = weights.blocks(lambda j: 0, 1)
    whole = fixed(frames, width)
    return pl.pallas_call(
        second_kernel,
        grid_spec=pltpu.PrefetchScalarGridSpec(
            num_scalar_prefetch=1,
            grid=(8,),
            in_specs=[whole, whole, fixed(*moments.shape), block]
            + slab_blocks
            + [fixed(*vectors.shape), whole],
            out_specs=[
                whole,
                whole,
                whole,
                whole,
                whole,
                fixed(8, width),
                fixed(*moments.shape),
                fixed(6, frames, width),
                pl.BlockSpec((1, frames, width), lambda j, c: (jnp.clip(j - 2, 0, 1), 0, 0)),
                pl.BlockSpec((1, frames, width), lambda j, c: (jnp.clip(j - 6, 0, 1), 0, 0)),
            ],
            scratch_shapes=[
                pltpu.VMEM((frames, width), F32),
                pltpu.VMEM((frames, width), F32),
                pltpu.VMEM((4, frames, width), BF),
                pltpu.VMEM((frames, width), F32),
                pltpu.VMEM((frames, width), BF),
                pltpu.VMEM((frames, width), F32),
            ],
        ),
        out_shape=[
            jax.ShapeDtypeStruct((frames, width), BF),
            jax.ShapeDtypeStruct((frames, width), BF),
            jax.ShapeDtypeStruct((frames, width), F32),
            jax.ShapeDtypeStruct((frames, width), BF),
            jax.ShapeDtypeStruct((frames, width), F32),
            jax.ShapeDtypeStruct((8, width), F32),
            jax.ShapeDtypeStruct(moments.shape, F32),
            jax.ShapeDtypeStruct((6, frames, width), BF),
            jax.ShapeDtypeStruct((2, frames, width), BF),
            jax.ShapeDtypeStruct((2, frames, width), BF),
        ],
        compiler_params=pltpu.CompilerParams(vmem_limit_bytes=VMEM_BYTES),
        cost_estimate=pl.CostEstimate(
            flops=36 * frames * width * width,
            bytes_accessed=34 * width * width + 40 * frames * width,
            transcendentals=5 * frames * width,
        ),
        name="second_part",
    )(core, x2, conv, moments, array, *slabs, vectors, out_grad)


def back_kernel(
    extra,
    dz_ref,
    conv_ref,
    edge_before_ref,
    edge_after_ref,
    g_ref,
    g_before_ref,
    g_after_ref,
    mom_ref,
    tot_ref,
    lin_ref,
    sig_ref,
    x2_ref,
    dx3_ref,
    w_ref,
    vec_ref,
    cols_ref,
    *refs,
):
    pg_ref, dx2_ref, ey_ref, do_ref, sums_ref, ext, g_ext, acc_ref, b_ref = refs[extra:]
    step = pl.program_id(0)
    frames, width = dz_ref.shape

    @pl.when(step == 0)
    def _():
        count = vec_ref[8:9, :]
        gain = vec_ref[5:6, :]
        mean, inv = batch_stats(mom_ref, count)
        totals = jnp.sum(tot_ref[...], axis=0) * gain

        def conv_grad(dz, conv, valid):
            zhat = (conv - mean) * inv
            dc = inv * (dz * gain - valid * (totals[1:2, :] + zhat * totals[0:1, :]) / count)
            return dc.astype(BF).astype(F32)

        valid = cols_ref[:, KSIZE : KSIZE + 1]
        dc = conv_grad(dz_ref[...], conv_ref[...], valid)
        edges = []
        for at, ref in ((0, edge_before_ref), (REACH, edge_after_ref)):
            edges.append(
                conv_grad(
                    ref[0:REACH, :],
                    ref[REACH : 2 * REACH, :],
                    cols_ref[at : at + REACH, KSIZE + 1 : KSIZE + 2],
                )
            )
        lay_out(ext, edges[0], dc, edges[1])
        lay_out(
            g_ext,
            g_before_ref[...].astype(F32),
            g_ref[...].astype(F32),
            g_after_ref[...].astype(F32),
        )
        dg = jnp.zeros((frames, width), F32)
        for m in range(KSIZE):
            back = 2 * REACH - m
            rows = ext[PAD - REACH + back : PAD - REACH + back + frames, :]
            dg = dg + vec_ref[m : m + 1, :] * rows * cols_ref[:, back : back + 1]
            there = g_ext[PAD - REACH + m : PAD - REACH + m + frames, :]
            sums_ref[2 + m : 3 + m, :] = jnp.sum(
                dc * there * cols_ref[:, m : m + 1], axis=0, keepdims=True
            )
        sums_ref[7:8, :] = jnp.zeros((1, width), F32)
        de = dg * valid
        sig = sig_ref[...]
        pa = (de * sig).astype(BF)
        pb = (de * lin_ref[...] * sig * (1.0 - sig)).astype(BF)
        pg_ref[:, :width] = pa
        pg_ref[:, width:] = pb
        b_ref[...] = pb
        acc_ref[...] = dot_nt(pa, square(w_ref))

    @pl.when(step == 1)
    def _():
        dn = acc_ref[...] + dot_nt(b_ref[...], square(w_ref))
        normed, inv_std = norm_stats(x2_ref[...])
        dx2 = dx3_ref[...] + norm_back(dn, normed, inv_std, vec_ref[6:7, :])
        dx2_ref[...] = dx2
        ey_ref[...] = dx2.astype(BF)
        sums_ref[0:1, :] = jnp.sum(dn * normed, axis=0, keepdims=True)
        sums_ref[1:2, :] = jnp.sum(dn, axis=0, keepdims=True)

    @pl.when(step == 2)
    def _():
        grads = dot_nt(ey_ref[...], square(w_ref)).astype(BF)
        for h in range(do_ref.shape[0]):
            do_ref[h] = grads[:, h * DH : (h + 1) * DH]


def back_call(dz, conv, edges, g, g_edges, moments, totals, lin, sig, x2, dx3, weights, vectors, columns, order):
    frames, width = dz.shape
    fixed = lambda *shape: pl.BlockSpec(shape, lambda j: (0,) * len(shape))
    array, block = weights.blocks(lambda j: (j + 1) % 3, 3)
    whole = fixed(frames, width)
    return pl.pallas_call(
        functools.partial(back_kernel, len(order)),
        grid=(3,),
        in_specs=[
            whole,
            whole,
            fixed(2 * REACH, width),
            fixed(2 * REACH, width),
            whole,
            fixed(REACH, width),
            fixed(REACH, width),
            fixed(*moments.shape),
            fixed(*totals.shape),
            whole,
            whole,
            whole,
            whole,
            block,
            fixed(*vectors.shape),
            fixed(*columns.shape),
        ]
        + [pl.BlockSpec(memory_space=pl.ANY)] * len(order),
        out_specs=[
            fixed(frames, 2 * width),
            whole,
            whole,
            fixed(width // DH, frames, DH),
            fixed(8, width),
        ],
        out_shape=[
            jax.ShapeDtypeStruct((frames, 2 * width), BF),
            jax.ShapeDtypeStruct((frames, width), F32),
            jax.ShapeDtypeStruct((frames, width), BF),
            jax.ShapeDtypeStruct((width // DH, frames, DH), BF),
            jax.ShapeDtypeStruct((8, width), F32),
        ],
        scratch_shapes=[
            pltpu.VMEM((frames + 2 * PAD, width), F32),
            pltpu.VMEM((frames + 2 * PAD, width), F32),
            pltpu.VMEM((frames, width), F32),
            pltpu.VMEM((frames, width), BF),
        ],
        compiler_params=pltpu.CompilerParams(vmem_limit_bytes=VMEM_BYTES),
        cost_estimate=pl.CostEstimate(
            flops=6 * frames * width * width,
            bytes_accessed=6 * width * width + 34 * frames * width,
            transcendentals=0,
        ),
        name="convolution_backward",
    )(
        dz,
        conv,
        edges[0],
        edges[1],
        g,
        g_edges[0],
        g_edges[1],
        moments,
        totals,
        lin,
        sig,
        x2,
        dx3,
        array,
        vectors,
        columns,
        *order,
    )


def proj_back_kernel(extra, dq_ref, dkv_ref, dx2_ref, x1_ref, wp_ref, vec_ref, *refs):
    dx1_ref, ef_ref, sums_ref, acc_ref = refs[extra:]
    step = pl.program_id(0)

    @pl.when(step == 0)
    def _():
        dq = heads_of(dq_ref, 0, DH)
        acc_ref[...] = dot_nt(dq, square(wp_ref))
        sums_ref[2:3, :] = jnp.sum(dq.astype(F32), axis=0, keepdims=True)
        sums_ref[3:8, :] = jnp.zeros((5, dq.shape[1]), F32)

    @pl.when(step == 1)
    def _():
        acc_ref[...] += dot_nt(heads_of(dkv_ref, 0, DH), square(wp_ref))

    @pl.when(step == 2)
    def _():
        dn = acc_ref[...] + dot_nt(heads_of(dkv_ref, DH, 2 * DH), square(wp_ref))
        normed, inv_std = norm_stats(x1_ref[...])
        dx1 = dx2_ref[...] + norm_back(dn, normed, inv_std, vec_ref[1:2, :])
        dx1_ref[...] = dx1
        ef_ref[0] = (0.5 * dx1).astype(BF)
        sums_ref[0:1, :] = jnp.sum(dn * normed, axis=0, keepdims=True)
        sums_ref[1:2, :] = jnp.sum(dn, axis=0, keepdims=True)


def proj_back_call(dq, dkv, dx2, x1, proj, vectors, order):
    frames, width = x1.shape
    fixed = lambda *shape: pl.BlockSpec(shape, lambda j: (0,) * len(shape))
    array, block = proj.blocks(lambda j: j, 3)
    whole = fixed(frames, width)
    return pl.pallas_call(
        functools.partial(proj_back_kernel, len(order)),
        grid=(3,),
        in_specs=[fixed(*dq.shape), fixed(*dkv.shape), whole, whole, block, fixed(*vectors.shape)]
        + [pl.BlockSpec(memory_space=pl.ANY)] * len(order),
        out_specs=[whole, fixed(1, frames, width), fixed(8, width)],
        out_shape=[
            jax.ShapeDtypeStruct((frames, width), F32),
            jax.ShapeDtypeStruct((1, frames, width), BF),
            jax.ShapeDtypeStruct((8, width), F32),
        ],
        scratch_shapes=[pltpu.VMEM((frames, width), F32)],
        compiler_params=pltpu.CompilerParams(vmem_limit_bytes=VMEM_BYTES),
        cost_estimate=pl.CostEstimate(flops=1024, bytes_accessed=1024, transcendentals=0),
        name="projections_backward",
    )(dq, dkv, dx2, x1, array, vectors, *order)


def last_kernel(extra, core_ref, dx1_ref, ef_ref, x_ref, w1_ref, w2_ref, d_ref, vec_ref, *refs):
    gin_ref, sums_ref, first_ref, second_ref, own_ref, acc_ref, da_ref = refs[extra:]
    step = pl.program_id(0)

    @pl.when(step == 0)
    def _():
        acc_ref[...] = jnp.zeros_like(acc_ref)

    acc_ref[...] += backward_slab(ef_ref[0], w1_ref, w2_ref, d_ref.at[0], da_ref)
    for at, ref in enumerate((first_ref, second_ref)):

        @pl.when(step == at)
        def _():
            ref[0] = da_ref[...]

    @pl.when(step >= 2)
    def _():
        own_ref[0] = da_ref[...]

    @pl.when(step == 3)
    def _():
        normed, inv_std = norm_stats(x_ref[...].astype(F32))
        dn = acc_ref[...]
        dx = dx1_ref[...] + norm_back(dn, normed, inv_std, vec_ref[0:1, :])
        gin_ref[...] = dx.astype(BF)
        sums_ref[0:1, :] = jnp.sum(dn * normed, axis=0, keepdims=True)
        sums_ref[1:2, :] = jnp.sum(dn, axis=0, keepdims=True)
        sums_ref[2:8, :] = jnp.zeros((6, dn.shape[1]), F32)


def last_call(core, dx1, ef, x, gathered, rows, slope, vectors, order):
    frames, width = x.shape
    fixed = lambda *shape: pl.BlockSpec(shape, lambda j, c: (0,) * len(shape))
    slabs, slab_blocks = slab_specs(gathered, rows, lambda j: j)
    whole = fixed(frames, width)
    return pl.pallas_call(
        functools.partial(last_kernel, len(order)),
        grid_spec=pltpu.PrefetchScalarGridSpec(
            num_scalar_prefetch=1,
            grid=(4,),
            in_specs=[whole, fixed(1, frames, width), whole]
            + slab_blocks
            + [pl.BlockSpec((1, frames, width), lambda j, c: (j, 0, 0)), fixed(*vectors.shape)]
            + [pl.BlockSpec(memory_space=pl.ANY)] * len(order),
            out_specs=[
                whole,
                fixed(8, width),
                fixed(1, frames, width),
                fixed(1, frames, width),
                pl.BlockSpec((1, frames, width), lambda j, c: (jnp.clip(j - 2, 0, 1), 0, 0)),
            ],
            scratch_shapes=[pltpu.VMEM((frames, width), F32), pltpu.VMEM((frames, width), BF)],
        ),
        out_shape=[
            jax.ShapeDtypeStruct((frames, width), BF),
            jax.ShapeDtypeStruct((8, width), F32),
            jax.ShapeDtypeStruct((1, frames, width), BF),
            jax.ShapeDtypeStruct((1, frames, width), BF),
            jax.ShapeDtypeStruct((2, frames, width), BF),
        ],
        compiler_params=pltpu.CompilerParams(vmem_limit_bytes=VMEM_BYTES),
        cost_estimate=pl.CostEstimate(flops=1024, bytes_accessed=1024, transcendentals=0),
        name="last_part",
    )(core, dx1, ef, x, *slabs, slope, vectors, *order)


def fill_window(kv_ref, parts):
    for column, refs in ((0, parts[:3]), (DH, parts[3:])):
        at = 0
        for ref in refs:
            kv_ref[at : at + ref.shape[0], column : column + DH] = ref[...]
            at += ref.shape[0]
    kv_ref[at:, :] = jnp.zeros((kv_ref.shape[0] - at, kv_ref.shape[1]), kv_ref.dtype)


def attn_fwd_kernel(
    origin,
    low_ref,
    high_ref,
    c2_ref,
    q_ref,
    *refs,
):
    lo_ref, hi_ref, o_ref, lse_ref, kv_ref = refs[6:]
    block = pl.program_id(0)

    @pl.when(block == 0)
    def _():
        fill_window(kv_ref, refs[:6])

    rows = q_ref.shape[0]
    q = q_ref[...]
    c1 = LOG2E * DH**-0.5
    c2 = c2_ref[0]
    at = lax.broadcasted_iota(jnp.int32, (1, rows), 1) + (origin + block * rows)
    q_pos = at.astype(F32)
    lo_q, hi_q = lo_ref[...], hi_ref[...]
    first = low_ref[block]
    steps = (high_ref[block] - first + (BK - 1)) // BK

    def step(t, carry):
        top, total, mixed = carry
        start = pl.multiple_of(first + t * BK, 128)
        k = kv_ref[pl.ds(start, BK), :DH]
        v = kv_ref[pl.ds(start, BK), DH:]
        k_pos = (lax.broadcasted_iota(jnp.int32, (BK, 1), 0) + start).astype(F32)
        scores = dot_nt(k, q) * c1 - jnp.abs(k_pos - q_pos) * c2
        scores = jnp.where((k_pos >= lo_q) & (k_pos < hi_q), scores, MASKED)
        new_top = jnp.maximum(top, jnp.max(scores, axis=0, keepdims=True))
        expo = jnp.exp2(scores - new_top)
        keep = jnp.exp2(top - new_top)
        total = total * keep + jnp.sum(expo, axis=0, keepdims=True)
        mixed = mixed * keep + dot_tn(v, expo.astype(BF))
        return new_top, total, mixed

    top, total, mixed = lax.fori_loop(
        0,
        steps,
        step,
        (
            jnp.full((1, rows), MASKED, F32),
            jnp.zeros((1, rows), F32),
            jnp.zeros((DH, rows), F32),
        ),
    )
    o_ref[...] = (mixed / total).T.astype(BF)
    lse_ref[...] = top + jnp.log2(total)


def attn_fwd(q, kv, low, high, c2, lo_q, hi_q, origin):
    frames = q.shape[0]
    window = sum(v.shape[0] for v in kv[:3]) + BK
    parts = [pl.BlockSpec(v.shape, lambda i, *_: (0, 0)) for v in kv]
    blocks = frames // BQ
    pairs = frames * 1024 * DH
    grid_spec = pltpu.PrefetchScalarGridSpec(
        num_scalar_prefetch=3,
        grid=(blocks,),
        in_specs=[
            pl.BlockSpec((BQ, DH), lambda i, *_: (i, 0)),
            *parts,
            pl.BlockSpec((1, BQ), lambda i, *_: (0, i)),
            pl.BlockSpec((1, BQ), lambda i, *_: (0, i)),
        ],
        out_specs=[
            pl.BlockSpec((BQ, DH), lambda i, *_: (i, 0)),
            pl.BlockSpec((1, BQ), lambda i, *_: (0, i)),
        ],
        scratch_shapes=[pltpu.VMEM((window, 2 * DH), BF)],
    )

    def kernel(*refs):
        attn_fwd_kernel(origin, *refs)

    return pl.pallas_call(
        kernel,
        grid_spec=grid_spec,
        out_shape=[
            jax.ShapeDtypeStruct((frames, DH), BF),
            jax.ShapeDtypeStruct((1, frames), F32),
        ],
        compiler_params=pltpu.CompilerParams(vmem_limit_bytes=VMEM_BYTES),
        cost_estimate=pl.CostEstimate(
            flops=4 * pairs, bytes_accessed=4 * window * DH, transcendentals=frames * 1024
        ),
        name="attention_forward",
    )(low, high, c2, q, *kv, lo_q, hi_q)


def attn_bwd_kernel(
    origin,
    extra,
    low_ref,
    high_ref,
    c2_ref,
    q_ref,
    o_ref,
    do_ref,
    lse_ref,
    lo_ref,
    hi_ref,
    *refs,
):
    dq_ref, prev_ref, own_ref, next_ref, dk_acc, dv_acc, kv_ref = refs[6 + extra :]
    block = pl.program_id(0)
    rows = q_ref.shape[0]
    frames = own_ref.shape[0]
    scale = DH**-0.5
    c1 = LOG2E * scale

    @pl.when(block == 0)
    def _():
        fill_window(kv_ref, refs[:6])
        dk_acc[...] = jnp.zeros_like(dk_acc)
        dv_acc[...] = jnp.zeros_like(dv_acc)

    q = q_ref[...]
    do = do_ref[...]
    c2 = c2_ref[0]
    delta = jnp.sum((o_ref[...].astype(F32) * do.astype(F32)).T, axis=0, keepdims=True)
    lse = lse_ref[...]
    at = lax.broadcasted_iota(jnp.int32, (1, rows), 1) + (origin + block * rows)
    q_pos = at.astype(F32)
    lo_q, hi_q = lo_ref[...], hi_ref[...]
    first = low_ref[block]
    steps = (high_ref[block] - first + (BK - 1)) // BK

    def step(t, dq):
        start = pl.multiple_of(first + t * BK, 128)
        here = pl.ds(start, BK)
        k = kv_ref[here, :DH]
        v = kv_ref[here, DH:]
        k_pos = (lax.broadcasted_iota(jnp.int32, (BK, 1), 0) + start).astype(F32)
        scores = dot_nt(k, q) * c1 - jnp.abs(k_pos - q_pos) * c2 - lse
        scores = jnp.where((k_pos >= lo_q) & (k_pos < hi_q), scores, MASKED)
        probs = jnp.exp2(scores)
        grads = (probs * (dot_nt(v, do) - delta)).astype(BF)
        dv_acc[here, :] += dot_nn(probs.astype(BF), do)
        dk_acc[here, :] += dot_nn(grads, q)
        return dq + dot_tn(k, grads)

    dq = lax.fori_loop(0, steps, step, jnp.zeros((DH, rows), F32))
    dq_ref[...] = (dq * scale).T.astype(BF)

    @pl.when(block == pl.num_programs(0) - 1)
    def _():
        prev_ref[:, :DH] = (dk_acc[:origin, :] * scale).astype(BF)
        prev_ref[:, DH:] = dv_acc[:origin, :].astype(BF)
        own_ref[:, :DH] = dk_acc[origin : origin + frames, :] * scale
        own_ref[:, DH:] = dv_acc[origin : origin + frames, :]
        next_ref[:, :DH] = (dk_acc[origin + frames : 2 * origin + frames, :] * scale).astype(BF)
        next_ref[:, DH:] = dv_acc[origin + frames : 2 * origin + frames, :].astype(BF)


def attn_bwd(q, o, do, lse, kv, low, high, c2, lo_q, hi_q, origin, order=()):
    frames = q.shape[0]
    blocks = frames // BQ
    pairs = frames * 1024 * DH
    window = sum(v.shape[0] for v in kv[:3]) + BK
    parts = [pl.BlockSpec(v.shape, lambda i, *_: (0, 0)) for v in kv]
    tile = pl.BlockSpec((BQ, DH), lambda i, *_: (i, 0))
    row = pl.BlockSpec((1, BQ), lambda i, *_: (0, i))
    grid_spec = pltpu.PrefetchScalarGridSpec(
        num_scalar_prefetch=3,
        grid=(blocks,),
        in_specs=[
            tile,
            tile,
            tile,
            row,
            row,
            row,
            *parts,
        ]
        + [pl.BlockSpec(memory_space=pl.ANY)] * len(order),
        out_specs=[
            tile,
            pl.BlockSpec((origin, 2 * DH), lambda i, *_: (0, 0)),
            pl.BlockSpec((frames, 2 * DH), lambda i, *_: (0, 0)),
            pl.BlockSpec((origin, 2 * DH), lambda i, *_: (0, 0)),
        ],
        scratch_shapes=[
            pltpu.VMEM((window, DH), F32),
            pltpu.VMEM((window, DH), F32),
            pltpu.VMEM((window, 2 * DH), BF),
        ],
    )

    def kernel(*refs):
        attn_bwd_kernel(origin, len(order), *refs)

    return pl.pallas_call(
        kernel,
        grid_spec=grid_spec,
        out_shape=[
            jax.ShapeDtypeStruct((frames, DH), BF),
            jax.ShapeDtypeStruct((origin, 2 * DH), BF),
            jax.ShapeDtypeStruct((frames, 2 * DH), F32),
            jax.ShapeDtypeStruct((origin, 2 * DH), BF),
        ],
        compiler_params=pltpu.CompilerParams(vmem_limit_bytes=VMEM_BYTES),
        cost_estimate=pl.CostEstimate(
            flops=80 * pairs, bytes_accessed=8 * window * DH, transcendentals=frames * 1024
        ),
        name="attention_backward",
    )(low, high, c2, q, o, do, lse, lo_q, hi_q, *kv, *order)


def pass_on_kernel(extra, *refs):
    count = (len(refs) - extra) // 2
    for a, b in zip(refs[:count], refs[count + extra :]):
        b[...] = a[...]


def pass_on(arrays, order):
    return pl.pallas_call(
        functools.partial(pass_on_kernel, len(order)),
        in_specs=[pl.BlockSpec(v.shape, lambda n=v.ndim: (0,) * n) for v in arrays]
        + [pl.BlockSpec(memory_space=pl.ANY)] * len(order),
        out_specs=[pl.BlockSpec(v.shape, lambda n=v.ndim: (0,) * n) for v in arrays],
        out_shape=[jax.ShapeDtypeStruct(v.shape, v.dtype) for v in arrays],
        compiler_params=pltpu.CompilerParams(vmem_limit_bytes=VMEM_BYTES // 3),
        cost_estimate=pl.CostEstimate(flops=1, bytes_accessed=1024, transcendentals=0),
        name="pass_on",
    )(*arrays, *order)


def join_kernel(extra, own_ref, before_ref, after_ref, *refs):
    out_ref = refs[extra]
    span = before_ref.shape[0]
    rows = own_ref.shape[0]
    out_ref[:span, :] = (own_ref[:span, :] + before_ref[...].astype(F32)).astype(BF)
    if rows > 2 * span:
        out_ref[span : rows - span, :] = own_ref[span : rows - span, :].astype(BF)
    out_ref[rows - span :, :] = (own_ref[rows - span :, :] + after_ref[...].astype(F32)).astype(BF)


def join_edges(own, before, after, order=()):
    return pl.pallas_call(
        functools.partial(join_kernel, len(order)),
        in_specs=[pl.BlockSpec(v.shape, lambda: (0, 0)) for v in (own, before, after)]
        + [pl.BlockSpec(memory_space=pl.ANY)] * len(order),
        out_specs=pl.BlockSpec(own.shape, lambda: (0, 0)),
        out_shape=jax.ShapeDtypeStruct(own.shape, BF),
        compiler_params=pltpu.CompilerParams(vmem_limit_bytes=VMEM_BYTES // 2),
        cost_estimate=pl.CostEstimate(
            flops=own.size, bytes_accessed=8 * own.size, transcendentals=0
        ),
        name="join_edges",
    )(own, before, after, *order)


def stack_kernel(extra, places, *refs):
    out_ref = refs[-1]
    for at, (source, row) in enumerate(places):
        out_ref[at : at + 1, :] = refs[source][row : row + 1, :]


def stack_rows(arrays, places, order=()):
    width = arrays[0].shape[1]
    return pl.pallas_call(
        functools.partial(stack_kernel, len(order), places),
        in_specs=[pl.BlockSpec(v.shape, lambda: (0, 0)) for v in arrays]
        + [pl.BlockSpec(memory_space=pl.ANY)] * len(order),
        out_specs=pl.BlockSpec((len(places), width), lambda: (0, 0)),
        out_shape=jax.ShapeDtypeStruct((len(places), width), F32),
        name="stack_rows",
    )(*arrays, *order)


def halve_kernel(extra, sel_ref, kept_a, kept_b, got_a, got_b, *refs):
    send_ref, keep_ref = refs[extra:]
    send_ref[...] = (kept_a[0].astype(F32) + got_a[0].astype(F32)).astype(BF)
    keep_ref[...] = (kept_b[0].astype(F32) + got_b[0].astype(F32)).astype(BF)


def halve(kept, got, mine, order=()):
    count, _, rows, columns = kept.shape
    step = rows
    while step % 32 == 0 and step * columns > 512 * 1024:
        step //= 2
    block = (1, 1, step, columns)
    other = pl.BlockSpec(block, lambda i, j, m: (i, 1 - m[0], j, 0))
    own = pl.BlockSpec(block, lambda i, j, m: (i, m[0], j, 0))
    out = pl.BlockSpec((1, step, columns), lambda i, j, m: (i, j, 0))
    return pl.pallas_call(
        functools.partial(halve_kernel, len(order)),
        grid_spec=pltpu.PrefetchScalarGridSpec(
            num_scalar_prefetch=1,
            grid=(count, rows // step),
            in_specs=[other, own, other, own]
            + [pl.BlockSpec(memory_space=pl.ANY)] * len(order),
            out_specs=[out, out],
        ),
        out_shape=[jax.ShapeDtypeStruct((count, rows, columns), BF)] * 2,
        compiler_params=pltpu.CompilerParams(vmem_limit_bytes=VMEM_BYTES // 3),
        cost_estimate=pl.CostEstimate(flops=1024, bytes_accessed=1024, transcendentals=0),
        name="halve",
    )(mine.astype(jnp.int32)[None], kept, kept, got, got, *order)


def finish_kernel(extra, turned, kept_ref, got_ref, *refs):
    total = kept_ref[...].astype(F32) + got_ref[...].astype(F32)
    refs[extra][...] = total.T if turned else total


def finish(kept, got, turned=False, order=()):
    rows, columns = kept.shape
    fixed = pl.BlockSpec((rows, columns), lambda: (0, 0))
    shape = (columns, rows) if turned else (rows, columns)
    if turned and rows % 128:
        return finish(kept, got, False, order).T
    return pl.pallas_call(
        functools.partial(finish_kernel, len(order), turned),
        in_specs=[fixed, fixed] + [pl.BlockSpec(memory_space=pl.ANY)] * len(order),
        out_specs=pl.BlockSpec(shape, lambda: (0, 0)),
        out_shape=jax.ShapeDtypeStruct(shape, F32),
        compiler_params=pltpu.CompilerParams(vmem_limit_bytes=VMEM_BYTES // 3),
        name="finish",
    )(kept, got, *order)


class Sum:
    def __init__(self, kept, send, axis, bit):
        self.kept = kept
        self.send = send
        self.got = xor_send(send, axis, bit)

    def step(self, shape, axis, bit=1, order=()):
        mine = (lax.axis_index(axis) // bit) % 2
        send, kept = halve(self.kept.reshape(shape), self.got.reshape(shape), mine, order)
        return Sum(kept, send, axis, bit)

    def finish(self, shape, turned=False, order=()):
        return finish(self.kept.reshape(shape), self.got.reshape(shape), turned, order)


def slab_grad_kernel(split, extra, pair, sel_ref, la_ref, lb_ref, ra_ref, rb_ref, *refs):
    if pair:
        rb_ref = [jnp.where(pl.program_id(0) == 0, rb_ref[0], refs[0][0])]
        refs = refs[1:]
    out_ref = refs[extra]
    if split is None:
        out = dot_tn(la_ref[0], ra_ref[0]) + dot_tn(lb_ref[0], rb_ref[0])
    else:
        zs, rows = split
        take = [pl.ds(pl.multiple_of((z * 2 + sel_ref[0]) * rows, rows), rows) for z in range(zs)]
        left = [jnp.concatenate([ref[0, :, t] for t in take], axis=1) for ref in (la_ref, lb_ref)]
        out = dot_tn(left[0], ra_ref[0]) + dot_tn(left[1], rb_ref[0])
    out_ref[0] = out.astype(BF)


def slab_grad(left, right, x, y, order=()):
    left_a, left_b, left_at = left
    right_a, right_b, right_at = right
    pair = isinstance(right_b, tuple)
    _, frames, width = left_a.shape
    hidden = right_a.shape[2]
    zs = lax.axis_size("z")
    rows = width // (2 * zs)
    half = width // 2
    if x is None:
        split = None
        sel = y
        left_block = pl.BlockSpec((1, frames, half), lambda i, s: (left_at, 0, i))
        right = [
            pl.BlockSpec((1, frames, hidden), lambda i, s: (s[0], 0, 0)),
            pl.BlockSpec((1, frames, hidden), lambda i, s: (s[0] + right_at, 0, 0)),
        ]
    else:
        sel = x
        right = [
            pl.BlockSpec((1, frames, hidden), lambda i, s: (i, 0, 0)),
            pl.BlockSpec((1, frames, hidden), lambda i, s: (i + right_at, 0, 0)),
        ]
        if pair:
            right[1:] = [pl.BlockSpec((1, frames, hidden), lambda i, s: (0, 0, 0))] * 2
        if rows % 128 == 0:
            split = (zs, rows)
            left_block = pl.BlockSpec((1, frames, width), lambda i, s: (left_at, 0, 0))
        else:
            split = None
            left_block = pl.BlockSpec((1, frames, half), lambda i, s: (0, 0, 0))
            left_a, left_b = (
                pick(l[left_at].reshape(frames, zs, 2, rows), x, 2).reshape(1, frames, half)
                for l in (left_a, left_b)
            )
    return pl.pallas_call(
        functools.partial(slab_grad_kernel, split, len(order), pair),
        grid_spec=pltpu.PrefetchScalarGridSpec(
            num_scalar_prefetch=1,
            grid=(2,),
            in_specs=[left_block, left_block]
            + right
            + [pl.BlockSpec(memory_space=pl.ANY)] * len(order),
            out_specs=pl.BlockSpec((1, half, hidden), lambda i, s: (i, 0, 0)),
        ),
        out_shape=jax.ShapeDtypeStruct((2, half, hidden), BF),
        compiler_params=pltpu.CompilerParams(vmem_limit_bytes=VMEM_BYTES),
        cost_estimate=pl.CostEstimate(flops=1024, bytes_accessed=1024, transcendentals=0),
        name="slab_grad",
    )(sel.astype(jnp.int32)[None], left_a, left_b, right_a, *(right_b if pair else (right_b,)), *order)


def slab_sum(left, right, first, order=(), kept_order=()):
    place = lax.axis_index(first)
    picks = lambda i: (i, None) if first == "x" else (None, i)
    away = slab_grad(left, right, *picks(1 - place), order)
    return Sum(slab_grad(left, right, *picks(place), (away,) + tuple(kept_order)), away, first, 1)


def slab_second(total, first, order=()):
    zs = lax.axis_size("z")
    _, half, hidden = total.kept.shape
    if first == "x":
        return total.step((1, 2, half, hidden), "y", 1, order)
    return total.step((zs, 2, half // zs, hidden), "x", 1, order)


def z_steps(total, rows, columns, bits=None, order=()):
    zs = lax.axis_size("z")
    for bit in z_bits() if bits is None else bits:
        total = total.step((zs // (2 * bit), 2, rows, columns), "z", bit, order)
    return total


def z_bits():
    bits = []
    while 1 << len(bits) < lax.axis_size("z"):
        bits.append(1 << len(bits))
    return bits


def right_of(ref):
    if len(ref.shape) == 2:
        return ref[...]
    return jnp.concatenate([heads_of(ref, at, at + DH) for at in range(0, ref.shape[2], DH)], axis=1)


def row_grad_kernel(pairs, rows, core_ref, *refs):
    send_ref, keep_ref = refs[-2:]
    at = 0
    for i in range(pairs):
        whole = dot_tn(refs[2 * i][...], right_of(refs[2 * i + 1])).astype(BF)
        columns = whole.shape[1]
        parts = [whole[k * rows : (k + 1) * rows] for k in range(whole.shape[0] // rows)]
        even = jnp.concatenate(parts[0::2], axis=0)
        odd = jnp.concatenate(parts[1::2], axis=0)
        first = core_ref[0] == 0
        keep_ref[:, at : at + columns] = jnp.where(first, even, odd)
        send_ref[:, at : at + columns] = jnp.where(first, odd, even)
        at += columns


def row_grad(core, pairs):
    frames, width = pairs[0][0].shape
    zs = lax.axis_size("z")
    rows = width // (8 * zs)
    columns = sum(right.size // frames for _, right in pairs)
    if rows % 16:
        whole = jnp.concatenate(
            [dot_tn(left, right_of(right)).astype(BF) for left, right in pairs], axis=1
        )
        whole = whole.reshape(4 * zs, 2, rows, columns)
        flat = lambda v: v.reshape(width // 2, columns)
        return flat(pick(whole, 1 - core[0], 1)), flat(pick(whole, core[0], 1))
    tile = 256
    specs, args = [], []
    for left, right in pairs:
        specs += [
            pl.BlockSpec((frames, tile), lambda i, c: (0, i)),
            pl.BlockSpec(right.shape, lambda i, c, n=right.ndim: (0,) * n),
        ]
        args += [left, right]
    out = pl.BlockSpec((tile // 2, columns), lambda i, c: (i, 0))
    return pl.pallas_call(
        functools.partial(row_grad_kernel, len(pairs), rows),
        grid_spec=pltpu.PrefetchScalarGridSpec(
            num_scalar_prefetch=1, grid=(width // tile,), in_specs=specs, out_specs=[out, out]
        ),
        out_shape=[jax.ShapeDtypeStruct((width // 2, columns), BF)] * 2,
        compiler_params=pltpu.CompilerParams(vmem_limit_bytes=VMEM_BYTES),
        cost_estimate=pl.CostEstimate(flops=1024, bytes_accessed=1024, transcendentals=0),
        name="row_grad",
    )(core, *args)


def body(
    block_in,
    out_grad,
    utt_ends,
    valid_ends,
    ffn1_in,
    ffn1_out,
    att_qkv,
    att_out,
    content_bias,
    conv_in,
    conv_out,
    ffn2_in,
    ffn2_out,
    conv_depth,
    norm_gain,
    norm_bias,
):
    zs = lax.axis_size("z")
    devices = 8 * zs
    frames, width = block_in.shape
    heads = width // DH
    z, x, y, c = (lax.axis_index(axis) for axis in DEV)
    place = ((z * 2 + x) * 2 + y) * 2 + c
    head = (x * 2 + y) * 2 + c

    small = jnp.concatenate([norm_gain, norm_bias, conv_depth, content_bias[None]], axis=0)
    small = jnp.broadcast_to(small[None], (devices,) + small.shape)
    small = lax.all_to_all(small, DEV, split_axis=0, concat_axis=0, tiled=True)
    small = small.transpose(1, 0, 2).reshape(small.shape[1], width).astype(F32)
    gains, shifts, taps, q_bias = small[:6], small[6:12], small[12 : 12 + KSIZE], small[12 + KSIZE]

    rows, few = ffn1_in.shape[0], att_qkv.shape[0]
    blocks = lambda w: [w[:, i : i + width] for i in range(0, w.shape[1], width)]

    def gather(*parts):
        mine = jnp.concatenate(parts, axis=0)
        return lax.all_gather(mine, DEV, axis=0, tiled=True).reshape(devices, -1, width)

    w_first = gather(pack_ffn(ffn1_in, ffn1_out), *blocks(att_qkv))
    w_mid = gather(att_out, *blocks(conv_in), conv_out)
    w_second = gather(pack_ffn(ffn2_in, ffn2_out, order=(small,)))
    w_proj = Rows(w_first, 2 * rows, few)
    w_conv = Rows(w_mid, 0, few)
    w_cout = Rows(w_mid, 3 * few, few)
    core = c.astype(jnp.int32)[None]

    all_frames = frames * devices
    first_frame = place * frames
    span = 4 * frames
    group = 8 * frames
    origin = span
    group_first = z * group
    starts = jnp.concatenate([jnp.zeros((1,), jnp.int32), utt_ends[:-1]])
    valid_count = jnp.sum((valid_ends - starts).astype(F32))

    def segments(positions):
        seg = jnp.sum((utt_ends[None, :] <= positions[:, None]).astype(jnp.int32), axis=1)
        valid_seg = jnp.sum((valid_ends[None, :] <= positions[:, None]).astype(jnp.int32), axis=1)
        valid = seg == valid_seg
        return jnp.where(positions < 0, -1, jnp.where(positions >= all_frames, -2, seg)), valid

    ext_seg, ext_valid = segments(
        first_frame - REACH + jnp.arange(frames + 2 * REACH, dtype=jnp.int32)
    )
    own_seg = ext_seg[REACH : REACH + frames]
    ext_valid = ext_valid.astype(F32)
    edge_valid = jnp.concatenate([ext_valid[:REACH], ext_valid[-REACH:]])
    edge_valid = jnp.concatenate([edge_valid, jnp.zeros((frames - 2 * REACH,), F32)])
    columns = jnp.stack(
        [(ext_seg[m : m + frames] == own_seg).astype(F32) for m in range(KSIZE)]
        + [ext_valid[REACH : REACH + frames], edge_valid, jnp.zeros((frames,), F32)],
        axis=1,
    )
    group_pos = group_first + jnp.arange(group, dtype=jnp.int32)
    ended = utt_ends[None, :] <= group_pos[:, None]
    group_seg = jnp.sum(ended.astype(jnp.int32), axis=1)
    group_lo = jnp.max(jnp.where(ended, utt_ends[None, :], 0), axis=1)
    slots = jnp.arange(utt_ends.shape[0], dtype=jnp.int32)
    group_hi = jnp.sum(
        jnp.where(group_seg[:, None] == slots[None, :], valid_ends[None, :], 0), axis=1
    )
    window_first = group_first - origin
    lo_q = group_lo - window_first
    hi_q = group_hi - window_first
    low = (lo_q[::BQ] // 128) * 128
    high = hi_q[BQ - 1 :: BQ]
    lo_q = lo_q.astype(F32)[None, :]
    hi_q = hi_q.astype(F32)[None, :]
    c2 = (32.0 * jnp.exp2(-head.astype(F32)) * (LOG2E / span))[None]

    def vectors(*rows):
        rows = jnp.stack(rows)
        return jnp.concatenate([rows, jnp.zeros((-len(rows) % 8, width), F32)], axis=0)

    count_row = jnp.broadcast_to(valid_count, (width,))

    x1, n2, pack1, s1, d1, q_heads, k_heads, v_heads = first_call(
        core,
        block_in,
        w_first,
        rows,
        w_proj,
        vectors(gains[0], shifts[0], gains[1], shifts[1], q_bias),
    )
    pack1_sib = xor_send(pack1, "c", 1)

    def to_heads(cells):
        got = lax.all_to_all(cells, LAYER, split_axis=0, concat_axis=0, tiled=True)
        return got.reshape(group, cells.shape[2])

    def to_frames(cells):
        cells = cells.reshape(heads, frames, cells.shape[1])
        return lax.all_to_all(cells, LAYER, split_axis=0, concat_axis=0, tiled=True)

    up = [(i, i + 1) for i in range(zs - 1)]
    down = [(i + 1, i) for i in range(zs - 1)]

    def with_edges(cells):
        return lax.ppermute(cells[-span:], "z", up), cells, lax.ppermute(cells[:span], "z", down)

    kv = with_edges(to_heads(k_heads)) + with_edges(to_heads(v_heads))
    q_own = to_heads(q_heads)
    o_own, lse = attn_fwd(q_own, kv, low, high, c2, lo_q, hi_q, origin)
    mixed, x2, n3, lin, sig, gated = gate_call(
        to_frames(o_own), x1, w_conv, vectors(gains[2], shifts[2]), columns
    )
    g_edges = neighbour_rows(gated)
    tap_rows = [taps[m] for m in range(KSIZE)]
    conv, moments = conv_call(gated, *g_edges, vectors(*tap_rows), columns, devices)
    spread = lambda cells: lax.all_to_all(cells, DEV, split_axis=0, concat_axis=0, tiled=True)
    moments = spread(moments)

    final_out, swished, dx3, ew, dz, sums_c, totals, pack2, s2, da2 = second_call(
        core,
        x2,
        conv,
        moments,
        w_cout,
        w_second,
        rows,
        vectors(gains[3], shifts[3], gains[4], shifts[4], gains[5], shifts[5], count_row),
        out_grad,
    )
    totals = spread(totals)
    edges = neighbour_rows(jnp.concatenate([dz[-REACH:], conv[-REACH:]]), jnp.concatenate([dz[:REACH], conv[:REACH]]))
    pack2_sib = xor_send(pack2, "c", 1)
    hidden = pack2.shape[2]
    f2i = slab_sum((pack2, pack2_sib, 0), (da2, pack2_sib, 4), "x")
    f2o = slab_sum((pack2, pack2_sib, 3), (s2, pack2_sib, 1), "y")

    point_grad, dx2, ey, mixed_grad, sums_b = back_call(
        dz,
        conv,
        edges,
        gated,
        g_edges,
        moments,
        totals,
        lin,
        sig,
        x2,
        dx3,
        w_conv,
        vectors(*tap_rows, gains[3], gains[2], gains[2], count_row),
        columns,
        order=(f2i.send, f2o.send),
    )
    do_own = to_heads(mixed_grad)
    send, kept = row_grad(core, [(mixed, ey), (n3, point_grad), (swished, ew)])
    mid = Sum(kept, send, "c", 1)
    dq, dkv_prev, dkv, dkv_next = attn_bwd(
        q_own,
        o_own,
        do_own,
        lse,
        kv,
        low,
        high,
        c2,
        lo_q,
        hi_q,
        origin,
        order=(f2i.kept, f2o.kept, kept),
    )
    dq = to_frames(dq)
    f2i = slab_second(f2i, "x")
    f2o = slab_second(f2o, "y", order=(f2i.send,))
    dkv = join_edges(
        dkv,
        lax.ppermute(dkv_next, "z", up),
        lax.ppermute(dkv_prev, "z", down),
        order=(f2i.send, f2o.send),
    )
    dkv = to_frames(dkv)

    low_z, high_z = z_bits()[:1], z_bits()[1:]
    send, kept = row_grad(core, [(n2, dq), (n2, dkv)])
    qkv = Sum(kept, send, "c", 1)
    mid = mid.step((zs, 2, 2 * few, 4 * width), "x", order=(qkv.send,))
    dx1, ef1, sums_p = proj_back_call(
        dq, dkv, dx2, x1, w_proj, vectors(gains[0], gains[1]), (mid.send,)
    )
    ef1_sib = xor_send(ef1, "c", 1)
    f2i = z_steps(f2i, rows, hidden, low_z, order=(ef1,))
    f2o = z_steps(f2o, rows, hidden, low_z, order=(f2i.send,))
    qkv = z_steps(qkv, 4 * few, 3 * width, low_z, order=(f2o.send,))
    f1o_left, f1o_right = (ef1, ef1_sib, 0), (s1, pack1_sib, 1)
    f1o_away = slab_grad(f1o_left, f1o_right, None, 1 - y, (qkv.send,))
    grad_input, sums_a, da_first, da_second, da1 = last_call(
        core,
        dx1,
        ef1,
        block_in,
        w_first,
        rows,
        d1,
        vectors(gains[0]),
        order=(f1o_away,),
    )
    da_sib = (xor_send(da_first, "c", 1), xor_send(da_second, "c", 1))
    f2i = z_steps(f2i, rows, hidden, high_z, order=(da1,))
    f2o = z_steps(f2o, rows, hidden, high_z, order=(f2i.send,))
    f1i = slab_sum((pack1, pack1_sib, 0), (da1, da_sib, 0), "x", order=(f2o.send,))
    f1o = Sum(slab_grad(f1o_left, f1o_right, None, y, (f1i.kept,)), f1o_away, "y", 1)
    mid = mid.step((zs, 2, few, 4 * width), "y", order=(f1o.kept,))
    f1o = slab_second(f1o, "y", order=(mid.send,))
    qkv = qkv.step((zs, 2, few, 3 * width), "y", order=(f1o.send,))
    mid = z_steps(mid, few, 4 * width, low_z, order=(qkv.send,))
    f1i = slab_second(f1i, "x", order=(mid.send,))
    qkv = z_steps(qkv, 2 * few, 3 * width, high_z, order=(f1i.send,))
    f1o = z_steps(f1o, rows, hidden, low_z, order=(qkv.send,))
    f1i = z_steps(f1i, rows, hidden, low_z, order=(f1o.send,))
    mid = z_steps(mid, few, 4 * width, high_z, order=(f1i.send,))
    qkv = qkv.step((1, 2, few, 3 * width), "x", order=(mid.send,))
    f1o = z_steps(f1o, rows, hidden, high_z, order=(qkv.send,))
    f1i = z_steps(f1i, rows, hidden, high_z, order=(f1o.send,))
    grad_f2i = f2i.finish((rows, hidden), order=(f1i.send,))
    grad_f2o = f2o.finish((rows, hidden), True, order=(f1i.send,))
    mid = mid.finish((few, 4 * width), order=(f1i.send,))
    out_att, out_cin, out_cout = mid[:, :width], mid[:, width : 3 * width], mid[:, 3 * width :]
    out_qkv = qkv.finish((few, 3 * width), order=(f1i.send,))
    grad_f1o = f1o.finish((rows, hidden), True, order=(f1i.send,))
    grad_f1i = f1i.finish((rows, hidden))

    a, b, c, p = 0, 1, 2, 3
    places = [(a, 0), (p, 0), (b, 0), (c, 4), (c, 2), (c, 0)]
    places += [(a, 1), (p, 1), (b, 1), (c, 5), (c, 3), (c, 1)]
    places += [(b, 2 + m) for m in range(KSIZE)] + [(p, 2)]
    rows = stack_rows([sums_a, sums_b, sums_c, sums_p], places, order=(f1o.kept,))
    rows = rows.reshape(rows.shape[0], devices, width // devices).transpose(1, 0, 2)
    rows = jnp.sum(lax.all_to_all(rows, DEV, split_axis=0, concat_axis=0, tiled=True), axis=0)

    return (
        final_out,
        grad_input,
        grad_f1i,
        grad_f1o,
        out_qkv,
        out_att,
        rows[12 + KSIZE],
        out_cin,
        out_cout,
        grad_f2i,
        grad_f2o,
        rows[12 : 12 + KSIZE],
        rows[:6],
        rows[6:12],
    )


def solution(mesh):
    seq, heads = mesh.shape["seq"], mesh.shape["head"]
    grid = Mesh(mesh.devices.reshape(seq // 2, 2, heads // 2, 2), DEV)
    both = P(DEV, None)
    inward = P(("z", "x"), ("y", "c"))
    outward = P(("y", "c"), ("z", "x"))
    columns = P(None, DEV)
    return jax.shard_map(
        body,
        mesh=grid,
        in_specs=(
            both,
            both,
            P(),
            P(),
            inward,
            outward,
            both,
            both,
            P(DEV),
            both,
            both,
            inward,
            outward,
            columns,
            columns,
            columns,
        ),
        out_specs=(
            both,
            both,
            inward,
            outward,
            both,
            both,
            P(DEV),
            both,
            both,
            inward,
            outward,
            columns,
            columns,
            columns,
        ),
        check_vma=False,
    )
```

```python
import functools
import math

import jax
import jax.numpy as jnp
from jax import lax
from jax.experimental import pallas as pl
from jax.experimental.pallas import tpu as pltpu
from jax.sharding import Mesh
from jax.sharding import PartitionSpec as P

DH = 128
KSIZE = 5
REACH = (KSIZE - 1) // 2
EPSILON = 1e-05
MASKED = -1e30
LOG2E = math.log2(math.e)
DEV = ("z", "x", "y", "c")
LAYER = ("x", "y", "c")
BQ = 512
BK = 512
BF = jnp.bfloat16
F32 = jnp.float32
VMEM_BYTES = 56 * 1024 * 1024


def takes(microseconds):
    return pl.CostEstimate(
        flops=1024, bytes_accessed=1024 + int(microseconds * 3.7e6), transcendentals=0
    )


def pick(cells, index, dim):
    return lax.dynamic_index_in_dim(cells, index, dim, keepdims=False)


def xor_send(cells, axis, bit):
    count = lax.axis_size(axis)
    return lax.ppermute(cells, axis, [(i, i ^ bit) for i in range(count)])


def neighbour_rows(tail, head=None):
    if head is None:
        tail, head = tail[-REACH:], tail[:REACH]
    count = 1
    for axis in DEV:
        count *= lax.axis_size(axis)
    before = lax.ppermute(tail, DEV, [(i, i + 1) for i in range(count - 1)])
    after = lax.ppermute(head, DEV, [(i + 1, i) for i in range(count - 1)])
    return before, after


def dot_nn(a, b):
    return lax.dot_general(a, b, (((1,), (0,)), ((), ())), preferred_element_type=F32)


def dot_nt(a, b):
    return lax.dot_general(a, b, (((1,), (1,)), ((), ())), preferred_element_type=F32)


def dot_tn(a, b):
    return lax.dot_general(a, b, (((0,), (0,)), ((), ())), preferred_element_type=F32)


def norm_stats(values):
    centred = values - jnp.mean(values, axis=-1, keepdims=True)
    inv_std = lax.rsqrt(jnp.mean(centred * centred, axis=-1, keepdims=True) + EPSILON)
    return centred * inv_std, inv_std


def norm_back(upstream, normed, inv_std, gain):
    scaled = upstream * gain
    inner = (
        scaled
        - jnp.mean(scaled, axis=-1, keepdims=True)
        - normed * jnp.mean(scaled * normed, axis=-1, keepdims=True)
    )
    return inv_std * inner


def pack_kernel(extra, in_ref, out_ref, *refs):
    rows = in_ref.shape[0]
    refs[extra][:rows] = in_ref[...]
    refs[extra][rows:] = out_ref[...].T


def pack_ffn(w_in, w_out, order=()):
    rows, width = w_in.shape
    whole = lambda v: pl.BlockSpec(v.shape, lambda: (0, 0))
    if rows % 128:
        return jnp.concatenate([w_in, w_out.T], axis=0)
    return pl.pallas_call(
        functools.partial(pack_kernel, len(order)),
        in_specs=[whole(w_in), whole(w_out)] + [pl.BlockSpec(memory_space=pl.ANY)] * len(order),
        out_specs=pl.BlockSpec((2 * rows, width), lambda: (0, 0)),
        out_shape=jax.ShapeDtypeStruct((2 * rows, width), BF),
        name="pack_ffn",
    )(w_in, w_out, *order)


class Rows:
    def __init__(self, gathered, first, count):
        self.stepped = count % 16 == 0 and first % count == 0
        devices, _, width = gathered.shape
        self.count = count
        if self.stepped:
            self.at = first // count
            self.array = gathered
            self.block = (devices, count, width)
        else:
            self.first = first
            self.gathered = gathered
            self.width = width

    def blocks(self, pick_block, total):
        if self.stepped:
            at = self.at
            return self.array, pl.BlockSpec(self.block, lambda j, *_: (0, at + pick_block(j), 0))
        cut = [
            self.gathered[:, self.first + i * self.count : self.first + (i + 1) * self.count]
            for i in range(total)
        ]
        cut = jnp.stack([v.reshape(-1, self.width) for v in cut])
        return cut, pl.BlockSpec((1,) + cut.shape[1:], lambda j, *_: (pick_block(j), 0, 0))


def square(ref):
    return ref[...].reshape(-1, ref.shape[-1])


def slab_of(step, core):
    return (step % 2) * 2 + jnp.where(step < 2, 1 - core, core)


def slab_specs(gathered, rows, step_of):
    devices, total, width = gathered.shape
    array = gathered.reshape(devices // 4, 4, total, width)
    block = (devices // 4, 1, rows, width)
    specs = [
        pl.BlockSpec(block, lambda j, c, i=i: (0, slab_of(step_of(j), c[0]), i, 0)) for i in (0, 1)
    ]
    return [array, array], specs


def heads_of(ref, lo, hi):
    return jnp.concatenate([ref[h, :, lo:hi] for h in range(ref.shape[0])], axis=1)


def forward_slab(n, w1_ref, w2_ref, s_ref, d_out):
    width = n.shape[1]
    w1 = square(w1_ref)
    chunk = 256
    for at in range(0, width, chunk):
        a = dot_nn(n, w1[:, at : at + chunk])
        sig = jax.nn.sigmoid(a)
        s_ref[:, at : at + chunk] = (a * sig).astype(BF)
        d_out[:, at : at + chunk] = (sig * (1.0 + a * (1.0 - sig))).astype(BF)
    return dot_nt(s_ref[...], square(w2_ref))


def backward_slab(ef, w1_ref, w2_ref, d_in, da_ref):
    width = ef.shape[1]
    w2 = square(w2_ref)
    chunk = 256
    for at in range(0, width, chunk):
        ds = dot_nn(ef, w2[:, at : at + chunk])
        da_ref[:, at : at + chunk] = (ds * d_in[:, at : at + chunk].astype(F32)).astype(BF)
    return dot_nt(da_ref[...], square(w1_ref))


def keep_slab(step, cells, pack_ref, pack_at, own_ref):
    @pl.when(step < 2)
    def _():
        pack_ref[pack_at + step] = cells

    @pl.when(step >= 2)
    def _():
        own_ref[0] = cells


def first_kernel(
    core_ref,
    x_ref,
    w1_ref,
    w2_ref,
    wp_ref,
    vec_ref,
    x1_ref,
    n2_ref,
    pack_ref,
    own_ref,
    d_ref,
    q_ref,
    k_ref,
    v_ref,
    acc_ref,
    s_ref,
):
    step = pl.program_id(0)

    @pl.when(step == 0)
    def _():
        normed, _ = norm_stats(x_ref[...].astype(F32))
        pack_ref[0] = (normed * vec_ref[0:1, :] + vec_ref[1:2, :]).astype(BF)
        acc_ref[...] = jnp.zeros_like(acc_ref)

    @pl.when(step < 4)
    def _():
        acc_ref[...] += forward_slab(pack_ref[0], w1_ref, w2_ref, s_ref, d_ref.at[0])
        keep_slab(step, s_ref[...], pack_ref, 1, own_ref)

    @pl.when(step == 3)
    def _():
        x1 = x_ref[...].astype(F32) + 0.5 * acc_ref[...]
        x1_ref[...] = x1
        normed, _ = norm_stats(x1)
        n2_ref[...] = (normed * vec_ref[2:3, :] + vec_ref[3:4, :]).astype(BF)

    for part, ref in enumerate((q_ref, k_ref, v_ref)):

        @pl.when(step == 4 + part)
        def _():
            projected = dot_nn(n2_ref[...], square(wp_ref))
            if part == 0:
                projected = projected + vec_ref[4:5, :]
            projected = projected.astype(BF)
            for h in range(ref.shape[0]):
                ref[h] = projected[:, h * DH : (h + 1) * DH]


def first_call(core, x, gathered, rows, proj, vectors):
    frames, width = x.shape
    heads = width // DH
    fixed = lambda *shape: pl.BlockSpec(shape, lambda j, c: (0,) * len(shape))
    slabs, slab_blocks = slab_specs(gathered, rows, lambda j: jnp.minimum(j, 3))
    proj_array, proj_block = proj.blocks(lambda j: jnp.clip(j - 4, 0, 2), 3)
    return pl.pallas_call(
        first_kernel,
        grid_spec=pltpu.PrefetchScalarGridSpec(
            num_scalar_prefetch=1,
            grid=(7,),
            in_specs=[fixed(frames, width)] + slab_blocks + [proj_block, fixed(*vectors.shape)],
            out_specs=[
                fixed(frames, width),
                fixed(frames, width),
                fixed(3, frames, width),
                pl.BlockSpec((1, frames, width), lambda j, c: (jnp.clip(j - 2, 0, 1), 0, 0)),
                pl.BlockSpec((1, frames, width), lambda j, c: (jnp.minimum(j, 3), 0, 0)),
                fixed(heads, frames, DH),
                fixed(heads, frames, DH),
                fixed(heads, frames, DH),
            ],
            scratch_shapes=[pltpu.VMEM((frames, width), F32), pltpu.VMEM((frames, width), BF)],
        ),
        out_shape=[
            jax.ShapeDtypeStruct((frames, width), F32),
            jax.ShapeDtypeStruct((frames, width), BF),
            jax.ShapeDtypeStruct((3, frames, width), BF),
            jax.ShapeDtypeStruct((2, frames, width), BF),
            jax.ShapeDtypeStruct((4, frames, width), BF),
            jax.ShapeDtypeStruct((heads, frames, DH), BF),
            jax.ShapeDtypeStruct((heads, frames, DH), BF),
            jax.ShapeDtypeStruct((heads, frames, DH), BF),
        ],
        compiler_params=pltpu.CompilerParams(vmem_limit_bytes=VMEM_BYTES),
        cost_estimate=pl.CostEstimate(
            flops=22 * frames * width * width,
            bytes_accessed=22 * width * width + 40 * frames * width,
            transcendentals=4 * frames * width,
        ),
        name="first_part",
    )(core, x, *slabs, proj_array, vectors)


def gate_kernel(extra, mh_ref, x1_ref, w_ref, vec_ref, cols_ref, *refs):
    mixed_ref, x2_ref, n3_ref, lin_ref, sig_ref, g_ref = refs[extra:]
    step = pl.program_id(0)

    @pl.when(step == 0)
    def _():
        mixed = heads_of(mh_ref, 0, DH)
        mixed_ref[...] = mixed
        x2 = x1_ref[...] + dot_nn(mixed, square(w_ref))
        x2_ref[...] = x2
        normed, _ = norm_stats(x2)
        n3_ref[...] = (normed * vec_ref[0:1, :] + vec_ref[1:2, :]).astype(BF)

    @pl.when(step == 1)
    def _():
        lin_ref[...] = dot_nn(n3_ref[...], square(w_ref))

    @pl.when(step == 2)
    def _():
        sig = jax.nn.sigmoid(dot_nn(n3_ref[...], square(w_ref)))
        sig_ref[...] = sig
        g_ref[...] = (lin_ref[...] * sig * cols_ref[:, KSIZE : KSIZE + 1]).astype(BF)


def gate_call(mixed_heads, x1, weights, vectors, columns, order=()):
    frames, width = x1.shape
    fixed = lambda *shape: pl.BlockSpec(shape, lambda j: (0,) * len(shape))
    array, block = weights.blocks(lambda j: j, 3)
    return pl.pallas_call(
        functools.partial(gate_kernel, len(order)),
        grid=(3,),
        in_specs=[
            fixed(*mixed_heads.shape),
            fixed(frames, width),
            block,
            fixed(*vectors.shape),
            fixed(*columns.shape),
        ]
        + [pl.BlockSpec(memory_space=pl.ANY)] * len(order),
        out_specs=[fixed(frames, width)] * 6,
        out_shape=[jax.ShapeDtypeStruct((frames, width), t) for t in (BF, F32, BF, F32, F32, BF)],
        compiler_params=pltpu.CompilerParams(vmem_limit_bytes=VMEM_BYTES),
        cost_estimate=pl.CostEstimate(
            flops=6 * frames * width * width,
            bytes_accessed=6 * width * width + 24 * frames * width,
            transcendentals=frames * width,
        ),
        name="attention_out_and_gate",
    )(mixed_heads, x1, array, vectors, columns, *order)


PAD = 8


def lay_out(scratch, before, cells, after):
    frames = cells.shape[0]
    scratch[PAD - REACH : PAD, :] = before
    scratch[PAD : PAD + frames, :] = cells
    scratch[PAD + frames : PAD + frames + REACH, :] = after


def conv_kernel(g_ref, before_ref, after_ref, vec_ref, cols_ref, conv_ref, sums_ref, ext):
    frames = g_ref.shape[0]
    lay_out(
        ext, before_ref[...].astype(F32), g_ref[...].astype(F32), after_ref[...].astype(F32)
    )
    conv = jnp.zeros(g_ref.shape, F32)
    for m in range(KSIZE):
        rows = ext[PAD - REACH + m : PAD - REACH + m + frames, :]
        conv = conv + vec_ref[m : m + 1, :] * rows * cols_ref[:, m : m + 1]
    conv_ref[...] = conv
    counted = conv * cols_ref[:, KSIZE : KSIZE + 1]
    sums = jnp.concatenate(
        [jnp.sum(counted, axis=0, keepdims=True), jnp.sum(counted * conv, axis=0, keepdims=True)]
    )
    sums_ref[...] = jnp.broadcast_to(sums[None], sums_ref.shape)


def conv_call(g, before, after, taps, columns, devices):
    frames, width = g.shape
    return pl.pallas_call(
        conv_kernel,
        out_shape=[
            jax.ShapeDtypeStruct((frames, width), F32),
            jax.ShapeDtypeStruct((devices, 2, width), F32),
        ],
        scratch_shapes=[pltpu.VMEM((frames + 2 * PAD, width), F32)],
        compiler_params=pltpu.CompilerParams(vmem_limit_bytes=VMEM_BYTES),
        cost_estimate=pl.CostEstimate(
            flops=20 * frames * width, bytes_accessed=8 * frames * width, transcendentals=0
        ),
        name="depthwise",
    )(g, before, after, taps, columns)


def batch_stats(moments_ref, count):
    sums = jnp.sum(moments_ref[...], axis=0)
    mean = sums[0:1, :] / count
    return mean, lax.rsqrt(sums[1:2, :] / count - mean * mean + EPSILON)


def second_kernel(
    core_ref,
    x2_ref,
    conv_ref,
    mom_ref,
    wc_ref,
    w1_ref,
    w2_ref,
    vec_ref,
    og_ref,
    out_ref,
    swish_ref,
    dx_ref,
    ew_ref,
    dz_ref,
    sums_ref,
    spread_ref,
    pack_ref,
    s_own_ref,
    da_own_ref,
    x3_ref,
    acc_ref,
    d_ref,
    dsilu_ref,
    s_ref,
    dx4_ref,
):
    step = pl.program_id(0)
    count = vec_ref[6:7, :]

    @pl.when(step == 0)
    def _():
        mean, inv = batch_stats(mom_ref, count)
        z = (conv_ref[...] - mean) * inv * vec_ref[0:1, :] + vec_ref[1:2, :]
        sig = jax.nn.sigmoid(z)
        swish = (z * sig).astype(BF)
        swish_ref[...] = swish
        dsilu_ref[...] = sig * (1.0 + z * (1.0 - sig))
        x3 = x2_ref[...] + dot_nn(swish, square(wc_ref))
        x3_ref[...] = x3
        normed, _ = norm_stats(x3)
        pack_ref[0] = (normed * vec_ref[2:3, :] + vec_ref[3:4, :]).astype(BF)
        acc_ref[...] = jnp.zeros_like(acc_ref)

    @pl.when(step < 4)
    def _():
        acc_ref[...] += forward_slab(pack_ref[0], w1_ref, w2_ref, s_ref, d_ref.at[step])
        keep_slab(step, s_ref[...], pack_ref, 1, s_own_ref)

    @pl.when(step == 3)
    def _():
        normed, inv_std = norm_stats(x3_ref[...] + 0.5 * acc_ref[...])
        gain = vec_ref[4:5, :]
        out_ref[...] = (normed * gain + vec_ref[5:6, :]).astype(BF)
        upstream = og_ref[...].astype(F32)
        dx4 = norm_back(upstream, normed, inv_std, gain)
        dx4_ref[...] = dx4
        pack_ref[3] = (0.5 * dx4).astype(BF)
        sums_ref[0:1, :] = jnp.sum(upstream * normed, axis=0, keepdims=True)
        sums_ref[1:2, :] = jnp.sum(upstream, axis=0, keepdims=True)
        acc_ref[...] = jnp.zeros_like(acc_ref)

    @pl.when(step >= 4)
    def _():
        acc_ref[...] += backward_slab(pack_ref[3], w1_ref, w2_ref, d_ref.at[step - 4], s_ref)
        keep_slab(step - 4, s_ref[...], pack_ref, 4, da_own_ref)

    @pl.when(step == 7)
    def _():
        normed, inv_std = norm_stats(x3_ref[...])
        dn = acc_ref[...]
        dx3 = dx4_ref[...] + norm_back(dn, normed, inv_std, vec_ref[2:3, :])
        dx_ref[...] = dx3
        sums_ref[2:3, :] = jnp.sum(dn * normed, axis=0, keepdims=True)
        sums_ref[3:4, :] = jnp.sum(dn, axis=0, keepdims=True)
        ew = dx3.astype(BF)
        ew_ref[...] = ew
        dz = dot_nt(ew, square(wc_ref)) * dsilu_ref[...]
        dz_ref[...] = dz
        mean, inv = batch_stats(mom_ref, count)
        zhat = (conv_ref[...] - mean) * inv
        totals = jnp.concatenate(
            [jnp.sum(dz * zhat, axis=0, keepdims=True), jnp.sum(dz, axis=0, keepdims=True)]
        )
        sums_ref[4:6, :] = totals
        sums_ref[6:8, :] = jnp.zeros((2, dz.shape[1]), F32)
        spread_ref[...] = jnp.broadcast_to(totals[None], spread_ref.shape)


def second_call(core, x2, conv, moments, weights, gathered, rows, vectors, out_grad):
    frames, width = x2.shape
    fixed = lambda *shape: pl.BlockSpec(shape, lambda j, c: (0,) * len(shape))
    slabs, slab_blocks = slab_specs(gathered, rows, lambda j: j % 4)
    array, block = weights.blocks(lambda j: 0, 1)
    whole = fixed(frames, width)
    return pl.pallas_call(
        second_kernel,
        grid_spec=pltpu.PrefetchScalarGridSpec(
            num_scalar_prefetch=1,
            grid=(8,),
            in_specs=[whole, whole, fixed(*moments.shape), block]
            + slab_blocks
            + [fixed(*vectors.shape), whole],
            out_specs=[
                whole,
                whole,
                whole,
                whole,
                whole,
                fixed(8, width),
                fixed(*moments.shape),
                fixed(6, frames, width),
                pl.BlockSpec((1, frames, width), lambda j, c: (jnp.clip(j - 2, 0, 1), 0, 0)),
                pl.BlockSpec((1, frames, width), lambda j, c: (jnp.clip(j - 6, 0, 1), 0, 0)),
            ],
            scratch_shapes=[
                pltpu.VMEM((frames, width), F32),
                pltpu.VMEM((frames, width), F32),
                pltpu.VMEM((4, frames, width), BF),
                pltpu.VMEM((frames, width), F32),
                pltpu.VMEM((frames, width), BF),
                pltpu.VMEM((frames, width), F32),
            ],
        ),
        out_shape=[
            jax.ShapeDtypeStruct((frames, width), BF),
            jax.ShapeDtypeStruct((frames, width), BF),
            jax.ShapeDtypeStruct((frames, width), F32),
            jax.ShapeDtypeStruct((frames, width), BF),
            jax.ShapeDtypeStruct((frames, width), F32),
            jax.ShapeDtypeStruct((8, width), F32),
            jax.ShapeDtypeStruct(moments.shape, F32),
            jax.ShapeDtypeStruct((6, frames, width), BF),
            jax.ShapeDtypeStruct((2, frames, width), BF),
            jax.ShapeDtypeStruct((2, frames, width), BF),
        ],
        compiler_params=pltpu.CompilerParams(vmem_limit_bytes=VMEM_BYTES),
        cost_estimate=pl.CostEstimate(
            flops=36 * frames * width * width,
            bytes_accessed=34 * width * width + 40 * frames * width,
            transcendentals=5 * frames * width,
        ),
        name="second_part",
    )(core, x2, conv, moments, array, *slabs, vectors, out_grad)


def back_kernel(
    extra,
    dz_ref,
    conv_ref,
    edge_before_ref,
    edge_after_ref,
    g_ref,
    g_before_ref,
    g_after_ref,
    mom_ref,
    tot_ref,
    lin_ref,
    sig_ref,
    x2_ref,
    dx3_ref,
    w_ref,
    vec_ref,
    cols_ref,
    *refs,
):
    pg_ref, dx2_ref, ey_ref, do_ref, sums_ref, ext, g_ext, acc_ref, b_ref = refs[extra:]
    step = pl.program_id(0)
    frames, width = dz_ref.shape

    @pl.when(step == 0)
    def _():
        count = vec_ref[8:9, :]
        gain = vec_ref[5:6, :]
        mean, inv = batch_stats(mom_ref, count)
        totals = jnp.sum(tot_ref[...], axis=0) * gain

        def conv_grad(dz, conv, valid):
            zhat = (conv - mean) * inv
            dc = inv * (dz * gain - valid * (totals[1:2, :] + zhat * totals[0:1, :]) / count)
            return dc.astype(BF).astype(F32)

        valid = cols_ref[:, KSIZE : KSIZE + 1]
        dc = conv_grad(dz_ref[...], conv_ref[...], valid)
        edges = []
        for at, ref in ((0, edge_before_ref), (REACH, edge_after_ref)):
            edges.append(
                conv_grad(
                    ref[0:REACH, :],
                    ref[REACH : 2 * REACH, :],
                    cols_ref[at : at + REACH, KSIZE + 1 : KSIZE + 2],
                )
            )
        lay_out(ext, edges[0], dc, edges[1])
        lay_out(
            g_ext,
            g_before_ref[...].astype(F32),
            g_ref[...].astype(F32),
            g_after_ref[...].astype(F32),
        )
        dg = jnp.zeros((frames, width), F32)
        for m in range(KSIZE):
            back = 2 * REACH - m
            rows = ext[PAD - REACH + back : PAD - REACH + back + frames, :]
            dg = dg + vec_ref[m : m + 1, :] * rows * cols_ref[:, back : back + 1]
            there = g_ext[PAD - REACH + m : PAD - REACH + m + frames, :]
            sums_ref[2 + m : 3 + m, :] = jnp.sum(
                dc * there * cols_ref[:, m : m + 1], axis=0, keepdims=True
            )
        sums_ref[7:8, :] = jnp.zeros((1, width), F32)
        de = dg * valid
        sig = sig_ref[...]
        pa = (de * sig).astype(BF)
        pb = (de * lin_ref[...] * sig * (1.0 - sig)).astype(BF)
        pg_ref[:, :width] = pa
        pg_ref[:, width:] = pb
        b_ref[...] = pb
        acc_ref[...] = dot_nt(pa, square(w_ref))

    @pl.when(step == 1)
    def _():
        dn = acc_ref[...] + dot_nt(b_ref[...], square(w_ref))
        normed, inv_std = norm_stats(x2_ref[...])
        dx2 = dx3_ref[...] + norm_back(dn, normed, inv_std, vec_ref[6:7, :])
        dx2_ref[...] = dx2
        ey_ref[...] = dx2.astype(BF)
        sums_ref[0:1, :] = jnp.sum(dn * normed, axis=0, keepdims=True)
        sums_ref[1:2, :] = jnp.sum(dn, axis=0, keepdims=True)

    @pl.when(step == 2)
    def _():
        grads = dot_nt(ey_ref[...], square(w_ref)).astype(BF)
        for h in range(do_ref.shape[0]):
            do_ref[h] = grads[:, h * DH : (h + 1) * DH]


def back_call(dz, conv, edges, g, g_edges, moments, totals, lin, sig, x2, dx3, weights, vectors, columns, order):
    frames, width = dz.shape
    fixed = lambda *shape: pl.BlockSpec(shape, lambda j: (0,) * len(shape))
    array, block = weights.blocks(lambda j: (j + 1) % 3, 3)
    whole = fixed(frames, width)
    return pl.pallas_call(
        functools.partial(back_kernel, len(order)),
        grid=(3,),
        in_specs=[
            whole,
            whole,
            fixed(2 * REACH, width),
            fixed(2 * REACH, width),
            whole,
            fixed(REACH, width),
            fixed(REACH, width),
            fixed(*moments.shape),
            fixed(*totals.shape),
            whole,
            whole,
            whole,
            whole,
            block,
            fixed(*vectors.shape),
            fixed(*columns.shape),
        ]
        + [pl.BlockSpec(memory_space=pl.ANY)] * len(order),
        out_specs=[
            fixed(frames, 2 * width),
            whole,
            whole,
            fixed(width // DH, frames, DH),
            fixed(8, width),
        ],
        out_shape=[
            jax.ShapeDtypeStruct((frames, 2 * width), BF),
            jax.ShapeDtypeStruct((frames, width), F32),
            jax.ShapeDtypeStruct((frames, width), BF),
            jax.ShapeDtypeStruct((width // DH, frames, DH), BF),
            jax.ShapeDtypeStruct((8, width), F32),
        ],
        scratch_shapes=[
            pltpu.VMEM((frames + 2 * PAD, width), F32),
            pltpu.VMEM((frames + 2 * PAD, width), F32),
            pltpu.VMEM((frames, width), F32),
            pltpu.VMEM((frames, width), BF),
        ],
        compiler_params=pltpu.CompilerParams(vmem_limit_bytes=VMEM_BYTES),
        cost_estimate=pl.CostEstimate(
            flops=6 * frames * width * width,
            bytes_accessed=6 * width * width + 34 * frames * width,
            transcendentals=0,
        ),
        name="convolution_backward",
    )(
        dz,
        conv,
        edges[0],
        edges[1],
        g,
        g_edges[0],
        g_edges[1],
        moments,
        totals,
        lin,
        sig,
        x2,
        dx3,
        array,
        vectors,
        columns,
        *order,
    )


def proj_back_kernel(extra, dq_ref, dkv_ref, dx2_ref, x1_ref, wp_ref, vec_ref, *refs):
    dx1_ref, ef_ref, sums_ref, acc_ref = refs[extra:]
    step = pl.program_id(0)

    @pl.when(step == 0)
    def _():
        dq = heads_of(dq_ref, 0, DH)
        acc_ref[...] = dot_nt(dq, square(wp_ref))
        sums_ref[2:3, :] = jnp.sum(dq.astype(F32), axis=0, keepdims=True)
        sums_ref[3:8, :] = jnp.zeros((5, dq.shape[1]), F32)

    @pl.when(step == 1)
    def _():
        acc_ref[...] += dot_nt(heads_of(dkv_ref, 0, DH), square(wp_ref))

    @pl.when(step == 2)
    def _():
        dn = acc_ref[...] + dot_nt(heads_of(dkv_ref, DH, 2 * DH), square(wp_ref))
        normed, inv_std = norm_stats(x1_ref[...])
        dx1 = dx2_ref[...] + norm_back(dn, normed, inv_std, vec_ref[1:2, :])
        dx1_ref[...] = dx1
        ef_ref[0] = (0.5 * dx1).astype(BF)
        sums_ref[0:1, :] = jnp.sum(dn * normed, axis=0, keepdims=True)
        sums_ref[1:2, :] = jnp.sum(dn, axis=0, keepdims=True)


def proj_back_call(dq, dkv, dx2, x1, proj, vectors, order):
    frames, width = x1.shape
    fixed = lambda *shape: pl.BlockSpec(shape, lambda j: (0,) * len(shape))
    array, block = proj.blocks(lambda j: j, 3)
    whole = fixed(frames, width)
    return pl.pallas_call(
        functools.partial(proj_back_kernel, len(order)),
        grid=(3,),
        in_specs=[fixed(*dq.shape), fixed(*dkv.shape), whole, whole, block, fixed(*vectors.shape)]
        + [pl.BlockSpec(memory_space=pl.ANY)] * len(order),
        out_specs=[whole, fixed(1, frames, width), fixed(8, width)],
        out_shape=[
            jax.ShapeDtypeStruct((frames, width), F32),
            jax.ShapeDtypeStruct((1, frames, width), BF),
            jax.ShapeDtypeStruct((8, width), F32),
        ],
        scratch_shapes=[pltpu.VMEM((frames, width), F32)],
        compiler_params=pltpu.CompilerParams(vmem_limit_bytes=VMEM_BYTES),
        cost_estimate=takes(9),
        name="projections_backward",
    )(dq, dkv, dx2, x1, array, vectors, *order)


def last_kernel(extra, core_ref, dx1_ref, ef_ref, x_ref, w1_ref, w2_ref, d_ref, vec_ref, *refs):
    gin_ref, sums_ref, first_ref, second_ref, own_ref, acc_ref, da_ref = refs[extra:]
    step = pl.program_id(0)

    @pl.when(step == 0)
    def _():
        acc_ref[...] = jnp.zeros_like(acc_ref)

    acc_ref[...] += backward_slab(ef_ref[0], w1_ref, w2_ref, d_ref.at[0], da_ref)
    for at, ref in enumerate((first_ref, second_ref)):

        @pl.when(step == at)
        def _():
            ref[0] = da_ref[...]

    @pl.when(step >= 2)
    def _():
        own_ref[0] = da_ref[...]

    @pl.when(step == 3)
    def _():
        normed, inv_std = norm_stats(x_ref[...].astype(F32))
        dn = acc_ref[...]
        dx = dx1_ref[...] + norm_back(dn, normed, inv_std, vec_ref[0:1, :])
        gin_ref[...] = dx.astype(BF)
        sums_ref[0:1, :] = jnp.sum(dn * normed, axis=0, keepdims=True)
        sums_ref[1:2, :] = jnp.sum(dn, axis=0, keepdims=True)
        sums_ref[2:8, :] = jnp.zeros((6, dn.shape[1]), F32)


def last_call(core, dx1, ef, x, gathered, rows, slope, vectors, order):
    frames, width = x.shape
    fixed = lambda *shape: pl.BlockSpec(shape, lambda j, c: (0,) * len(shape))
    slabs, slab_blocks = slab_specs(gathered, rows, lambda j: j)
    whole = fixed(frames, width)
    return pl.pallas_call(
        functools.partial(last_kernel, len(order)),
        grid_spec=pltpu.PrefetchScalarGridSpec(
            num_scalar_prefetch=1,
            grid=(4,),
            in_specs=[whole, fixed(1, frames, width), whole]
            + slab_blocks
            + [pl.BlockSpec((1, frames, width), lambda j, c: (j, 0, 0)), fixed(*vectors.shape)]
            + [pl.BlockSpec(memory_space=pl.ANY)] * len(order),
            out_specs=[
                whole,
                fixed(8, width),
                fixed(1, frames, width),
                fixed(1, frames, width),
                pl.BlockSpec((1, frames, width), lambda j, c: (jnp.clip(j - 2, 0, 1), 0, 0)),
            ],
            scratch_shapes=[pltpu.VMEM((frames, width), F32), pltpu.VMEM((frames, width), BF)],
        ),
        out_shape=[
            jax.ShapeDtypeStruct((frames, width), BF),
            jax.ShapeDtypeStruct((8, width), F32),
            jax.ShapeDtypeStruct((1, frames, width), BF),
            jax.ShapeDtypeStruct((1, frames, width), BF),
            jax.ShapeDtypeStruct((2, frames, width), BF),
        ],
        compiler_params=pltpu.CompilerParams(vmem_limit_bytes=VMEM_BYTES),
        cost_estimate=takes(15),
        name="last_part",
    )(core, dx1, ef, x, *slabs, slope, vectors, *order)


def fill_window(kv_ref, parts):
    for column, refs in ((0, parts[:3]), (DH, parts[3:])):
        at = 0
        for ref in refs:
            kv_ref[at : at + ref.shape[0], column : column + DH] = ref[...]
            at += ref.shape[0]
    kv_ref[at:, :] = jnp.zeros((kv_ref.shape[0] - at, kv_ref.shape[1]), kv_ref.dtype)


def attn_fwd_kernel(
    origin,
    low_ref,
    high_ref,
    c2_ref,
    q_ref,
    *refs,
):
    lo_ref, hi_ref, o_ref, lse_ref, kv_ref = refs[6:]
    block = pl.program_id(0)

    @pl.when(block == 0)
    def _():
        fill_window(kv_ref, refs[:6])

    rows = q_ref.shape[0]
    q = q_ref[...]
    c1 = LOG2E * DH**-0.5
    c2 = c2_ref[0]
    at = lax.broadcasted_iota(jnp.int32, (1, rows), 1) + (origin + block * rows)
    q_pos = at.astype(F32)
    lo_q, hi_q = lo_ref[...], hi_ref[...]
    first = low_ref[block]
    steps = (high_ref[block] - first + (BK - 1)) // BK

    def step(t, carry):
        top, total, mixed = carry
        start = pl.multiple_of(first + t * BK, 128)
        k = kv_ref[pl.ds(start, BK), :DH]
        v = kv_ref[pl.ds(start, BK), DH:]
        k_pos = (lax.broadcasted_iota(jnp.int32, (BK, 1), 0) + start).astype(F32)
        scores = dot_nt(k, q) * c1 - jnp.abs(k_pos - q_pos) * c2
        scores = jnp.where((k_pos >= lo_q) & (k_pos < hi_q), scores, MASKED)
        new_top = jnp.maximum(top, jnp.max(scores, axis=0, keepdims=True))
        expo = jnp.exp2(scores - new_top)
        keep = jnp.exp2(top - new_top)
        total = total * keep + jnp.sum(expo, axis=0, keepdims=True)
        mixed = mixed * keep + dot_tn(v, expo.astype(BF))
        return new_top, total, mixed

    top, total, mixed = lax.fori_loop(
        0,
        steps,
        step,
        (
            jnp.full((1, rows), MASKED, F32),
            jnp.zeros((1, rows), F32),
            jnp.zeros((DH, rows), F32),
        ),
    )
    o_ref[...] = (mixed / total).T.astype(BF)
    lse_ref[...] = top + jnp.log2(total)


def attn_fwd(q, kv, low, high, c2, lo_q, hi_q, origin):
    frames = q.shape[0]
    window = sum(v.shape[0] for v in kv[:3]) + BK
    parts = [pl.BlockSpec(v.shape, lambda i, *_: (0, 0)) for v in kv]
    blocks = frames // BQ
    pairs = frames * 1024 * DH
    grid_spec = pltpu.PrefetchScalarGridSpec(
        num_scalar_prefetch=3,
        grid=(blocks,),
        in_specs=[
            pl.BlockSpec((BQ, DH), lambda i, *_: (i, 0)),
            *parts,
            pl.BlockSpec((1, BQ), lambda i, *_: (0, i)),
            pl.BlockSpec((1, BQ), lambda i, *_: (0, i)),
        ],
        out_specs=[
            pl.BlockSpec((BQ, DH), lambda i, *_: (i, 0)),
            pl.BlockSpec((1, BQ), lambda i, *_: (0, i)),
        ],
        scratch_shapes=[pltpu.VMEM((window, 2 * DH), BF)],
    )

    def kernel(*refs):
        attn_fwd_kernel(origin, *refs)

    return pl.pallas_call(
        kernel,
        grid_spec=grid_spec,
        out_shape=[
            jax.ShapeDtypeStruct((frames, DH), BF),
            jax.ShapeDtypeStruct((1, frames), F32),
        ],
        compiler_params=pltpu.CompilerParams(vmem_limit_bytes=VMEM_BYTES),
        cost_estimate=pl.CostEstimate(
            flops=4 * pairs, bytes_accessed=4 * window * DH, transcendentals=frames * 1024
        ),
        name="attention_forward",
    )(low, high, c2, q, *kv, lo_q, hi_q)


def attn_bwd_kernel(
    origin,
    extra,
    low_ref,
    high_ref,
    c2_ref,
    q_ref,
    o_ref,
    do_ref,
    lse_ref,
    lo_ref,
    hi_ref,
    *refs,
):
    dq_ref, prev_ref, own_ref, next_ref, dk_acc, dv_acc, kv_ref = refs[6 + extra :]
    block = pl.program_id(0)
    rows = q_ref.shape[0]
    frames = own_ref.shape[0]
    scale = DH**-0.5
    c1 = LOG2E * scale

    @pl.when(block == 0)
    def _():
        fill_window(kv_ref, refs[:6])
        dk_acc[...] = jnp.zeros_like(dk_acc)
        dv_acc[...] = jnp.zeros_like(dv_acc)

    q = q_ref[...]
    do = do_ref[...]
    c2 = c2_ref[0]
    delta = jnp.sum((o_ref[...].astype(F32) * do.astype(F32)).T, axis=0, keepdims=True)
    lse = lse_ref[...]
    at = lax.broadcasted_iota(jnp.int32, (1, rows), 1) + (origin + block * rows)
    q_pos = at.astype(F32)
    lo_q, hi_q = lo_ref[...], hi_ref[...]
    first = low_ref[block]
    steps = (high_ref[block] - first + (BK - 1)) // BK

    def step(t, dq):
        start = pl.multiple_of(first + t * BK, 128)
        here = pl.ds(start, BK)
        k = kv_ref[here, :DH]
        v = kv_ref[here, DH:]
        k_pos = (lax.broadcasted_iota(jnp.int32, (BK, 1), 0) + start).astype(F32)
        scores = dot_nt(k, q) * c1 - jnp.abs(k_pos - q_pos) * c2 - lse
        scores = jnp.where((k_pos >= lo_q) & (k_pos < hi_q), scores, MASKED)
        probs = jnp.exp2(scores)
        grads = (probs * (dot_nt(v, do) - delta)).astype(BF)
        dv_acc[here, :] += dot_nn(probs.astype(BF), do)
        dk_acc[here, :] += dot_nn(grads, q)
        return dq + dot_tn(k, grads)

    dq = lax.fori_loop(0, steps, step, jnp.zeros((DH, rows), F32))
    dq_ref[...] = (dq * scale).T.astype(BF)

    @pl.when(block == pl.num_programs(0) - 1)
    def _():
        prev_ref[:, :DH] = (dk_acc[:origin, :] * scale).astype(BF)
        prev_ref[:, DH:] = dv_acc[:origin, :].astype(BF)
        own_ref[:, :DH] = dk_acc[origin : origin + frames, :] * scale
        own_ref[:, DH:] = dv_acc[origin : origin + frames, :]
        next_ref[:, :DH] = (dk_acc[origin + frames : 2 * origin + frames, :] * scale).astype(BF)
        next_ref[:, DH:] = dv_acc[origin + frames : 2 * origin + frames, :].astype(BF)


def attn_bwd(q, o, do, lse, kv, low, high, c2, lo_q, hi_q, origin, order=()):
    frames = q.shape[0]
    blocks = frames // BQ
    pairs = frames * 1024 * DH
    window = sum(v.shape[0] for v in kv[:3]) + BK
    parts = [pl.BlockSpec(v.shape, lambda i, *_: (0, 0)) for v in kv]
    tile = pl.BlockSpec((BQ, DH), lambda i, *_: (i, 0))
    row = pl.BlockSpec((1, BQ), lambda i, *_: (0, i))
    grid_spec = pltpu.PrefetchScalarGridSpec(
        num_scalar_prefetch=3,
        grid=(blocks,),
        in_specs=[
            tile,
            tile,
            tile,
            row,
            row,
            row,
            *parts,
        ]
        + [pl.BlockSpec(memory_space=pl.ANY)] * len(order),
        out_specs=[
            tile,
            pl.BlockSpec((origin, 2 * DH), lambda i, *_: (0, 0)),
            pl.BlockSpec((frames, 2 * DH), lambda i, *_: (0, 0)),
            pl.BlockSpec((origin, 2 * DH), lambda i, *_: (0, 0)),
        ],
        scratch_shapes=[
            pltpu.VMEM((window, DH), F32),
            pltpu.VMEM((window, DH), F32),
            pltpu.VMEM((window, 2 * DH), BF),
        ],
    )

    def kernel(*refs):
        attn_bwd_kernel(origin, len(order), *refs)

    return pl.pallas_call(
        kernel,
        grid_spec=grid_spec,
        out_shape=[
            jax.ShapeDtypeStruct((frames, DH), BF),
            jax.ShapeDtypeStruct((origin, 2 * DH), BF),
            jax.ShapeDtypeStruct((frames, 2 * DH), F32),
            jax.ShapeDtypeStruct((origin, 2 * DH), BF),
        ],
        compiler_params=pltpu.CompilerParams(vmem_limit_bytes=VMEM_BYTES),
        cost_estimate=pl.CostEstimate(
            flops=80 * pairs, bytes_accessed=8 * window * DH, transcendentals=frames * 1024
        ),
        name="attention_backward",
    )(low, high, c2, q, o, do, lse, lo_q, hi_q, *kv, *order)


def pass_on_kernel(extra, *refs):
    count = (len(refs) - extra) // 2
    for a, b in zip(refs[:count], refs[count + extra :]):
        b[...] = a[...]


def pass_on(arrays, order):
    return pl.pallas_call(
        functools.partial(pass_on_kernel, len(order)),
        in_specs=[pl.BlockSpec(v.shape, lambda n=v.ndim: (0,) * n) for v in arrays]
        + [pl.BlockSpec(memory_space=pl.ANY)] * len(order),
        out_specs=[pl.BlockSpec(v.shape, lambda n=v.ndim: (0,) * n) for v in arrays],
        out_shape=[jax.ShapeDtypeStruct(v.shape, v.dtype) for v in arrays],
        compiler_params=pltpu.CompilerParams(vmem_limit_bytes=VMEM_BYTES // 3),
        cost_estimate=pl.CostEstimate(flops=1, bytes_accessed=1024, transcendentals=0),
        name="pass_on",
    )(*arrays, *order)


def join_kernel(extra, own_ref, before_ref, after_ref, *refs):
    out_ref = refs[extra]
    span = before_ref.shape[0]
    rows = own_ref.shape[0]
    out_ref[:span, :] = (own_ref[:span, :] + before_ref[...].astype(F32)).astype(BF)
    if rows > 2 * span:
        out_ref[span : rows - span, :] = own_ref[span : rows - span, :].astype(BF)
    out_ref[rows - span :, :] = (own_ref[rows - span :, :] + after_ref[...].astype(F32)).astype(BF)


def join_edges(own, before, after, order=()):
    return pl.pallas_call(
        functools.partial(join_kernel, len(order)),
        in_specs=[pl.BlockSpec(v.shape, lambda: (0, 0)) for v in (own, before, after)]
        + [pl.BlockSpec(memory_space=pl.ANY)] * len(order),
        out_specs=pl.BlockSpec(own.shape, lambda: (0, 0)),
        out_shape=jax.ShapeDtypeStruct(own.shape, BF),
        compiler_params=pltpu.CompilerParams(vmem_limit_bytes=VMEM_BYTES // 2),
        cost_estimate=pl.CostEstimate(
            flops=own.size, bytes_accessed=8 * own.size, transcendentals=0
        ),
        name="join_edges",
    )(own, before, after, *order)


def stack_kernel(extra, places, arrays, *refs):
    out_ref = refs[arrays + extra]
    rows_ref = refs[arrays + extra + 1]
    for at, (source, row) in enumerate(places):
        rows_ref[at : at + 1, :] = refs[source][row : row + 1, :]
    share = out_ref.shape[2]
    rows = rows_ref[...]
    for i in range(out_ref.shape[0]):
        out_ref[i] = rows[:, i * share : (i + 1) * share]


def stack_rows(arrays, places, devices, order=()):
    width = arrays[0].shape[1]
    share = width // devices
    if share % 32:
        rows = jnp.stack([arrays[source][row] for source, row in places])
        return rows.reshape(len(places), devices, share).transpose(1, 0, 2)
    return pl.pallas_call(
        functools.partial(stack_kernel, len(order), places, len(arrays)),
        in_specs=[pl.BlockSpec(v.shape, lambda: (0, 0)) for v in arrays]
        + [pl.BlockSpec(memory_space=pl.ANY)] * len(order),
        out_specs=pl.BlockSpec((devices, len(places), share), lambda: (0, 0, 0)),
        out_shape=jax.ShapeDtypeStruct((devices, len(places), share), F32),
        scratch_shapes=[pltpu.VMEM((len(places), width), F32)],
        name="stack_rows",
    )(*arrays, *order)


def halve_kernel(extra, sel_ref, kept_a, kept_b, got_a, got_b, *refs):
    send_ref, keep_ref = refs[extra:]
    send_ref[...] = (kept_a[0].astype(F32) + got_a[0].astype(F32)).astype(BF)
    keep_ref[...] = (kept_b[0].astype(F32) + got_b[0].astype(F32)).astype(BF)


def halve(kept, got, mine, order=()):
    count, _, rows, columns = kept.shape
    step = rows
    while step % 32 == 0 and step * columns > 512 * 1024:
        step //= 2
    block = (1, 1, step, columns)
    other = pl.BlockSpec(block, lambda i, j, m: (i, 1 - m[0], j, 0))
    own = pl.BlockSpec(block, lambda i, j, m: (i, m[0], j, 0))
    out = pl.BlockSpec((1, step, columns), lambda i, j, m: (i, j, 0))
    return pl.pallas_call(
        functools.partial(halve_kernel, len(order)),
        grid_spec=pltpu.PrefetchScalarGridSpec(
            num_scalar_prefetch=1,
            grid=(count, rows // step),
            in_specs=[other, own, other, own]
            + [pl.BlockSpec(memory_space=pl.ANY)] * len(order),
            out_specs=[out, out],
        ),
        out_shape=[jax.ShapeDtypeStruct((count, rows, columns), BF)] * 2,
        compiler_params=pltpu.CompilerParams(vmem_limit_bytes=VMEM_BYTES // 3),
        cost_estimate=pl.CostEstimate(flops=1024, bytes_accessed=1024, transcendentals=0),
        name="halve",
    )(mine.astype(jnp.int32)[None], kept, kept, got, got, *order)


def finish_kernel(extra, turned, kept_ref, got_ref, *refs):
    total = kept_ref[...].astype(F32) + got_ref[...].astype(F32)
    refs[extra][...] = total.T if turned else total


def finish(kept, got, turned=False, order=()):
    rows, columns = kept.shape
    fixed = pl.BlockSpec((rows, columns), lambda: (0, 0))
    shape = (columns, rows) if turned else (rows, columns)
    if turned and rows % 128:
        return finish(kept, got, False, order).T
    return pl.pallas_call(
        functools.partial(finish_kernel, len(order), turned),
        in_specs=[fixed, fixed] + [pl.BlockSpec(memory_space=pl.ANY)] * len(order),
        out_specs=pl.BlockSpec(shape, lambda: (0, 0)),
        out_shape=jax.ShapeDtypeStruct(shape, F32),
        compiler_params=pltpu.CompilerParams(vmem_limit_bytes=VMEM_BYTES // 3),
        name="finish",
    )(kept, got, *order)


def halve_both_kernel(extra, sel_ref, *refs):
    send_ref, keep_ref = refs[8 + extra :]
    for i in (0, 1):
        kept_a, kept_b, got_a, got_b = refs[4 * i : 4 * i + 4]
        rows = kept_a.shape[2]
        here = slice(i * rows, (i + 1) * rows)
        send_ref[0, here, :] = (kept_a[0, 0].astype(F32) + got_a[0, 0].astype(F32)).astype(BF)
        keep_ref[0, here, :] = (kept_b[0, 0].astype(F32) + got_b[0, 0].astype(F32)).astype(BF)


def halve_both(first, second, shape, mine, order=()):
    count, _, rows, columns = shape
    block = (1, 1, rows, columns)
    other = pl.BlockSpec(block, lambda i, m: (i, 1 - m[0], 0, 0))
    own = pl.BlockSpec(block, lambda i, m: (i, m[0], 0, 0))
    out = pl.BlockSpec((1, 2 * rows, columns), lambda i, m: (i, 0, 0))
    arrays = []
    for part in (first, second):
        kept, got = part.kept.reshape(shape), part.got.reshape(shape)
        arrays += [kept, kept, got, got]
    return pl.pallas_call(
        functools.partial(halve_both_kernel, len(order)),
        grid_spec=pltpu.PrefetchScalarGridSpec(
            num_scalar_prefetch=1,
            grid=(count,),
            in_specs=[other, own, other, own] * 2
            + [pl.BlockSpec(memory_space=pl.ANY)] * len(order),
            out_specs=[out, out],
        ),
        out_shape=[jax.ShapeDtypeStruct((count, 2 * rows, columns), BF)] * 2,
        compiler_params=pltpu.CompilerParams(vmem_limit_bytes=VMEM_BYTES // 3),
        cost_estimate=pl.CostEstimate(flops=1024, bytes_accessed=1024, transcendentals=0),
        name="halve_both",
    )(mine.astype(jnp.int32)[None], *arrays, *order)


def finish_both_kernel(extra, kept_ref, got_ref, *refs):
    first_ref, second_ref = refs[extra:]
    rows = first_ref.shape[0]
    total = kept_ref[...].astype(F32) + got_ref[...].astype(F32)
    first_ref[...] = total[:rows]
    second_ref[...] = total[rows:].T


def finish_both(total, rows, columns, order=()):
    kept, got = total.kept.reshape(2 * rows, columns), total.got.reshape(2 * rows, columns)
    if rows % 128:
        both = kept.astype(F32) + got.astype(F32)
        return both[:rows], both[rows:].T
    fixed = lambda *shape: pl.BlockSpec(shape, lambda: (0, 0))
    return pl.pallas_call(
        functools.partial(finish_both_kernel, len(order)),
        in_specs=[fixed(2 * rows, columns)] * 2
        + [pl.BlockSpec(memory_space=pl.ANY)] * len(order),
        out_specs=[fixed(rows, columns), fixed(columns, rows)],
        out_shape=[
            jax.ShapeDtypeStruct((rows, columns), F32),
            jax.ShapeDtypeStruct((columns, rows), F32),
        ],
        compiler_params=pltpu.CompilerParams(vmem_limit_bytes=VMEM_BYTES // 3),
        cost_estimate=pl.CostEstimate(flops=1024, bytes_accessed=1024, transcendentals=0),
        name="finish_both",
    )(kept, got, *order)


def total_kernel(extra, parts_ref, *refs):
    total = jnp.sum(parts_ref[...], axis=0)
    at = 0
    for ref in refs[extra:]:
        ref[...] = total[at : at + ref.shape[0]]
        at += ref.shape[0]


def total_of(parts, counts, order=()):
    columns = parts.shape[2]
    return pl.pallas_call(
        functools.partial(total_kernel, len(order)),
        in_specs=[pl.BlockSpec(parts.shape, lambda: (0, 0, 0))]
        + [pl.BlockSpec(memory_space=pl.ANY)] * len(order),
        out_specs=[pl.BlockSpec((n, columns), lambda: (0, 0)) for n in counts],
        out_shape=[jax.ShapeDtypeStruct((n, columns), F32) for n in counts],
        name="total_of",
    )(parts, *order)


class Sum:
    def __init__(self, kept, send, axis, bit):
        self.kept = kept
        self.send = send
        self.got = xor_send(send, axis, bit)

    def step(self, shape, axis, bit=1, order=()):
        mine = (lax.axis_index(axis) // bit) % 2
        send, kept = halve(self.kept.reshape(shape), self.got.reshape(shape), mine, order)
        return Sum(kept, send, axis, bit)

    def finish(self, shape, turned=False, order=()):
        return finish(self.kept.reshape(shape), self.got.reshape(shape), turned, order)


def slab_grad_kernel(split, extra, pair, sel_ref, la_ref, lb_ref, ra_ref, rb_ref, *refs):
    if pair:
        rb_ref = [jnp.where(pl.program_id(0) == 0, rb_ref[0], refs[0][0])]
        refs = refs[1:]
    out_ref = refs[extra]
    if split is None:
        out = dot_tn(la_ref[0], ra_ref[0]) + dot_tn(lb_ref[0], rb_ref[0])
    else:
        zs, rows = split
        take = [pl.ds(pl.multiple_of((z * 2 + sel_ref[0]) * rows, rows), rows) for z in range(zs)]
        left = [jnp.concatenate([ref[0, :, t] for t in take], axis=1) for ref in (la_ref, lb_ref)]
        out = dot_tn(left[0], ra_ref[0]) + dot_tn(left[1], rb_ref[0])
    out_ref[0] = out.astype(BF)


def slab_grad(left, right, x, y, order=(), lasting=0):
    left_a, left_b, left_at = left
    right_a, right_b, right_at = right
    pair = isinstance(right_b, tuple)
    _, frames, width = left_a.shape
    hidden = right_a.shape[2]
    zs = lax.axis_size("z")
    rows = width // (2 * zs)
    half = width // 2
    if x is None:
        split = None
        sel = y
        left_block = pl.BlockSpec((1, frames, half), lambda i, s: (left_at, 0, i))
        right = [
            pl.BlockSpec((1, frames, hidden), lambda i, s: (s[0], 0, 0)),
            pl.BlockSpec((1, frames, hidden), lambda i, s: (s[0] + right_at, 0, 0)),
        ]
    else:
        sel = x
        right = [
            pl.BlockSpec((1, frames, hidden), lambda i, s: (i, 0, 0)),
            pl.BlockSpec((1, frames, hidden), lambda i, s: (i + right_at, 0, 0)),
        ]
        if pair:
            right[1:] = [pl.BlockSpec((1, frames, hidden), lambda i, s: (0, 0, 0))] * 2
        if rows % 128 == 0:
            split = (zs, rows)
            left_block = pl.BlockSpec((1, frames, width), lambda i, s: (left_at, 0, 0))
        else:
            split = None
            left_block = pl.BlockSpec((1, frames, half), lambda i, s: (0, 0, 0))
            left_a, left_b = (
                pick(l[left_at].reshape(frames, zs, 2, rows), x, 2).reshape(1, frames, half)
                for l in (left_a, left_b)
            )
    return pl.pallas_call(
        functools.partial(slab_grad_kernel, split, len(order), pair),
        grid_spec=pltpu.PrefetchScalarGridSpec(
            num_scalar_prefetch=1,
            grid=(2,),
            in_specs=[left_block, left_block]
            + right
            + [pl.BlockSpec(memory_space=pl.ANY)] * len(order),
            out_specs=pl.BlockSpec((1, half, hidden), lambda i, s: (i, 0, 0)),
        ),
        out_shape=jax.ShapeDtypeStruct((2, half, hidden), BF),
        compiler_params=pltpu.CompilerParams(vmem_limit_bytes=VMEM_BYTES),
        cost_estimate=takes(lasting),
        name="slab_grad",
    )(sel.astype(jnp.int32)[None], left_a, left_b, right_a, *(right_b if pair else (right_b,)), *order)


def slab_sum(left, right, first, order=(), kept_order=()):
    place = lax.axis_index(first)
    picks = lambda i: (i, None) if first == "x" else (None, i)
    away = slab_grad(left, right, *picks(1 - place), order)
    return Sum(slab_grad(left, right, *picks(place), (away,) + tuple(kept_order)), away, first, 1)


def slab_second(total, first, order=()):
    zs = lax.axis_size("z")
    _, half, hidden = total.kept.shape
    if first == "x":
        return total.step((1, 2, half, hidden), "y", 1, order)
    return total.step((zs, 2, half // zs, hidden), "x", 1, order)


def z_steps(total, rows, columns, bits=None, order=()):
    zs = lax.axis_size("z")
    for bit in z_bits() if bits is None else bits:
        total = total.step((zs // (2 * bit), 2, rows, columns), "z", bit, order)
    return total


def z_both(first, second, rows, columns, order=()):
    zs = lax.axis_size("z")
    mine = lax.axis_index("z") % 2
    send, kept = halve_both(first, second, (zs // 2, 2, rows, columns), mine, order)
    return Sum(kept, send, "z", 1)


def z_bits():
    bits = []
    while 1 << len(bits) < lax.axis_size("z"):
        bits.append(1 << len(bits))
    return bits


def right_of(ref):
    if len(ref.shape) == 2:
        return ref[...]
    return jnp.concatenate([heads_of(ref, at, at + DH) for at in range(0, ref.shape[2], DH)], axis=1)


def row_grad_kernel(pairs, rows, core_ref, *refs):
    send_ref, keep_ref = refs[-2:]
    at = 0
    for i in range(pairs):
        whole = dot_tn(refs[2 * i][...], right_of(refs[2 * i + 1])).astype(BF)
        columns = whole.shape[1]
        parts = [whole[k * rows : (k + 1) * rows] for k in range(whole.shape[0] // rows)]
        even = jnp.concatenate(parts[0::2], axis=0)
        odd = jnp.concatenate(parts[1::2], axis=0)
        first = core_ref[0] == 0
        keep_ref[:, at : at + columns] = jnp.where(first, even, odd)
        send_ref[:, at : at + columns] = jnp.where(first, odd, even)
        at += columns


def row_grad(core, pairs, order=()):
    frames, width = pairs[0][0].shape
    zs = lax.axis_size("z")
    rows = width // (8 * zs)
    columns = sum(right.size // frames for _, right in pairs)
    if rows % 16:
        whole = jnp.concatenate(
            [dot_tn(left, right_of(right)).astype(BF) for left, right in pairs], axis=1
        )
        whole = whole.reshape(4 * zs, 2, rows, columns)
        flat = lambda v: v.reshape(width // 2, columns)
        return flat(pick(whole, 1 - core[0], 1)), flat(pick(whole, core[0], 1))
    tile = 256
    specs, args = [], []
    for left, right in pairs:
        specs += [
            pl.BlockSpec((frames, tile), lambda i, c: (0, i)),
            pl.BlockSpec(right.shape, lambda i, c, n=right.ndim: (0,) * n),
        ]
        args += [left, right]
    specs += [pl.BlockSpec(memory_space=pl.ANY)] * len(order)
    out = pl.BlockSpec((tile // 2, columns), lambda i, c: (i, 0))
    return pl.pallas_call(
        functools.partial(row_grad_kernel, len(pairs), rows),
        grid_spec=pltpu.PrefetchScalarGridSpec(
            num_scalar_prefetch=1, grid=(width // tile,), in_specs=specs, out_specs=[out, out]
        ),
        out_shape=[jax.ShapeDtypeStruct((width // 2, columns), BF)] * 2,
        compiler_params=pltpu.CompilerParams(vmem_limit_bytes=VMEM_BYTES),
        cost_estimate=takes(10),
        name="row_grad",
    )(core, *args, *order)


def body(
    block_in,
    out_grad,
    utt_ends,
    valid_ends,
    ffn1_in,
    ffn1_out,
    att_qkv,
    att_out,
    content_bias,
    conv_in,
    conv_out,
    ffn2_in,
    ffn2_out,
    conv_depth,
    norm_gain,
    norm_bias,
):
    zs = lax.axis_size("z")
    devices = 8 * zs
    frames, width = block_in.shape
    heads = width // DH
    z, x, y, c = (lax.axis_index(axis) for axis in DEV)
    place = ((z * 2 + x) * 2 + y) * 2 + c
    head = (x * 2 + y) * 2 + c

    small = jnp.concatenate([norm_gain, norm_bias, conv_depth, content_bias[None]], axis=0)
    small = jnp.broadcast_to(small[None], (devices,) + small.shape)
    small = lax.all_to_all(small, DEV, split_axis=0, concat_axis=0, tiled=True)
    small = small.transpose(1, 0, 2).reshape(small.shape[1], width).astype(F32)
    gains, shifts, taps, q_bias = small[:6], small[6:12], small[12 : 12 + KSIZE], small[12 + KSIZE]

    rows, few = ffn1_in.shape[0], att_qkv.shape[0]
    blocks = lambda w: [w[:, i : i + width] for i in range(0, w.shape[1], width)]

    def gather(*parts):
        mine = jnp.concatenate(parts, axis=0)
        return lax.all_gather(mine, DEV, axis=0, tiled=True).reshape(devices, -1, width)

    w_first = gather(pack_ffn(ffn1_in, ffn1_out), *blocks(att_qkv))
    w_mid = gather(att_out, *blocks(conv_in), conv_out)
    w_second = gather(pack_ffn(ffn2_in, ffn2_out, order=(small,)))
    w_proj = Rows(w_first, 2 * rows, few)
    w_conv = Rows(w_mid, 0, few)
    w_cout = Rows(w_mid, 3 * few, few)
    core = c.astype(jnp.int32)[None]

    all_frames = frames * devices
    first_frame = place * frames
    span = 4 * frames
    group = 8 * frames
    origin = span
    group_first = z * group
    starts = jnp.concatenate([jnp.zeros((1,), jnp.int32), utt_ends[:-1]])
    valid_count = jnp.sum((valid_ends - starts).astype(F32))

    def segments(positions):
        seg = jnp.sum((utt_ends[None, :] <= positions[:, None]).astype(jnp.int32), axis=1)
        valid_seg = jnp.sum((valid_ends[None, :] <= positions[:, None]).astype(jnp.int32), axis=1)
        valid = seg == valid_seg
        return jnp.where(positions < 0, -1, jnp.where(positions >= all_frames, -2, seg)), valid

    ext_seg, ext_valid = segments(
        first_frame - REACH + jnp.arange(frames + 2 * REACH, dtype=jnp.int32)
    )
    own_seg = ext_seg[REACH : REACH + frames]
    ext_valid = ext_valid.astype(F32)
    edge_valid = jnp.concatenate([ext_valid[:REACH], ext_valid[-REACH:]])
    edge_valid = jnp.concatenate([edge_valid, jnp.zeros((frames - 2 * REACH,), F32)])
    columns = jnp.stack(
        [(ext_seg[m : m + frames] == own_seg).astype(F32) for m in range(KSIZE)]
        + [ext_valid[REACH : REACH + frames], edge_valid, jnp.zeros((frames,), F32)],
        axis=1,
    )
    group_pos = group_first + jnp.arange(group, dtype=jnp.int32)
    ended = utt_ends[None, :] <= group_pos[:, None]
    group_seg = jnp.sum(ended.astype(jnp.int32), axis=1)
    group_lo = jnp.max(jnp.where(ended, utt_ends[None, :], 0), axis=1)
    slots = jnp.arange(utt_ends.shape[0], dtype=jnp.int32)
    group_hi = jnp.sum(
        jnp.where(group_seg[:, None] == slots[None, :], valid_ends[None, :], 0), axis=1
    )
    window_first = group_first - origin
    lo_q = group_lo - window_first
    hi_q = group_hi - window_first
    low = (lo_q[::BQ] // 128) * 128
    high = hi_q[BQ - 1 :: BQ]
    lo_q = lo_q.astype(F32)[None, :]
    hi_q = hi_q.astype(F32)[None, :]
    c2 = (32.0 * jnp.exp2(-head.astype(F32)) * (LOG2E / span))[None]

    def vectors(*rows):
        rows = jnp.stack(rows)
        return jnp.concatenate([rows, jnp.zeros((-len(rows) % 8, width), F32)], axis=0)

    count_row = jnp.broadcast_to(valid_count, (width,))

    x1, n2, pack1, s1, d1, q_heads, k_heads, v_heads = first_call(
        core,
        block_in,
        w_first,
        rows,
        w_proj,
        vectors(gains[0], shifts[0], gains[1], shifts[1], q_bias),
    )
    pack1_sib = xor_send(pack1, "c", 1)

    def to_heads(cells):
        got = lax.all_to_all(cells, LAYER, split_axis=0, concat_axis=0, tiled=True)
        return got.reshape(group, cells.shape[2])

    def to_frames(cells):
        cells = cells.reshape(heads, frames, cells.shape[1])
        return lax.all_to_all(cells, LAYER, split_axis=0, concat_axis=0, tiled=True)

    up = [(i, i + 1) for i in range(zs - 1)]
    down = [(i + 1, i) for i in range(zs - 1)]

    def with_edges(cells):
        return lax.ppermute(cells[-span:], "z", up), cells, lax.ppermute(cells[:span], "z", down)

    kv = with_edges(to_heads(k_heads)) + with_edges(to_heads(v_heads))
    q_own = to_heads(q_heads)
    o_own, lse = attn_fwd(q_own, kv, low, high, c2, lo_q, hi_q, origin)
    mixed, x2, n3, lin, sig, gated = gate_call(
        to_frames(o_own), x1, w_conv, vectors(gains[2], shifts[2]), columns, (pack1_sib,)
    )
    g_edges = neighbour_rows(gated)
    tap_rows = [taps[m] for m in range(KSIZE)]
    conv, moments = conv_call(gated, *g_edges, vectors(*tap_rows), columns, devices)
    spread = lambda cells: lax.all_to_all(cells, DEV, split_axis=0, concat_axis=0, tiled=True)
    moments = spread(moments)

    final_out, swished, dx3, ew, dz, sums_c, totals, pack2, s2, da2 = second_call(
        core,
        x2,
        conv,
        moments,
        w_cout,
        w_second,
        rows,
        vectors(gains[3], shifts[3], gains[4], shifts[4], gains[5], shifts[5], count_row),
        out_grad,
    )
    totals = spread(totals)
    edges = neighbour_rows(jnp.concatenate([dz[-REACH:], conv[-REACH:]]), jnp.concatenate([dz[:REACH], conv[:REACH]]))
    pack2_sib = xor_send(pack2, "c", 1)
    hidden = pack2.shape[2]
    f2i = slab_sum((pack2, pack2_sib, 0), (da2, pack2_sib, 4), "x")
    f2o = slab_sum((pack2, pack2_sib, 3), (s2, pack2_sib, 1), "y")

    point_grad, dx2, ey, mixed_grad, sums_b = back_call(
        dz,
        conv,
        edges,
        gated,
        g_edges,
        moments,
        totals,
        lin,
        sig,
        x2,
        dx3,
        w_conv,
        vectors(*tap_rows, gains[3], gains[2], gains[2], count_row),
        columns,
        order=(f2i.send, f2o.send),
    )
    do_own = to_heads(mixed_grad)
    send, kept = row_grad(core, [(mixed, ey), (n3, point_grad), (swished, ew)])
    mid = Sum(kept, send, "c", 1)
    dq, dkv_prev, dkv, dkv_next = attn_bwd(
        q_own,
        o_own,
        do_own,
        lse,
        kv,
        low,
        high,
        c2,
        lo_q,
        hi_q,
        origin,
        order=(f2i.kept, f2o.kept, kept),
    )
    dq = to_frames(dq)
    f2i = slab_second(f2i, "x")
    f2o = slab_second(f2o, "y", order=(f2i.send,))
    dkv = join_edges(
        dkv,
        lax.ppermute(dkv_next, "z", up),
        lax.ppermute(dkv_prev, "z", down),
        order=(f2i.send, f2o.send),
    )
    dkv = to_frames(dkv)

    low_z, high_z = z_bits()[:1], z_bits()[1:]
    dx1, ef1, sums_p = proj_back_call(dq, dkv, dx2, x1, w_proj, vectors(gains[0], gains[1]), ())
    ef1_sib = xor_send(ef1, "c", 1)
    send, kept = row_grad(core, [(n2, dq), (n2, dkv)], order=(ef1,))
    qkv = Sum(kept, send, "c", 1)
    f1o_left, f1o_right = (ef1, ef1_sib, 0), (s1, pack1_sib, 1)
    f1o_away = slab_grad(f1o_left, f1o_right, None, 1 - y, (qkv.send,))
    mid = mid.step((zs, 2, 2 * few, 4 * width), "x", order=(f1o_away,))
    f2 = z_both(f2i, f2o, rows, hidden, order=(mid.send,))
    grad_input, sums_a, da_first, da_second, da1 = last_call(
        core,
        dx1,
        ef1,
        block_in,
        w_first,
        rows,
        d1,
        vectors(gains[0]),
        order=(f2.send,),
    )
    da_sib = (xor_send(da_first, "c", 1), xor_send(da_second, "c", 1))
    f2 = z_steps(f2, 2 * rows, hidden, high_z, order=(da1,))
    f1o = Sum(slab_grad(f1o_left, f1o_right, None, y, (f2.send,), 10), f1o_away, "y", 1)
    f1i = slab_sum((pack1, pack1_sib, 0), (da1, da_sib, 0), "x", order=(f1o.kept,))
    grad_f2i, grad_f2o = finish_both(f2, rows, hidden, order=(f1i.kept,))
    qkv = z_steps(qkv, 4 * few, 3 * width, low_z, order=(grad_f2i,))
    f1o = slab_second(f1o, "y", order=(qkv.send,))
    mid = mid.step((zs, 2, few, 4 * width), "y", order=(f1o.send,))
    qkv = qkv.step((zs, 2, few, 3 * width), "y", order=(mid.send,))
    mid = z_steps(mid, few, 4 * width, low_z, order=(qkv.send,))
    f1i = slab_second(f1i, "x", order=(mid.send,))
    f1o = z_steps(f1o, rows, hidden, low_z, order=(f1i.send,))
    mid = z_steps(mid, few, 4 * width, high_z, order=(f1o.send,))
    f1o = z_steps(f1o, rows, hidden, high_z, order=(mid.send,))
    mid = mid.finish((few, 4 * width), order=(f1o.send,))
    out_att, out_cin, out_cout = mid[:, :width], mid[:, width : 3 * width], mid[:, 3 * width :]
    qkv = z_steps(qkv, 2 * few, 3 * width, high_z, order=(mid,))
    f1i = z_steps(f1i, rows, hidden, low_z, order=(qkv.send,))
    f1i = z_steps(f1i, rows, hidden, high_z, order=(f1i.send,))
    a, b, c, p = 0, 1, 2, 3
    places = [(a, 0), (p, 0), (b, 0), (c, 4), (c, 2), (c, 0)]
    places += [(a, 1), (p, 1), (b, 1), (c, 5), (c, 3), (c, 1)]
    places += [(b, 2 + m) for m in range(KSIZE)] + [(p, 2)]
    sums = stack_rows([sums_a, sums_b, sums_c, sums_p], places, devices, order=(f1i.send,))
    qkv = qkv.step((1, 2, few, 3 * width), "x", order=(sums,))
    grad_f1o = f1o.finish((rows, hidden), True, order=(qkv.send,))
    grad_f1i = f1i.finish((rows, hidden), order=(grad_f1o,))
    out_qkv = qkv.finish((few, 3 * width), order=(grad_f1i,))
    sums = lax.all_to_all(sums, DEV, split_axis=0, concat_axis=0, tiled=True)
    gain_sums, bias_sums, tap_sums, query_sums = total_of(
        sums, (6, 6, KSIZE, 1), order=(out_qkv,)
    )

    return (
        final_out,
        grad_input,
        grad_f1i,
        grad_f1o,
        out_qkv,
        out_att,
        query_sums[0],
        out_cin,
        out_cout,
        grad_f2i,
        grad_f2o,
        tap_sums,
        gain_sums,
        bias_sums,
    )


def solution(mesh):
    seq, heads = mesh.shape["seq"], mesh.shape["head"]
    grid = Mesh(mesh.devices.reshape(seq // 2, 2, heads // 2, 2), DEV)
    both = P(DEV, None)
    inward = P(("z", "x"), ("y", "c"))
    outward = P(("y", "c"), ("z", "x"))
    columns = P(None, DEV)
    return jax.shard_map(
        body,
        mesh=grid,
        in_specs=(
            both,
            both,
            P(),
            P(),
            inward,
            outward,
            both,
            both,
            P(DEV),
            both,
            both,
            inward,
            outward,
            columns,
            columns,
            columns,
        ),
        out_specs=(
            both,
            both,
            inward,
            outward,
            both,
            both,
            P(DEV),
            both,
            both,
            inward,
            outward,
            columns,
            columns,
            columns,
        ),
        check_vma=False,
    )
```

```python
import functools
import math

import jax
import jax.numpy as jnp
from jax import lax
from jax.experimental import pallas as pl
from jax.experimental.pallas import tpu as pltpu
from jax.sharding import Mesh
from jax.sharding import PartitionSpec as P

DH = 128
KSIZE = 5
REACH = (KSIZE - 1) // 2
EPSILON = 1e-05
MASKED = -1e30
LOG2E = math.log2(math.e)
DEV = ("z", "x", "y", "c")
LAYER = ("x", "y", "c")
BQ = 512
BK = 512
BF = jnp.bfloat16
F32 = jnp.float32
VMEM_BYTES = 56 * 1024 * 1024


def takes(microseconds):
    return pl.CostEstimate(
        flops=1024, bytes_accessed=1024 + int(microseconds * 3.7e6), transcendentals=0
    )


def pick(cells, index, dim):
    return lax.dynamic_index_in_dim(cells, index, dim, keepdims=False)


def xor_send(cells, axis, bit):
    count = lax.axis_size(axis)
    return lax.ppermute(cells, axis, [(i, i ^ bit) for i in range(count)])


def neighbour_rows(tail, head=None):
    if head is None:
        tail, head = tail[-REACH:], tail[:REACH]
    count = 1
    for axis in DEV:
        count *= lax.axis_size(axis)
    before = lax.ppermute(tail, DEV, [(i, i + 1) for i in range(count - 1)])
    after = lax.ppermute(head, DEV, [(i + 1, i) for i in range(count - 1)])
    return before, after


def dot_nn(a, b):
    return lax.dot_general(a, b, (((1,), (0,)), ((), ())), preferred_element_type=F32)


def dot_nt(a, b):
    return lax.dot_general(a, b, (((1,), (1,)), ((), ())), preferred_element_type=F32)


def dot_tn(a, b):
    return lax.dot_general(a, b, (((0,), (0,)), ((), ())), preferred_element_type=F32)


def norm_stats(values):
    centred = values - jnp.mean(values, axis=-1, keepdims=True)
    inv_std = lax.rsqrt(jnp.mean(centred * centred, axis=-1, keepdims=True) + EPSILON)
    return centred * inv_std, inv_std


def norm_back(upstream, normed, inv_std, gain):
    scaled = upstream * gain
    inner = (
        scaled
        - jnp.mean(scaled, axis=-1, keepdims=True)
        - normed * jnp.mean(scaled * normed, axis=-1, keepdims=True)
    )
    return inv_std * inner


def pack_kernel(extra, in_ref, out_ref, *refs):
    rows = in_ref.shape[0]
    refs[extra][:rows] = in_ref[...]
    refs[extra][rows:] = out_ref[...].T


def pack_ffn(w_in, w_out, order=()):
    rows, width = w_in.shape
    whole = lambda v: pl.BlockSpec(v.shape, lambda: (0, 0))
    if rows % 128:
        return jnp.concatenate([w_in, w_out.T], axis=0)
    return pl.pallas_call(
        functools.partial(pack_kernel, len(order)),
        in_specs=[whole(w_in), whole(w_out)] + [pl.BlockSpec(memory_space=pl.ANY)] * len(order),
        out_specs=pl.BlockSpec((2 * rows, width), lambda: (0, 0)),
        out_shape=jax.ShapeDtypeStruct((2 * rows, width), BF),
        name="pack_ffn",
    )(w_in, w_out, *order)


class Rows:
    def __init__(self, gathered, first, count):
        self.stepped = count % 16 == 0 and first % count == 0
        devices, _, width = gathered.shape
        self.count = count
        if self.stepped:
            self.at = first // count
            self.array = gathered
            self.block = (devices, count, width)
        else:
            self.first = first
            self.gathered = gathered
            self.width = width

    def blocks(self, pick_block, total):
        if self.stepped:
            at = self.at
            return self.array, pl.BlockSpec(self.block, lambda j, *_: (0, at + pick_block(j), 0))
        cut = [
            self.gathered[:, self.first + i * self.count : self.first + (i + 1) * self.count]
            for i in range(total)
        ]
        cut = jnp.stack([v.reshape(-1, self.width) for v in cut])
        return cut, pl.BlockSpec((1,) + cut.shape[1:], lambda j, *_: (pick_block(j), 0, 0))


def square(ref):
    return ref[...].reshape(-1, ref.shape[-1])


def slab_of(step, core):
    return (step % 2) * 2 + jnp.where(step < 2, 1 - core, core)


def slab_specs(gathered, rows, step_of):
    devices, total, width = gathered.shape
    array = gathered.reshape(devices // 4, 4, total, width)
    block = (devices // 4, 1, rows, width)
    specs = [
        pl.BlockSpec(block, lambda j, c, i=i: (0, slab_of(step_of(j), c[0]), i, 0)) for i in (0, 1)
    ]
    return [array, array], specs


def heads_of(ref, lo, hi):
    return jnp.concatenate([ref[h, :, lo:hi] for h in range(ref.shape[0])], axis=1)


def forward_slab(n, w1_ref, w2_ref, s_ref, d_out):
    width = n.shape[1]
    w1 = square(w1_ref)
    chunk = 256
    for at in range(0, width, chunk):
        a = dot_nn(n, w1[:, at : at + chunk])
        sig = jax.nn.sigmoid(a)
        s_ref[:, at : at + chunk] = (a * sig).astype(BF)
        d_out[:, at : at + chunk] = (sig * (1.0 + a * (1.0 - sig))).astype(BF)
    return dot_nt(s_ref[...], square(w2_ref))


def backward_slab(ef, w1_ref, w2_ref, d_in, da_ref):
    width = ef.shape[1]
    w2 = square(w2_ref)
    chunk = 256
    for at in range(0, width, chunk):
        ds = dot_nn(ef, w2[:, at : at + chunk])
        da_ref[:, at : at + chunk] = (ds * d_in[:, at : at + chunk].astype(F32)).astype(BF)
    return dot_nt(da_ref[...], square(w1_ref))


def keep_slab(step, cells, pack_ref, pack_at, own_ref):
    @pl.when(step < 2)
    def _():
        pack_ref[pack_at + step] = cells

    @pl.when(step >= 2)
    def _():
        own_ref[0] = cells


def first_kernel(
    core_ref,
    x_ref,
    w1_ref,
    w2_ref,
    wp_ref,
    vec_ref,
    x1_ref,
    n2_ref,
    pack_ref,
    own_ref,
    d_ref,
    q_ref,
    k_ref,
    v_ref,
    acc_ref,
    s_ref,
):
    step = pl.program_id(0)

    @pl.when(step == 0)
    def _():
        normed, _ = norm_stats(x_ref[...].astype(F32))
        pack_ref[0] = (normed * vec_ref[0:1, :] + vec_ref[1:2, :]).astype(BF)
        acc_ref[...] = jnp.zeros_like(acc_ref)

    @pl.when(step < 4)
    def _():
        acc_ref[...] += forward_slab(pack_ref[0], w1_ref, w2_ref, s_ref, d_ref.at[0])
        keep_slab(step, s_ref[...], pack_ref, 1, own_ref)

    @pl.when(step == 3)
    def _():
        x1 = x_ref[...].astype(F32) + 0.5 * acc_ref[...]
        x1_ref[...] = x1
        normed, _ = norm_stats(x1)
        n2_ref[...] = (normed * vec_ref[2:3, :] + vec_ref[3:4, :]).astype(BF)

    for part, ref in enumerate((q_ref, k_ref, v_ref)):

        @pl.when(step == 4 + part)
        def _():
            projected = dot_nn(n2_ref[...], square(wp_ref))
            if part == 0:
                projected = projected + vec_ref[4:5, :]
            projected = projected.astype(BF)
            for h in range(ref.shape[0]):
                ref[h] = projected[:, h * DH : (h + 1) * DH]


def first_call(core, x, gathered, rows, proj, vectors):
    frames, width = x.shape
    heads = width // DH
    fixed = lambda *shape: pl.BlockSpec(shape, lambda j, c: (0,) * len(shape))
    slabs, slab_blocks = slab_specs(gathered, rows, lambda j: jnp.minimum(j, 3))
    proj_array, proj_block = proj.blocks(lambda j: jnp.clip(j - 4, 0, 2), 3)
    return pl.pallas_call(
        first_kernel,
        grid_spec=pltpu.PrefetchScalarGridSpec(
            num_scalar_prefetch=1,
            grid=(7,),
            in_specs=[fixed(frames, width)] + slab_blocks + [proj_block, fixed(*vectors.shape)],
            out_specs=[
                fixed(frames, width),
                fixed(frames, width),
                fixed(3, frames, width),
                pl.BlockSpec((1, frames, width), lambda j, c: (jnp.clip(j - 2, 0, 1), 0, 0)),
                pl.BlockSpec((1, frames, width), lambda j, c: (jnp.minimum(j, 3), 0, 0)),
                fixed(heads, frames, DH),
                fixed(heads, frames, DH),
                fixed(heads, frames, DH),
            ],
            scratch_shapes=[pltpu.VMEM((frames, width), F32), pltpu.VMEM((frames, width), BF)],
        ),
        out_shape=[
            jax.ShapeDtypeStruct((frames, width), F32),
            jax.ShapeDtypeStruct((frames, width), BF),
            jax.ShapeDtypeStruct((3, frames, width), BF),
            jax.ShapeDtypeStruct((2, frames, width), BF),
            jax.ShapeDtypeStruct((4, frames, width), BF),
            jax.ShapeDtypeStruct((heads, frames, DH), BF),
            jax.ShapeDtypeStruct((heads, frames, DH), BF),
            jax.ShapeDtypeStruct((heads, frames, DH), BF),
        ],
        compiler_params=pltpu.CompilerParams(vmem_limit_bytes=VMEM_BYTES),
        cost_estimate=pl.CostEstimate(
            flops=22 * frames * width * width,
            bytes_accessed=22 * width * width + 40 * frames * width,
            transcendentals=4 * frames * width,
        ),
        name="first_part",
    )(core, x, *slabs, proj_array, vectors)


def gate_kernel(extra, mh_ref, x1_ref, w_ref, vec_ref, cols_ref, *refs):
    mixed_ref, x2_ref, n3_ref, lin_ref, sig_ref, g_ref = refs[extra:]
    step = pl.program_id(0)

    @pl.when(step == 0)
    def _():
        mixed = heads_of(mh_ref, 0, DH)
        mixed_ref[...] = mixed
        x2 = x1_ref[...] + dot_nn(mixed, square(w_ref))
        x2_ref[...] = x2
        normed, _ = norm_stats(x2)
        n3_ref[...] = (normed * vec_ref[0:1, :] + vec_ref[1:2, :]).astype(BF)

    @pl.when(step == 1)
    def _():
        lin_ref[...] = dot_nn(n3_ref[...], square(w_ref))

    @pl.when(step == 2)
    def _():
        sig = jax.nn.sigmoid(dot_nn(n3_ref[...], square(w_ref)))
        sig_ref[...] = sig
        g_ref[...] = (lin_ref[...] * sig * cols_ref[:, KSIZE : KSIZE + 1]).astype(BF)


def gate_call(mixed_heads, x1, weights, vectors, columns, order=()):
    frames, width = x1.shape
    fixed = lambda *shape: pl.BlockSpec(shape, lambda j: (0,) * len(shape))
    array, block = weights.blocks(lambda j: j, 3)
    return pl.pallas_call(
        functools.partial(gate_kernel, len(order)),
        grid=(3,),
        in_specs=[
            fixed(*mixed_heads.shape),
            fixed(frames, width),
            block,
            fixed(*vectors.shape),
            fixed(*columns.shape),
        ]
        + [pl.BlockSpec(memory_space=pl.ANY)] * len(order),
        out_specs=[fixed(frames, width)] * 6,
        out_shape=[jax.ShapeDtypeStruct((frames, width), t) for t in (BF, F32, BF, F32, F32, BF)],
        compiler_params=pltpu.CompilerParams(vmem_limit_bytes=VMEM_BYTES),
        cost_estimate=pl.CostEstimate(
            flops=6 * frames * width * width,
            bytes_accessed=6 * width * width + 24 * frames * width,
            transcendentals=frames * width,
        ),
        name="attention_out_and_gate",
    )(mixed_heads, x1, array, vectors, columns, *order)


PAD = 8


def lay_out(scratch, before, cells, after):
    frames = cells.shape[0]
    scratch[PAD - REACH : PAD, :] = before
    scratch[PAD : PAD + frames, :] = cells
    scratch[PAD + frames : PAD + frames + REACH, :] = after


def conv_kernel(g_ref, before_ref, after_ref, vec_ref, cols_ref, conv_ref, sums_ref, ext):
    frames = g_ref.shape[0]
    lay_out(
        ext, before_ref[...].astype(F32), g_ref[...].astype(F32), after_ref[...].astype(F32)
    )
    conv = jnp.zeros(g_ref.shape, F32)
    for m in range(KSIZE):
        rows = ext[PAD - REACH + m : PAD - REACH + m + frames, :]
        conv = conv + vec_ref[m : m + 1, :] * rows * cols_ref[:, m : m + 1]
    conv_ref[...] = conv
    counted = conv * cols_ref[:, KSIZE : KSIZE + 1]
    sums = jnp.concatenate(
        [jnp.sum(counted, axis=0, keepdims=True), jnp.sum(counted * conv, axis=0, keepdims=True)]
    )
    sums_ref[...] = jnp.broadcast_to(sums[None], sums_ref.shape)


def conv_call(g, before, after, taps, columns, devices):
    frames, width = g.shape
    return pl.pallas_call(
        conv_kernel,
        out_shape=[
            jax.ShapeDtypeStruct((frames, width), F32),
            jax.ShapeDtypeStruct((devices, 2, width), F32),
        ],
        scratch_shapes=[pltpu.VMEM((frames + 2 * PAD, width), F32)],
        compiler_params=pltpu.CompilerParams(vmem_limit_bytes=VMEM_BYTES),
        cost_estimate=pl.CostEstimate(
            flops=20 * frames * width, bytes_accessed=8 * frames * width, transcendentals=0
        ),
        name="depthwise",
    )(g, before, after, taps, columns)


def batch_stats(moments_ref, count):
    sums = jnp.sum(moments_ref[...], axis=0)
    mean = sums[0:1, :] / count
    return mean, lax.rsqrt(sums[1:2, :] / count - mean * mean + EPSILON)


def second_kernel(
    core_ref,
    x2_ref,
    conv_ref,
    mom_ref,
    wc_ref,
    w1_ref,
    w2_ref,
    vec_ref,
    og_ref,
    out_ref,
    swish_ref,
    dx_ref,
    ew_ref,
    dz_ref,
    sums_ref,
    spread_ref,
    pack_ref,
    s_own_ref,
    da_own_ref,
    x3_ref,
    acc_ref,
    d_ref,
    dsilu_ref,
    s_ref,
    dx4_ref,
):
    step = pl.program_id(0)
    count = vec_ref[6:7, :]

    @pl.when(step == 0)
    def _():
        mean, inv = batch_stats(mom_ref, count)
        z = (conv_ref[...] - mean) * inv * vec_ref[0:1, :] + vec_ref[1:2, :]
        sig = jax.nn.sigmoid(z)
        swish = (z * sig).astype(BF)
        swish_ref[...] = swish
        dsilu_ref[...] = sig * (1.0 + z * (1.0 - sig))
        x3 = x2_ref[...] + dot_nn(swish, square(wc_ref))
        x3_ref[...] = x3
        normed, _ = norm_stats(x3)
        pack_ref[0] = (normed * vec_ref[2:3, :] + vec_ref[3:4, :]).astype(BF)
        acc_ref[...] = jnp.zeros_like(acc_ref)

    @pl.when(step < 4)
    def _():
        acc_ref[...] += forward_slab(pack_ref[0], w1_ref, w2_ref, s_ref, d_ref.at[step])
        keep_slab(step, s_ref[...], pack_ref, 1, s_own_ref)

    @pl.when(step == 3)
    def _():
        normed, inv_std = norm_stats(x3_ref[...] + 0.5 * acc_ref[...])
        gain = vec_ref[4:5, :]
        out_ref[...] = (normed * gain + vec_ref[5:6, :]).astype(BF)
        upstream = og_ref[...].astype(F32)
        dx4 = norm_back(upstream, normed, inv_std, gain)
        dx4_ref[...] = dx4
        pack_ref[3] = (0.5 * dx4).astype(BF)
        sums_ref[0:1, :] = jnp.sum(upstream * normed, axis=0, keepdims=True)
        sums_ref[1:2, :] = jnp.sum(upstream, axis=0, keepdims=True)
        acc_ref[...] = jnp.zeros_like(acc_ref)

    @pl.when(step >= 4)
    def _():
        acc_ref[...] += backward_slab(pack_ref[3], w1_ref, w2_ref, d_ref.at[step - 4], s_ref)
        keep_slab(step - 4, s_ref[...], pack_ref, 4, da_own_ref)

    @pl.when(step == 7)
    def _():
        normed, inv_std = norm_stats(x3_ref[...])
        dn = acc_ref[...]
        dx3 = dx4_ref[...] + norm_back(dn, normed, inv_std, vec_ref[2:3, :])
        dx_ref[...] = dx3
        sums_ref[2:3, :] = jnp.sum(dn * normed, axis=0, keepdims=True)
        sums_ref[3:4, :] = jnp.sum(dn, axis=0, keepdims=True)
        ew = dx3.astype(BF)
        ew_ref[...] = ew
        dz = dot_nt(ew, square(wc_ref)) * dsilu_ref[...]
        dz_ref[...] = dz
        mean, inv = batch_stats(mom_ref, count)
        zhat = (conv_ref[...] - mean) * inv
        totals = jnp.concatenate(
            [jnp.sum(dz * zhat, axis=0, keepdims=True), jnp.sum(dz, axis=0, keepdims=True)]
        )
        sums_ref[4:6, :] = totals
        sums_ref[6:8, :] = jnp.zeros((2, dz.shape[1]), F32)
        spread_ref[...] = jnp.broadcast_to(totals[None], spread_ref.shape)


def second_call(core, x2, conv, moments, weights, gathered, rows, vectors, out_grad):
    frames, width = x2.shape
    fixed = lambda *shape: pl.BlockSpec(shape, lambda j, c: (0,) * len(shape))
    slabs, slab_blocks = slab_specs(gathered, rows, lambda j: j % 4)
    array, block = weights.blocks(lambda j: 0, 1)
    whole = fixed(frames, width)
    return pl.pallas_call(
        second_kernel,
        grid_spec=pltpu.PrefetchScalarGridSpec(
            num_scalar_prefetch=1,
            grid=(8,),
            in_specs=[whole, whole, fixed(*moments.shape), block]
            + slab_blocks
            + [fixed(*vectors.shape), whole],
            out_specs=[
                whole,
                whole,
                whole,
                whole,
                whole,
                fixed(8, width),
                fixed(*moments.shape),
                fixed(6, frames, width),
                pl.BlockSpec((1, frames, width), lambda j, c: (jnp.clip(j - 2, 0, 1), 0, 0)),
                pl.BlockSpec((1, frames, width), lambda j, c: (jnp.clip(j - 6, 0, 1), 0, 0)),
            ],
            scratch_shapes=[
                pltpu.VMEM((frames, width), F32),
                pltpu.VMEM((frames, width), F32),
                pltpu.VMEM((4, frames, width), BF),
                pltpu.VMEM((frames, width), F32),
                pltpu.VMEM((frames, width), BF),
                pltpu.VMEM((frames, width), F32),
            ],
        ),
        out_shape=[
            jax.ShapeDtypeStruct((frames, width), BF),
            jax.ShapeDtypeStruct((frames, width), BF),
            jax.ShapeDtypeStruct((frames, width), F32),
            jax.ShapeDtypeStruct((frames, width), BF),
            jax.ShapeDtypeStruct((frames, width), F32),
            jax.ShapeDtypeStruct((8, width), F32),
            jax.ShapeDtypeStruct(moments.shape, F32),
            jax.ShapeDtypeStruct((6, frames, width), BF),
            jax.ShapeDtypeStruct((2, frames, width), BF),
            jax.ShapeDtypeStruct((2, frames, width), BF),
        ],
        compiler_params=pltpu.CompilerParams(vmem_limit_bytes=VMEM_BYTES),
        cost_estimate=pl.CostEstimate(
            flops=36 * frames * width * width,
            bytes_accessed=34 * width * width + 40 * frames * width,
            transcendentals=5 * frames * width,
        ),
        name="second_part",
    )(core, x2, conv, moments, array, *slabs, vectors, out_grad)


def back_kernel(
    extra,
    dz_ref,
    conv_ref,
    edge_before_ref,
    edge_after_ref,
    g_ref,
    g_before_ref,
    g_after_ref,
    mom_ref,
    tot_ref,
    lin_ref,
    sig_ref,
    x2_ref,
    dx3_ref,
    w_ref,
    vec_ref,
    cols_ref,
    *refs,
):
    pg_ref, dx2_ref, ey_ref, do_ref, sums_ref, ext, g_ext, acc_ref, b_ref = refs[extra:]
    step = pl.program_id(0)
    frames, width = dz_ref.shape

    @pl.when(step == 0)
    def _():
        count = vec_ref[8:9, :]
        gain = vec_ref[5:6, :]
        mean, inv = batch_stats(mom_ref, count)
        totals = jnp.sum(tot_ref[...], axis=0) * gain

        def conv_grad(dz, conv, valid):
            zhat = (conv - mean) * inv
            dc = inv * (dz * gain - valid * (totals[1:2, :] + zhat * totals[0:1, :]) / count)
            return dc.astype(BF).astype(F32)

        valid = cols_ref[:, KSIZE : KSIZE + 1]
        dc = conv_grad(dz_ref[...], conv_ref[...], valid)
        edges = []
        for at, ref in ((0, edge_before_ref), (REACH, edge_after_ref)):
            edges.append(
                conv_grad(
                    ref[0:REACH, :],
                    ref[REACH : 2 * REACH, :],
                    cols_ref[at : at + REACH, KSIZE + 1 : KSIZE + 2],
                )
            )
        lay_out(ext, edges[0], dc, edges[1])
        lay_out(
            g_ext,
            g_before_ref[...].astype(F32),
            g_ref[...].astype(F32),
            g_after_ref[...].astype(F32),
        )
        dg = jnp.zeros((frames, width), F32)
        for m in range(KSIZE):
            back = 2 * REACH - m
            rows = ext[PAD - REACH + back : PAD - REACH + back + frames, :]
            dg = dg + vec_ref[m : m + 1, :] * rows * cols_ref[:, back : back + 1]
            there = g_ext[PAD - REACH + m : PAD - REACH + m + frames, :]
            sums_ref[2 + m : 3 + m, :] = jnp.sum(
                dc * there * cols_ref[:, m : m + 1], axis=0, keepdims=True
            )
        sums_ref[7:8, :] = jnp.zeros((1, width), F32)
        de = dg * valid
        sig = sig_ref[...]
        pa = (de * sig).astype(BF)
        pb = (de * lin_ref[...] * sig * (1.0 - sig)).astype(BF)
        pg_ref[:, :width] = pa
        pg_ref[:, width:] = pb
        b_ref[...] = pb
        acc_ref[...] = dot_nt(pa, square(w_ref))

    @pl.when(step == 1)
    def _():
        dn = acc_ref[...] + dot_nt(b_ref[...], square(w_ref))
        normed, inv_std = norm_stats(x2_ref[...])
        dx2 = dx3_ref[...] + norm_back(dn, normed, inv_std, vec_ref[6:7, :])
        dx2_ref[...] = dx2
        ey_ref[...] = dx2.astype(BF)
        sums_ref[0:1, :] = jnp.sum(dn * normed, axis=0, keepdims=True)
        sums_ref[1:2, :] = jnp.sum(dn, axis=0, keepdims=True)

    @pl.when(step == 2)
    def _():
        grads = dot_nt(ey_ref[...], square(w_ref)).astype(BF)
        for h in range(do_ref.shape[0]):
            do_ref[h] = grads[:, h * DH : (h + 1) * DH]


def back_call(dz, conv, edges, g, g_edges, moments, totals, lin, sig, x2, dx3, weights, vectors, columns, order):
    frames, width = dz.shape
    fixed = lambda *shape: pl.BlockSpec(shape, lambda j: (0,) * len(shape))
    array, block = weights.blocks(lambda j: (j + 1) % 3, 3)
    whole = fixed(frames, width)
    return pl.pallas_call(
        functools.partial(back_kernel, len(order)),
        grid=(3,),
        in_specs=[
            whole,
            whole,
            fixed(2 * REACH, width),
            fixed(2 * REACH, width),
            whole,
            fixed(REACH, width),
            fixed(REACH, width),
            fixed(*moments.shape),
            fixed(*totals.shape),
            whole,
            whole,
            whole,
            whole,
            block,
            fixed(*vectors.shape),
            fixed(*columns.shape),
        ]
        + [pl.BlockSpec(memory_space=pl.ANY)] * len(order),
        out_specs=[
            fixed(frames, 2 * width),
            whole,
            whole,
            fixed(width // DH, frames, DH),
            fixed(8, width),
        ],
        out_shape=[
            jax.ShapeDtypeStruct((frames, 2 * width), BF),
            jax.ShapeDtypeStruct((frames, width), F32),
            jax.ShapeDtypeStruct((frames, width), BF),
            jax.ShapeDtypeStruct((width // DH, frames, DH), BF),
            jax.ShapeDtypeStruct((8, width), F32),
        ],
        scratch_shapes=[
            pltpu.VMEM((frames + 2 * PAD, width), F32),
            pltpu.VMEM((frames + 2 * PAD, width), F32),
            pltpu.VMEM((frames, width), F32),
            pltpu.VMEM((frames, width), BF),
        ],
        compiler_params=pltpu.CompilerParams(vmem_limit_bytes=VMEM_BYTES),
        cost_estimate=pl.CostEstimate(
            flops=6 * frames * width * width,
            bytes_accessed=6 * width * width + 34 * frames * width,
            transcendentals=0,
        ),
        name="convolution_backward",
    )(
        dz,
        conv,
        edges[0],
        edges[1],
        g,
        g_edges[0],
        g_edges[1],
        moments,
        totals,
        lin,
        sig,
        x2,
        dx3,
        array,
        vectors,
        columns,
        *order,
    )


def proj_back_kernel(extra, dq_ref, dkv_ref, dx2_ref, x1_ref, wp_ref, vec_ref, *refs):
    dx1_ref, ef_ref, sums_ref, acc_ref = refs[extra:]
    step = pl.program_id(0)

    @pl.when(step == 0)
    def _():
        dq = heads_of(dq_ref, 0, DH)
        acc_ref[...] = dot_nt(dq, square(wp_ref))
        sums_ref[2:3, :] = jnp.sum(dq.astype(F32), axis=0, keepdims=True)
        sums_ref[3:8, :] = jnp.zeros((5, dq.shape[1]), F32)

    @pl.when(step == 1)
    def _():
        acc_ref[...] += dot_nt(heads_of(dkv_ref, 0, DH), square(wp_ref))

    @pl.when(step == 2)
    def _():
        dn = acc_ref[...] + dot_nt(heads_of(dkv_ref, DH, 2 * DH), square(wp_ref))
        normed, inv_std = norm_stats(x1_ref[...])
        dx1 = dx2_ref[...] + norm_back(dn, normed, inv_std, vec_ref[1:2, :])
        dx1_ref[...] = dx1
        ef_ref[0] = (0.5 * dx1).astype(BF)
        sums_ref[0:1, :] = jnp.sum(dn * normed, axis=0, keepdims=True)
        sums_ref[1:2, :] = jnp.sum(dn, axis=0, keepdims=True)


def proj_back_call(dq, dkv, dx2, x1, proj, vectors, order):
    frames, width = x1.shape
    fixed = lambda *shape: pl.BlockSpec(shape, lambda j: (0,) * len(shape))
    array, block = proj.blocks(lambda j: j, 3)
    whole = fixed(frames, width)
    return pl.pallas_call(
        functools.partial(proj_back_kernel, len(order)),
        grid=(3,),
        in_specs=[fixed(*dq.shape), fixed(*dkv.shape), whole, whole, block, fixed(*vectors.shape)]
        + [pl.BlockSpec(memory_space=pl.ANY)] * len(order),
        out_specs=[whole, fixed(1, frames, width), fixed(8, width)],
        out_shape=[
            jax.ShapeDtypeStruct((frames, width), F32),
            jax.ShapeDtypeStruct((1, frames, width), BF),
            jax.ShapeDtypeStruct((8, width), F32),
        ],
        scratch_shapes=[pltpu.VMEM((frames, width), F32)],
        compiler_params=pltpu.CompilerParams(vmem_limit_bytes=VMEM_BYTES),
        cost_estimate=takes(9),
        name="projections_backward",
    )(dq, dkv, dx2, x1, array, vectors, *order)


def last_kernel(extra, core_ref, dx1_ref, ef_ref, x_ref, w1_ref, w2_ref, d_ref, vec_ref, *refs):
    gin_ref, sums_ref, first_ref, second_ref, own_ref, acc_ref, da_ref = refs[extra:]
    step = pl.program_id(0)

    @pl.when(step == 0)
    def _():
        acc_ref[...] = jnp.zeros_like(acc_ref)

    acc_ref[...] += backward_slab(ef_ref[0], w1_ref, w2_ref, d_ref.at[0], da_ref)
    for at, ref in enumerate((first_ref, second_ref)):

        @pl.when(step == at)
        def _():
            ref[0] = da_ref[...]

    @pl.when(step >= 2)
    def _():
        own_ref[0] = da_ref[...]

    @pl.when(step == 3)
    def _():
        normed, inv_std = norm_stats(x_ref[...].astype(F32))
        dn = acc_ref[...]
        dx = dx1_ref[...] + norm_back(dn, normed, inv_std, vec_ref[0:1, :])
        gin_ref[...] = dx.astype(BF)
        sums_ref[0:1, :] = jnp.sum(dn * normed, axis=0, keepdims=True)
        sums_ref[1:2, :] = jnp.sum(dn, axis=0, keepdims=True)
        sums_ref[2:8, :] = jnp.zeros((6, dn.shape[1]), F32)


def last_call(core, dx1, ef, x, gathered, rows, slope, vectors, order):
    frames, width = x.shape
    fixed = lambda *shape: pl.BlockSpec(shape, lambda j, c: (0,) * len(shape))
    slabs, slab_blocks = slab_specs(gathered, rows, lambda j: j)
    whole = fixed(frames, width)
    return pl.pallas_call(
        functools.partial(last_kernel, len(order)),
        grid_spec=pltpu.PrefetchScalarGridSpec(
            num_scalar_prefetch=1,
            grid=(4,),
            in_specs=[whole, fixed(1, frames, width), whole]
            + slab_blocks
            + [pl.BlockSpec((1, frames, width), lambda j, c: (j, 0, 0)), fixed(*vectors.shape)]
            + [pl.BlockSpec(memory_space=pl.ANY)] * len(order),
            out_specs=[
                whole,
                fixed(8, width),
                fixed(1, frames, width),
                fixed(1, frames, width),
                pl.BlockSpec((1, frames, width), lambda j, c: (jnp.clip(j - 2, 0, 1), 0, 0)),
            ],
            scratch_shapes=[pltpu.VMEM((frames, width), F32), pltpu.VMEM((frames, width), BF)],
        ),
        out_shape=[
            jax.ShapeDtypeStruct((frames, width), BF),
            jax.ShapeDtypeStruct((8, width), F32),
            jax.ShapeDtypeStruct((1, frames, width), BF),
            jax.ShapeDtypeStruct((1, frames, width), BF),
            jax.ShapeDtypeStruct((2, frames, width), BF),
        ],
        compiler_params=pltpu.CompilerParams(vmem_limit_bytes=VMEM_BYTES),
        cost_estimate=takes(15),
        name="last_part",
    )(core, dx1, ef, x, *slabs, slope, vectors, *order)


def fill_window(kv_ref, parts):
    for column, refs in ((0, parts[:3]), (DH, parts[3:])):
        at = 0
        for ref in refs:
            kv_ref[at : at + ref.shape[0], column : column + DH] = ref[...]
            at += ref.shape[0]
    kv_ref[at:, :] = jnp.zeros((kv_ref.shape[0] - at, kv_ref.shape[1]), kv_ref.dtype)


def attn_fwd_kernel(
    origin,
    low_ref,
    high_ref,
    c2_ref,
    q_ref,
    *refs,
):
    lo_ref, hi_ref, o_ref, lse_ref, kv_ref = refs[6:]
    block = pl.program_id(0)

    @pl.when(block == 0)
    def _():
        fill_window(kv_ref, refs[:6])

    rows = q_ref.shape[0]
    q = q_ref[...]
    c1 = LOG2E * DH**-0.5
    c2 = c2_ref[0]
    at = lax.broadcasted_iota(jnp.int32, (1, rows), 1) + (origin + block * rows)
    q_pos = at.astype(F32)
    lo_q, hi_q = lo_ref[...], hi_ref[...]
    first = low_ref[block]
    steps = (high_ref[block] - first + (BK - 1)) // BK

    def step(t, carry):
        top, total, mixed = carry
        start = pl.multiple_of(first + t * BK, 128)
        k = kv_ref[pl.ds(start, BK), :DH]
        v = kv_ref[pl.ds(start, BK), DH:]
        k_pos = (lax.broadcasted_iota(jnp.int32, (BK, 1), 0) + start).astype(F32)
        scores = dot_nt(k, q) * c1 - jnp.abs(k_pos - q_pos) * c2
        scores = jnp.where((k_pos >= lo_q) & (k_pos < hi_q), scores, MASKED)
        new_top = jnp.maximum(top, jnp.max(scores, axis=0, keepdims=True))
        expo = jnp.exp2(scores - new_top)
        keep = jnp.exp2(top - new_top)
        total = total * keep + jnp.sum(expo, axis=0, keepdims=True)
        mixed = mixed * keep + dot_tn(v, expo.astype(BF))
        return new_top, total, mixed

    top, total, mixed = lax.fori_loop(
        0,
        steps,
        step,
        (
            jnp.full((1, rows), MASKED, F32),
            jnp.zeros((1, rows), F32),
            jnp.zeros((DH, rows), F32),
        ),
    )
    o_ref[...] = (mixed / total).T.astype(BF)
    lse_ref[...] = top + jnp.log2(total)


def attn_fwd(q, kv, low, high, c2, lo_q, hi_q, origin):
    frames = q.shape[0]
    window = sum(v.shape[0] for v in kv[:3]) + BK
    parts = [pl.BlockSpec(v.shape, lambda i, *_: (0, 0)) for v in kv]
    blocks = frames // BQ
    pairs = frames * 1024 * DH
    grid_spec = pltpu.PrefetchScalarGridSpec(
        num_scalar_prefetch=3,
        grid=(blocks,),
        in_specs=[
            pl.BlockSpec((BQ, DH), lambda i, *_: (i, 0)),
            *parts,
            pl.BlockSpec((1, BQ), lambda i, *_: (0, i)),
            pl.BlockSpec((1, BQ), lambda i, *_: (0, i)),
        ],
        out_specs=[
            pl.BlockSpec((BQ, DH), lambda i, *_: (i, 0)),
            pl.BlockSpec((1, BQ), lambda i, *_: (0, i)),
        ],
        scratch_shapes=[pltpu.VMEM((window, 2 * DH), BF)],
    )

    def kernel(*refs):
        attn_fwd_kernel(origin, *refs)

    return pl.pallas_call(
        kernel,
        grid_spec=grid_spec,
        out_shape=[
            jax.ShapeDtypeStruct((frames, DH), BF),
            jax.ShapeDtypeStruct((1, frames), F32),
        ],
        compiler_params=pltpu.CompilerParams(vmem_limit_bytes=VMEM_BYTES),
        cost_estimate=pl.CostEstimate(
            flops=4 * pairs, bytes_accessed=4 * window * DH, transcendentals=frames * 1024
        ),
        name="attention_forward",
    )(low, high, c2, q, *kv, lo_q, hi_q)


def attn_bwd_kernel(
    origin,
    extra,
    low_ref,
    high_ref,
    c2_ref,
    q_ref,
    o_ref,
    do_ref,
    lse_ref,
    lo_ref,
    hi_ref,
    *refs,
):
    dq_ref, prev_ref, own_ref, next_ref, dk_acc, dv_acc, kv_ref = refs[6 + extra :]
    block = pl.program_id(0)
    rows = q_ref.shape[0]
    frames = own_ref.shape[0]
    scale = DH**-0.5
    c1 = LOG2E * scale

    @pl.when(block == 0)
    def _():
        fill_window(kv_ref, refs[:6])
        dk_acc[...] = jnp.zeros_like(dk_acc)
        dv_acc[...] = jnp.zeros_like(dv_acc)

    q = q_ref[...]
    do = do_ref[...]
    c2 = c2_ref[0]
    delta = jnp.sum((o_ref[...].astype(F32) * do.astype(F32)).T, axis=0, keepdims=True)
    lse = lse_ref[...]
    at = lax.broadcasted_iota(jnp.int32, (1, rows), 1) + (origin + block * rows)
    q_pos = at.astype(F32)
    lo_q, hi_q = lo_ref[...], hi_ref[...]
    first = low_ref[block]
    steps = (high_ref[block] - first + (BK - 1)) // BK

    def step(t, dq):
        start = pl.multiple_of(first + t * BK, 128)
        here = pl.ds(start, BK)
        k = kv_ref[here, :DH]
        v = kv_ref[here, DH:]
        k_pos = (lax.broadcasted_iota(jnp.int32, (BK, 1), 0) + start).astype(F32)
        scores = dot_nt(k, q) * c1 - jnp.abs(k_pos - q_pos) * c2 - lse
        scores = jnp.where((k_pos >= lo_q) & (k_pos < hi_q), scores, MASKED)
        probs = jnp.exp2(scores)
        grads = (probs * (dot_nt(v, do) - delta)).astype(BF)
        dv_acc[here, :] += dot_nn(probs.astype(BF), do)
        dk_acc[here, :] += dot_nn(grads, q)
        return dq + dot_tn(k, grads)

    dq = lax.fori_loop(0, steps, step, jnp.zeros((DH, rows), F32))
    dq_ref[...] = (dq * scale).T.astype(BF)

    @pl.when(block == pl.num_programs(0) - 1)
    def _():
        prev_ref[:, :DH] = (dk_acc[:origin, :] * scale).astype(BF)
        prev_ref[:, DH:] = dv_acc[:origin, :].astype(BF)
        own_ref[:, :DH] = dk_acc[origin : origin + frames, :] * scale
        own_ref[:, DH:] = dv_acc[origin : origin + frames, :]
        next_ref[:, :DH] = (dk_acc[origin + frames : 2 * origin + frames, :] * scale).astype(BF)
        next_ref[:, DH:] = dv_acc[origin + frames : 2 * origin + frames, :].astype(BF)


def attn_bwd(q, o, do, lse, kv, low, high, c2, lo_q, hi_q, origin, order=()):
    frames = q.shape[0]
    blocks = frames // BQ
    pairs = frames * 1024 * DH
    window = sum(v.shape[0] for v in kv[:3]) + BK
    parts = [pl.BlockSpec(v.shape, lambda i, *_: (0, 0)) for v in kv]
    tile = pl.BlockSpec((BQ, DH), lambda i, *_: (i, 0))
    row = pl.BlockSpec((1, BQ), lambda i, *_: (0, i))
    grid_spec = pltpu.PrefetchScalarGridSpec(
        num_scalar_prefetch=3,
        grid=(blocks,),
        in_specs=[
            tile,
            tile,
            tile,
            row,
            row,
            row,
            *parts,
        ]
        + [pl.BlockSpec(memory_space=pl.ANY)] * len(order),
        out_specs=[
            tile,
            pl.BlockSpec((origin, 2 * DH), lambda i, *_: (0, 0)),
            pl.BlockSpec((frames, 2 * DH), lambda i, *_: (0, 0)),
            pl.BlockSpec((origin, 2 * DH), lambda i, *_: (0, 0)),
        ],
        scratch_shapes=[
            pltpu.VMEM((window, DH), F32),
            pltpu.VMEM((window, DH), F32),
            pltpu.VMEM((window, 2 * DH), BF),
        ],
    )

    def kernel(*refs):
        attn_bwd_kernel(origin, len(order), *refs)

    return pl.pallas_call(
        kernel,
        grid_spec=grid_spec,
        out_shape=[
            jax.ShapeDtypeStruct((frames, DH), BF),
            jax.ShapeDtypeStruct((origin, 2 * DH), BF),
            jax.ShapeDtypeStruct((frames, 2 * DH), F32),
            jax.ShapeDtypeStruct((origin, 2 * DH), BF),
        ],
        compiler_params=pltpu.CompilerParams(vmem_limit_bytes=VMEM_BYTES),
        cost_estimate=pl.CostEstimate(
            flops=80 * pairs, bytes_accessed=8 * window * DH, transcendentals=frames * 1024
        ),
        name="attention_backward",
    )(low, high, c2, q, o, do, lse, lo_q, hi_q, *kv, *order)


def pass_on_kernel(extra, *refs):
    count = (len(refs) - extra) // 2
    for a, b in zip(refs[:count], refs[count + extra :]):
        b[...] = a[...]


def pass_on(arrays, order):
    return pl.pallas_call(
        functools.partial(pass_on_kernel, len(order)),
        in_specs=[pl.BlockSpec(v.shape, lambda n=v.ndim: (0,) * n) for v in arrays]
        + [pl.BlockSpec(memory_space=pl.ANY)] * len(order),
        out_specs=[pl.BlockSpec(v.shape, lambda n=v.ndim: (0,) * n) for v in arrays],
        out_shape=[jax.ShapeDtypeStruct(v.shape, v.dtype) for v in arrays],
        compiler_params=pltpu.CompilerParams(vmem_limit_bytes=VMEM_BYTES // 3),
        cost_estimate=pl.CostEstimate(flops=1, bytes_accessed=1024, transcendentals=0),
        name="pass_on",
    )(*arrays, *order)


def join_kernel(extra, own_ref, before_ref, after_ref, *refs):
    out_ref = refs[extra]
    span = before_ref.shape[0]
    rows = own_ref.shape[0]
    out_ref[:span, :] = (own_ref[:span, :] + before_ref[...].astype(F32)).astype(BF)
    if rows > 2 * span:
        out_ref[span : rows - span, :] = own_ref[span : rows - span, :].astype(BF)
    out_ref[rows - span :, :] = (own_ref[rows - span :, :] + after_ref[...].astype(F32)).astype(BF)


def join_edges(own, before, after, order=()):
    return pl.pallas_call(
        functools.partial(join_kernel, len(order)),
        in_specs=[pl.BlockSpec(v.shape, lambda: (0, 0)) for v in (own, before, after)]
        + [pl.BlockSpec(memory_space=pl.ANY)] * len(order),
        out_specs=pl.BlockSpec(own.shape, lambda: (0, 0)),
        out_shape=jax.ShapeDtypeStruct(own.shape, BF),
        compiler_params=pltpu.CompilerParams(vmem_limit_bytes=VMEM_BYTES // 2),
        cost_estimate=pl.CostEstimate(
            flops=own.size, bytes_accessed=8 * own.size, transcendentals=0
        ),
        name="join_edges",
    )(own, before, after, *order)


def stack_kernel(extra, places, arrays, *refs):
    out_ref = refs[arrays + extra]
    rows_ref = refs[arrays + extra + 1]
    for at, (source, row) in enumerate(places):
        rows_ref[at : at + 1, :] = refs[source][row : row + 1, :]
    share = out_ref.shape[2]
    rows = rows_ref[...]
    for i in range(out_ref.shape[0]):
        out_ref[i] = rows[:, i * share : (i + 1) * share]


def stack_rows(arrays, places, devices, order=()):
    width = arrays[0].shape[1]
    share = width // devices
    if share % 32:
        rows = jnp.stack([arrays[source][row] for source, row in places])
        return rows.reshape(len(places), devices, share).transpose(1, 0, 2)
    return pl.pallas_call(
        functools.partial(stack_kernel, len(order), places, len(arrays)),
        in_specs=[pl.BlockSpec(v.shape, lambda: (0, 0)) for v in arrays]
        + [pl.BlockSpec(memory_space=pl.ANY)] * len(order),
        out_specs=pl.BlockSpec((devices, len(places), share), lambda: (0, 0, 0)),
        out_shape=jax.ShapeDtypeStruct((devices, len(places), share), F32),
        scratch_shapes=[pltpu.VMEM((len(places), width), F32)],
        name="stack_rows",
    )(*arrays, *order)


def halve_kernel(extra, sel_ref, kept_a, kept_b, got_a, got_b, *refs):
    send_ref, keep_ref = refs[extra:]
    send_ref[...] = (kept_a[0].astype(F32) + got_a[0].astype(F32)).astype(BF)
    keep_ref[...] = (kept_b[0].astype(F32) + got_b[0].astype(F32)).astype(BF)


def halve(kept, got, mine, order=()):
    count, _, rows, columns = kept.shape
    step = rows
    while step % 32 == 0 and step * columns > 512 * 1024:
        step //= 2
    block = (1, 1, step, columns)
    other = pl.BlockSpec(block, lambda i, j, m: (i, 1 - m[0], j, 0))
    own = pl.BlockSpec(block, lambda i, j, m: (i, m[0], j, 0))
    out = pl.BlockSpec((1, step, columns), lambda i, j, m: (i, j, 0))
    return pl.pallas_call(
        functools.partial(halve_kernel, len(order)),
        grid_spec=pltpu.PrefetchScalarGridSpec(
            num_scalar_prefetch=1,
            grid=(count, rows // step),
            in_specs=[other, own, other, own]
            + [pl.BlockSpec(memory_space=pl.ANY)] * len(order),
            out_specs=[out, out],
        ),
        out_shape=[jax.ShapeDtypeStruct((count, rows, columns), BF)] * 2,
        compiler_params=pltpu.CompilerParams(vmem_limit_bytes=VMEM_BYTES // 3),
        cost_estimate=pl.CostEstimate(flops=1024, bytes_accessed=1024, transcendentals=0),
        name="halve",
    )(mine.astype(jnp.int32)[None], kept, kept, got, got, *order)


def finish_kernel(extra, turned, kept_ref, got_ref, *refs):
    total = kept_ref[...].astype(F32) + got_ref[...].astype(F32)
    refs[extra][...] = total.T if turned else total


def finish(kept, got, turned=False, order=()):
    rows, columns = kept.shape
    fixed = pl.BlockSpec((rows, columns), lambda: (0, 0))
    shape = (columns, rows) if turned else (rows, columns)
    if turned and rows % 128:
        return finish(kept, got, False, order).T
    return pl.pallas_call(
        functools.partial(finish_kernel, len(order), turned),
        in_specs=[fixed, fixed] + [pl.BlockSpec(memory_space=pl.ANY)] * len(order),
        out_specs=pl.BlockSpec(shape, lambda: (0, 0)),
        out_shape=jax.ShapeDtypeStruct(shape, F32),
        compiler_params=pltpu.CompilerParams(vmem_limit_bytes=VMEM_BYTES // 3),
        name="finish",
    )(kept, got, *order)


def halve_both_kernel(extra, sel_ref, *refs):
    send_ref, keep_ref = refs[8 + extra :]
    for i in (0, 1):
        kept_a, kept_b, got_a, got_b = refs[4 * i : 4 * i + 4]
        rows = kept_a.shape[2]
        here = slice(i * rows, (i + 1) * rows)
        send_ref[0, here, :] = (kept_a[0, 0].astype(F32) + got_a[0, 0].astype(F32)).astype(BF)
        keep_ref[0, here, :] = (kept_b[0, 0].astype(F32) + got_b[0, 0].astype(F32)).astype(BF)


def halve_both(first, second, shape, mine, order=()):
    count, _, rows, columns = shape
    block = (1, 1, rows, columns)
    other = pl.BlockSpec(block, lambda i, m: (i, 1 - m[0], 0, 0))
    own = pl.BlockSpec(block, lambda i, m: (i, m[0], 0, 0))
    out = pl.BlockSpec((1, 2 * rows, columns), lambda i, m: (i, 0, 0))
    arrays = []
    for part in (first, second):
        kept, got = part.kept.reshape(shape), part.got.reshape(shape)
        arrays += [kept, kept, got, got]
    return pl.pallas_call(
        functools.partial(halve_both_kernel, len(order)),
        grid_spec=pltpu.PrefetchScalarGridSpec(
            num_scalar_prefetch=1,
            grid=(count,),
            in_specs=[other, own, other, own] * 2
            + [pl.BlockSpec(memory_space=pl.ANY)] * len(order),
            out_specs=[out, out],
        ),
        out_shape=[jax.ShapeDtypeStruct((count, 2 * rows, columns), BF)] * 2,
        compiler_params=pltpu.CompilerParams(vmem_limit_bytes=VMEM_BYTES // 3),
        cost_estimate=pl.CostEstimate(flops=1024, bytes_accessed=1024, transcendentals=0),
        name="halve_both",
    )(mine.astype(jnp.int32)[None], *arrays, *order)


def finish_both_kernel(extra, kept_ref, got_ref, *refs):
    first_ref, second_ref = refs[extra:]
    rows = first_ref.shape[0]
    total = kept_ref[...].astype(F32) + got_ref[...].astype(F32)
    first_ref[...] = total[:rows]
    second_ref[...] = total[rows:].T


def finish_both(total, rows, columns, order=()):
    kept, got = total.kept.reshape(2 * rows, columns), total.got.reshape(2 * rows, columns)
    if rows % 128:
        both = kept.astype(F32) + got.astype(F32)
        return both[:rows], both[rows:].T
    fixed = lambda *shape: pl.BlockSpec(shape, lambda: (0, 0))
    return pl.pallas_call(
        functools.partial(finish_both_kernel, len(order)),
        in_specs=[fixed(2 * rows, columns)] * 2
        + [pl.BlockSpec(memory_space=pl.ANY)] * len(order),
        out_specs=[fixed(rows, columns), fixed(columns, rows)],
        out_shape=[
            jax.ShapeDtypeStruct((rows, columns), F32),
            jax.ShapeDtypeStruct((columns, rows), F32),
        ],
        compiler_params=pltpu.CompilerParams(vmem_limit_bytes=VMEM_BYTES // 3),
        cost_estimate=pl.CostEstimate(flops=1024, bytes_accessed=1024, transcendentals=0),
        name="finish_both",
    )(kept, got, *order)


def total_kernel(extra, parts_ref, *refs):
    total = jnp.sum(parts_ref[...], axis=0)
    at = 0
    for ref in refs[extra:]:
        ref[...] = total[at : at + ref.shape[0]]
        at += ref.shape[0]


def total_of(parts, counts, order=()):
    columns = parts.shape[2]
    return pl.pallas_call(
        functools.partial(total_kernel, len(order)),
        in_specs=[pl.BlockSpec(parts.shape, lambda: (0, 0, 0))]
        + [pl.BlockSpec(memory_space=pl.ANY)] * len(order),
        out_specs=[pl.BlockSpec((n, columns), lambda: (0, 0)) for n in counts],
        out_shape=[jax.ShapeDtypeStruct((n, columns), F32) for n in counts],
        name="total_of",
    )(parts, *order)


class Sum:
    def __init__(self, kept, send, axis, bit):
        self.kept = kept
        self.send = send
        self.got = xor_send(send, axis, bit)

    def step(self, shape, axis, bit=1, order=()):
        mine = (lax.axis_index(axis) // bit) % 2
        send, kept = halve(self.kept.reshape(shape), self.got.reshape(shape), mine, order)
        return Sum(kept, send, axis, bit)

    def finish(self, shape, turned=False, order=()):
        return finish(self.kept.reshape(shape), self.got.reshape(shape), turned, order)


def slab_grad_kernel(split, extra, pair, sel_ref, la_ref, lb_ref, ra_ref, rb_ref, *refs):
    if pair:
        rb_ref = [jnp.where(pl.program_id(0) == 0, rb_ref[0], refs[0][0])]
        refs = refs[1:]
    out_ref = refs[extra]
    if split is None:
        out = dot_tn(la_ref[0], ra_ref[0]) + dot_tn(lb_ref[0], rb_ref[0])
    else:
        zs, rows = split
        take = [pl.ds(pl.multiple_of((z * 2 + sel_ref[0]) * rows, rows), rows) for z in range(zs)]
        left = [jnp.concatenate([ref[0, :, t] for t in take], axis=1) for ref in (la_ref, lb_ref)]
        out = dot_tn(left[0], ra_ref[0]) + dot_tn(left[1], rb_ref[0])
    out_ref[0] = out.astype(BF)


def slab_grad(left, right, x, y, order=(), lasting=0):
    left_a, left_b, left_at = left
    right_a, right_b, right_at = right
    pair = isinstance(right_b, tuple)
    _, frames, width = left_a.shape
    hidden = right_a.shape[2]
    zs = lax.axis_size("z")
    rows = width // (2 * zs)
    half = width // 2
    if x is None:
        split = None
        sel = y
        left_block = pl.BlockSpec((1, frames, half), lambda i, s: (left_at, 0, i))
        right = [
            pl.BlockSpec((1, frames, hidden), lambda i, s: (s[0], 0, 0)),
            pl.BlockSpec((1, frames, hidden), lambda i, s: (s[0] + right_at, 0, 0)),
        ]
    else:
        sel = x
        right = [
            pl.BlockSpec((1, frames, hidden), lambda i, s: (i, 0, 0)),
            pl.BlockSpec((1, frames, hidden), lambda i, s: (i + right_at, 0, 0)),
        ]
        if pair:
            right[1:] = [pl.BlockSpec((1, frames, hidden), lambda i, s: (0, 0, 0))] * 2
        if rows % 128 == 0:
            split = (zs, rows)
            left_block = pl.BlockSpec((1, frames, width), lambda i, s: (left_at, 0, 0))
        else:
            split = None
            left_block = pl.BlockSpec((1, frames, half), lambda i, s: (0, 0, 0))
            left_a, left_b = (
                pick(l[left_at].reshape(frames, zs, 2, rows), x, 2).reshape(1, frames, half)
                for l in (left_a, left_b)
            )
    return pl.pallas_call(
        functools.partial(slab_grad_kernel, split, len(order), pair),
        grid_spec=pltpu.PrefetchScalarGridSpec(
            num_scalar_prefetch=1,
            grid=(2,),
            in_specs=[left_block, left_block]
            + right
            + [pl.BlockSpec(memory_space=pl.ANY)] * len(order),
            out_specs=pl.BlockSpec((1, half, hidden), lambda i, s: (i, 0, 0)),
        ),
        out_shape=jax.ShapeDtypeStruct((2, half, hidden), BF),
        compiler_params=pltpu.CompilerParams(vmem_limit_bytes=VMEM_BYTES),
        cost_estimate=takes(lasting),
        name="slab_grad",
    )(sel.astype(jnp.int32)[None], left_a, left_b, right_a, *(right_b if pair else (right_b,)), *order)


def slab_sum(left, right, first, order=(), kept_order=()):
    place = lax.axis_index(first)
    picks = lambda i: (i, None) if first == "x" else (None, i)
    away = slab_grad(left, right, *picks(1 - place), order)
    return Sum(slab_grad(left, right, *picks(place), (away,) + tuple(kept_order)), away, first, 1)


def slab_second(total, first, order=()):
    zs = lax.axis_size("z")
    _, half, hidden = total.kept.shape
    if first == "x":
        return total.step((1, 2, half, hidden), "y", 1, order)
    return total.step((zs, 2, half // zs, hidden), "x", 1, order)


def z_steps(total, rows, columns, bits=None, order=()):
    zs = lax.axis_size("z")
    for bit in z_bits() if bits is None else bits:
        total = total.step((zs // (2 * bit), 2, rows, columns), "z", bit, order)
    return total


def z_both(first, second, rows, columns, order=()):
    zs = lax.axis_size("z")
    mine = lax.axis_index("z") % 2
    send, kept = halve_both(first, second, (zs // 2, 2, rows, columns), mine, order)
    return Sum(kept, send, "z", 1)


def z_bits():
    bits = []
    while 1 << len(bits) < lax.axis_size("z"):
        bits.append(1 << len(bits))
    return bits


def right_of(ref):
    if len(ref.shape) == 2:
        return ref[...]
    return jnp.concatenate([heads_of(ref, at, at + DH) for at in range(0, ref.shape[2], DH)], axis=1)


def row_grad_kernel(pairs, rows, core_ref, *refs):
    send_ref, keep_ref = refs[-2:]
    at = 0
    for i in range(pairs):
        whole = dot_tn(refs[2 * i][...], right_of(refs[2 * i + 1])).astype(BF)
        columns = whole.shape[1]
        parts = [whole[k * rows : (k + 1) * rows] for k in range(whole.shape[0] // rows)]
        even = jnp.concatenate(parts[0::2], axis=0)
        odd = jnp.concatenate(parts[1::2], axis=0)
        first = core_ref[0] == 0
        keep_ref[:, at : at + columns] = jnp.where(first, even, odd)
        send_ref[:, at : at + columns] = jnp.where(first, odd, even)
        at += columns


def row_grad(core, pairs, order=()):
    frames, width = pairs[0][0].shape
    zs = lax.axis_size("z")
    rows = width // (8 * zs)
    columns = sum(right.size // frames for _, right in pairs)
    if rows % 16:
        whole = jnp.concatenate(
            [dot_tn(left, right_of(right)).astype(BF) for left, right in pairs], axis=1
        )
        whole = whole.reshape(4 * zs, 2, rows, columns)
        flat = lambda v: v.reshape(width // 2, columns)
        return flat(pick(whole, 1 - core[0], 1)), flat(pick(whole, core[0], 1))
    tile = 256
    specs, args = [], []
    for left, right in pairs:
        specs += [
            pl.BlockSpec((frames, tile), lambda i, c: (0, i)),
            pl.BlockSpec(right.shape, lambda i, c, n=right.ndim: (0,) * n),
        ]
        args += [left, right]
    specs += [pl.BlockSpec(memory_space=pl.ANY)] * len(order)
    out = pl.BlockSpec((tile // 2, columns), lambda i, c: (i, 0))
    return pl.pallas_call(
        functools.partial(row_grad_kernel, len(pairs), rows),
        grid_spec=pltpu.PrefetchScalarGridSpec(
            num_scalar_prefetch=1, grid=(width // tile,), in_specs=specs, out_specs=[out, out]
        ),
        out_shape=[jax.ShapeDtypeStruct((width // 2, columns), BF)] * 2,
        compiler_params=pltpu.CompilerParams(vmem_limit_bytes=VMEM_BYTES),
        cost_estimate=takes(10),
        name="row_grad",
    )(core, *args, *order)


def body(
    block_in,
    out_grad,
    utt_ends,
    valid_ends,
    ffn1_in,
    ffn1_out,
    att_qkv,
    att_out,
    content_bias,
    conv_in,
    conv_out,
    ffn2_in,
    ffn2_out,
    conv_depth,
    norm_gain,
    norm_bias,
):
    zs = lax.axis_size("z")
    devices = 8 * zs
    frames, width = block_in.shape
    heads = width // DH
    z, x, y, c = (lax.axis_index(axis) for axis in DEV)
    place = ((z * 2 + x) * 2 + y) * 2 + c
    head = (x * 2 + y) * 2 + c

    small = jnp.concatenate([norm_gain, norm_bias, conv_depth, content_bias[None]], axis=0)
    small = jnp.broadcast_to(small[None], (devices,) + small.shape)
    small = lax.all_to_all(small, DEV, split_axis=0, concat_axis=0, tiled=True)
    small = small.transpose(1, 0, 2).reshape(small.shape[1], width).astype(F32)
    gains, shifts, taps, q_bias = small[:6], small[6:12], small[12 : 12 + KSIZE], small[12 + KSIZE]

    rows, few = ffn1_in.shape[0], att_qkv.shape[0]
    blocks = lambda w: [w[:, i : i + width] for i in range(0, w.shape[1], width)]

    def gather(*parts):
        mine = jnp.concatenate(parts, axis=0)
        return lax.all_gather(mine, DEV, axis=0, tiled=True).reshape(devices, -1, width)

    w_first = gather(pack_ffn(ffn1_in, ffn1_out), *blocks(att_qkv))
    w_mid = gather(att_out, *blocks(conv_in), conv_out)
    w_second = gather(pack_ffn(ffn2_in, ffn2_out, order=(small,)))
    w_proj = Rows(w_first, 2 * rows, few)
    w_conv = Rows(w_mid, 0, few)
    w_cout = Rows(w_mid, 3 * few, few)
    core = c.astype(jnp.int32)[None]

    all_frames = frames * devices
    first_frame = place * frames
    span = 4 * frames
    group = 8 * frames
    origin = span
    group_first = z * group
    starts = jnp.concatenate([jnp.zeros((1,), jnp.int32), utt_ends[:-1]])
    valid_count = jnp.sum((valid_ends - starts).astype(F32))

    def segments(positions):
        seg = jnp.sum((utt_ends[None, :] <= positions[:, None]).astype(jnp.int32), axis=1)
        valid_seg = jnp.sum((valid_ends[None, :] <= positions[:, None]).astype(jnp.int32), axis=1)
        valid = seg == valid_seg
        return jnp.where(positions < 0, -1, jnp.where(positions >= all_frames, -2, seg)), valid

    ext_seg, ext_valid = segments(
        first_frame - REACH + jnp.arange(frames + 2 * REACH, dtype=jnp.int32)
    )
    own_seg = ext_seg[REACH : REACH + frames]
    ext_valid = ext_valid.astype(F32)
    edge_valid = jnp.concatenate([ext_valid[:REACH], ext_valid[-REACH:]])
    edge_valid = jnp.concatenate([edge_valid, jnp.zeros((frames - 2 * REACH,), F32)])
    columns = jnp.stack(
        [(ext_seg[m : m + frames] == own_seg).astype(F32) for m in range(KSIZE)]
        + [ext_valid[REACH : REACH + frames], edge_valid, jnp.zeros((frames,), F32)],
        axis=1,
    )
    group_pos = group_first + jnp.arange(group, dtype=jnp.int32)
    ended = utt_ends[None, :] <= group_pos[:, None]
    group_seg = jnp.sum(ended.astype(jnp.int32), axis=1)
    group_lo = jnp.max(jnp.where(ended, utt_ends[None, :], 0), axis=1)
    slots = jnp.arange(utt_ends.shape[0], dtype=jnp.int32)
    group_hi = jnp.sum(
        jnp.where(group_seg[:, None] == slots[None, :], valid_ends[None, :], 0), axis=1
    )
    window_first = group_first - origin
    lo_q = group_lo - window_first
    hi_q = group_hi - window_first
    low = (lo_q[::BQ] // 128) * 128
    high = hi_q[BQ - 1 :: BQ]
    lo_q = lo_q.astype(F32)[None, :]
    hi_q = hi_q.astype(F32)[None, :]
    c2 = (32.0 * jnp.exp2(-head.astype(F32)) * (LOG2E / span))[None]

    def vectors(*rows):
        rows = jnp.stack(rows)
        return jnp.concatenate([rows, jnp.zeros((-len(rows) % 8, width), F32)], axis=0)

    count_row = jnp.broadcast_to(valid_count, (width,))

    x1, n2, pack1, s1, d1, q_heads, k_heads, v_heads = first_call(
        core,
        block_in,
        w_first,
        rows,
        w_proj,
        vectors(gains[0], shifts[0], gains[1], shifts[1], q_bias),
    )
    pack1_sib = xor_send(pack1, "c", 1)

    def to_heads(cells):
        got = lax.all_to_all(cells, LAYER, split_axis=0, concat_axis=0, tiled=True)
        return got.reshape(group, cells.shape[2])

    def to_frames(cells):
        cells = cells.reshape(heads, frames, cells.shape[1])
        return lax.all_to_all(cells, LAYER, split_axis=0, concat_axis=0, tiled=True)

    up = [(i, i + 1) for i in range(zs - 1)]
    down = [(i + 1, i) for i in range(zs - 1)]

    def with_edges(cells):
        return lax.ppermute(cells[-span:], "z", up), cells, lax.ppermute(cells[:span], "z", down)

    kv = with_edges(to_heads(k_heads)) + with_edges(to_heads(v_heads))
    q_own = to_heads(q_heads)
    o_own, lse = attn_fwd(q_own, kv, low, high, c2, lo_q, hi_q, origin)
    mixed, x2, n3, lin, sig, gated = gate_call(
        to_frames(o_own), x1, w_conv, vectors(gains[2], shifts[2]), columns, (pack1_sib,)
    )
    g_edges = neighbour_rows(gated)
    tap_rows = [taps[m] for m in range(KSIZE)]
    conv, moments = conv_call(gated, *g_edges, vectors(*tap_rows), columns, devices)
    spread = lambda cells: lax.all_to_all(cells, DEV, split_axis=0, concat_axis=0, tiled=True)
    moments = spread(moments)

    final_out, swished, dx3, ew, dz, sums_c, totals, pack2, s2, da2 = second_call(
        core,
        x2,
        conv,
        moments,
        w_cout,
        w_second,
        rows,
        vectors(gains[3], shifts[3], gains[4], shifts[4], gains[5], shifts[5], count_row),
        out_grad,
    )
    totals = spread(totals)
    edges = neighbour_rows(jnp.concatenate([dz[-REACH:], conv[-REACH:]]), jnp.concatenate([dz[:REACH], conv[:REACH]]))
    pack2_sib = xor_send(pack2, "c", 1)
    hidden = pack2.shape[2]
    f2i = slab_sum((pack2, pack2_sib, 0), (da2, pack2_sib, 4), "x")
    f2o = slab_sum((pack2, pack2_sib, 3), (s2, pack2_sib, 1), "y")

    point_grad, dx2, ey, mixed_grad, sums_b = back_call(
        dz,
        conv,
        edges,
        gated,
        g_edges,
        moments,
        totals,
        lin,
        sig,
        x2,
        dx3,
        w_conv,
        vectors(*tap_rows, gains[3], gains[2], gains[2], count_row),
        columns,
        order=(f2i.send, f2o.send),
    )
    do_own = to_heads(mixed_grad)
    send, kept = row_grad(core, [(mixed, ey), (n3, point_grad), (swished, ew)])
    mid = Sum(kept, send, "c", 1)
    dq, dkv_prev, dkv, dkv_next = attn_bwd(
        q_own,
        o_own,
        do_own,
        lse,
        kv,
        low,
        high,
        c2,
        lo_q,
        hi_q,
        origin,
        order=(f2i.kept, f2o.kept, kept),
    )
    dq = to_frames(dq)
    f2i = slab_second(f2i, "x")
    f2o = slab_second(f2o, "y", order=(f2i.send,))
    dkv = join_edges(
        dkv,
        lax.ppermute(dkv_next, "z", up),
        lax.ppermute(dkv_prev, "z", down),
        order=(f2i.send, f2o.send),
    )
    dkv = to_frames(dkv)

    low_z, high_z = z_bits()[:1], z_bits()[1:]
    dx1, ef1, sums_p = proj_back_call(dq, dkv, dx2, x1, w_proj, vectors(gains[0], gains[1]), ())
    ef1_sib = xor_send(ef1, "c", 1)
    send, kept = row_grad(core, [(n2, dq), (n2, dkv)], order=(ef1,))
    qkv = Sum(kept, send, "c", 1)
    f1o_left, f1o_right = (ef1, ef1_sib, 0), (s1, pack1_sib, 1)
    f1o_away = slab_grad(f1o_left, f1o_right, None, 1 - y, (qkv.send,))
    mid = mid.step((zs, 2, 2 * few, 4 * width), "x", order=(f1o_away,))
    f2 = z_both(f2i, f2o, rows, hidden, order=(mid.send,))
    grad_input, sums_a, da_first, da_second, da1 = last_call(
        core,
        dx1,
        ef1,
        block_in,
        w_first,
        rows,
        d1,
        vectors(gains[0]),
        order=(f2.send,),
    )
    da_sib = (xor_send(da_first, "c", 1), xor_send(da_second, "c", 1))
    f2 = z_steps(f2, 2 * rows, hidden, high_z, order=(da1,))
    f1o = Sum(slab_grad(f1o_left, f1o_right, None, y, (f2.send,), 10), f1o_away, "y", 1)
    f1i = slab_sum((pack1, pack1_sib, 0), (da1, da_sib, 0), "x", order=(f1o.kept,))
    grad_f2i, grad_f2o = finish_both(f2, rows, hidden, order=(f1i.kept,))
    qkv = z_steps(qkv, 4 * few, 3 * width, low_z, order=(grad_f2i,))
    f1o = slab_second(f1o, "y", order=(qkv.send,))
    mid = mid.step((zs, 2, few, 4 * width), "y", order=(f1o.send,))
    qkv = qkv.step((zs // 2, 2, 2 * few, 3 * width), "x", order=(mid.send,))
    mid = z_steps(mid, few, 4 * width, low_z, order=(qkv.send,))
    f1i = slab_second(f1i, "x", order=(mid.send,))
    f1o = z_steps(f1o, rows, hidden, low_z, order=(f1i.send,))
    mid = z_steps(mid, few, 4 * width, high_z, order=(f1o.send,))
    f1o = z_steps(f1o, rows, hidden, high_z, order=(mid.send,))
    mid = mid.finish((few, 4 * width), order=(f1o.send,))
    out_att, out_cin, out_cout = mid[:, :width], mid[:, width : 3 * width], mid[:, 3 * width :]
    qkv = qkv.step((zs // 2, 2, few, 3 * width), "y", order=(mid,))
    f1i = z_steps(f1i, rows, hidden, low_z, order=(qkv.send,))
    f1i = z_steps(f1i, rows, hidden, high_z, order=(f1i.send,))
    a, b, c, p = 0, 1, 2, 3
    places = [(a, 0), (p, 0), (b, 0), (c, 4), (c, 2), (c, 0)]
    places += [(a, 1), (p, 1), (b, 1), (c, 5), (c, 3), (c, 1)]
    places += [(b, 2 + m) for m in range(KSIZE)] + [(p, 2)]
    sums = stack_rows([sums_a, sums_b, sums_c, sums_p], places, devices, order=(f1i.send,))
    qkv = z_steps(qkv, few, 3 * width, high_z, order=(sums,))
    grad_f1o = f1o.finish((rows, hidden), True, order=(qkv.send,))
    grad_f1i = f1i.finish((rows, hidden), order=(grad_f1o,))
    out_qkv = qkv.finish((few, 3 * width), order=(grad_f1i,))
    sums = lax.all_to_all(sums, DEV, split_axis=0, concat_axis=0, tiled=True)
    gain_sums, bias_sums, tap_sums, query_sums = total_of(
        sums, (6, 6, KSIZE, 1), order=(out_qkv,)
    )

    return (
        final_out,
        grad_input,
        grad_f1i,
        grad_f1o,
        out_qkv,
        out_att,
        query_sums[0],
        out_cin,
        out_cout,
        grad_f2i,
        grad_f2o,
        tap_sums,
        gain_sums,
        bias_sums,
    )


def solution(mesh):
    seq, heads = mesh.shape["seq"], mesh.shape["head"]
    grid = Mesh(mesh.devices.reshape(seq // 2, 2, heads // 2, 2), DEV)
    both = P(DEV, None)
    inward = P(("z", "x"), ("y", "c"))
    outward = P(("y", "c"), ("z", "x"))
    columns = P(None, DEV)
    return jax.shard_map(
        body,
        mesh=grid,
        in_specs=(
            both,
            both,
            P(),
            P(),
            inward,
            outward,
            both,
            both,
            P(DEV),
            both,
            both,
            inward,
            outward,
            columns,
            columns,
            columns,
        ),
        out_specs=(
            both,
            both,
            inward,
            outward,
            both,
            both,
            P(DEV),
            both,
            both,
            inward,
            outward,
            columns,
            columns,
            columns,
        ),
        check_vma=False,
    )
```

```python
import functools
import math

import jax
import jax.numpy as jnp
from jax import lax
from jax.experimental import pallas as pl
from jax.experimental.pallas import tpu as pltpu
from jax.sharding import Mesh
from jax.sharding import PartitionSpec as P

DH = 128
KSIZE = 5
REACH = (KSIZE - 1) // 2
EPSILON = 1e-05
MASKED = -1e30
LOG2E = math.log2(math.e)
DEV = ("z", "x", "y", "c")
LAYER = ("x", "y", "c")
BQ = 512
BK = 512
BF = jnp.bfloat16
F32 = jnp.float32
VMEM_BYTES = 56 * 1024 * 1024


def takes(microseconds):
    return pl.CostEstimate(
        flops=1024, bytes_accessed=1024 + int(microseconds * 3.7e6), transcendentals=0
    )


def pick(cells, index, dim):
    return lax.dynamic_index_in_dim(cells, index, dim, keepdims=False)


def xor_send(cells, axis, bit):
    count = lax.axis_size(axis)
    return lax.ppermute(cells, axis, [(i, i ^ bit) for i in range(count)])


def neighbour_rows(tail, head=None):
    if head is None:
        tail, head = tail[-REACH:], tail[:REACH]
    count = 1
    for axis in DEV:
        count *= lax.axis_size(axis)
    before = lax.ppermute(tail, DEV, [(i, i + 1) for i in range(count - 1)])
    after = lax.ppermute(head, DEV, [(i + 1, i) for i in range(count - 1)])
    return before, after


def dot_nn(a, b):
    return lax.dot_general(a, b, (((1,), (0,)), ((), ())), preferred_element_type=F32)


def dot_nt(a, b):
    return lax.dot_general(a, b, (((1,), (1,)), ((), ())), preferred_element_type=F32)


def dot_tn(a, b):
    return lax.dot_general(a, b, (((0,), (0,)), ((), ())), preferred_element_type=F32)


def norm_stats(values):
    centred = values - jnp.mean(values, axis=-1, keepdims=True)
    inv_std = lax.rsqrt(jnp.mean(centred * centred, axis=-1, keepdims=True) + EPSILON)
    return centred * inv_std, inv_std


def norm_back(upstream, normed, inv_std, gain):
    scaled = upstream * gain
    inner = (
        scaled
        - jnp.mean(scaled, axis=-1, keepdims=True)
        - normed * jnp.mean(scaled * normed, axis=-1, keepdims=True)
    )
    return inv_std * inner


def pack_kernel(extra, in_ref, out_ref, *refs):
    rows = in_ref.shape[0]
    refs[extra][:rows] = in_ref[...]
    refs[extra][rows:] = out_ref[...].T


def pack_ffn(w_in, w_out, order=()):
    rows, width = w_in.shape
    whole = lambda v: pl.BlockSpec(v.shape, lambda: (0, 0))
    if rows % 128:
        return jnp.concatenate([w_in, w_out.T], axis=0)
    return pl.pallas_call(
        functools.partial(pack_kernel, len(order)),
        in_specs=[whole(w_in), whole(w_out)] + [pl.BlockSpec(memory_space=pl.ANY)] * len(order),
        out_specs=pl.BlockSpec((2 * rows, width), lambda: (0, 0)),
        out_shape=jax.ShapeDtypeStruct((2 * rows, width), BF),
        name="pack_ffn",
    )(w_in, w_out, *order)


class Rows:
    def __init__(self, gathered, first, count):
        self.stepped = count % 16 == 0 and first % count == 0
        devices, _, width = gathered.shape
        self.count = count
        if self.stepped:
            self.at = first // count
            self.array = gathered
            self.block = (devices, count, width)
        else:
            self.first = first
            self.gathered = gathered
            self.width = width

    def blocks(self, pick_block, total):
        if self.stepped:
            at = self.at
            return self.array, pl.BlockSpec(self.block, lambda j, *_: (0, at + pick_block(j), 0))
        cut = [
            self.gathered[:, self.first + i * self.count : self.first + (i + 1) * self.count]
            for i in range(total)
        ]
        cut = jnp.stack([v.reshape(-1, self.width) for v in cut])
        return cut, pl.BlockSpec((1,) + cut.shape[1:], lambda j, *_: (pick_block(j), 0, 0))


def square(ref):
    return ref[...].reshape(-1, ref.shape[-1])


def slab_of(step, core):
    return (step % 2) * 2 + jnp.where(step < 2, 1 - core, core)


def slab_specs(gathered, rows, step_of):
    devices, total, width = gathered.shape
    array = gathered.reshape(devices // 4, 4, total, width)
    block = (devices // 4, 1, rows, width)
    specs = [
        pl.BlockSpec(block, lambda j, c, i=i: (0, slab_of(step_of(j), c[0]), i, 0)) for i in (0, 1)
    ]
    return [array, array], specs


def heads_of(ref, lo, hi):
    return jnp.concatenate([ref[h, :, lo:hi] for h in range(ref.shape[0])], axis=1)


def forward_slab(n, w1_ref, w2_ref, s_ref, d_out):
    width = n.shape[1]
    w1 = square(w1_ref)
    chunk = 256
    for at in range(0, width, chunk):
        a = dot_nn(n, w1[:, at : at + chunk])
        sig = jax.nn.sigmoid(a)
        s_ref[:, at : at + chunk] = (a * sig).astype(BF)
        d_out[:, at : at + chunk] = (sig * (1.0 + a * (1.0 - sig))).astype(BF)
    return dot_nt(s_ref[...], square(w2_ref))


def backward_slab(ef, w1_ref, w2_ref, d_in, da_ref):
    width = ef.shape[1]
    w2 = square(w2_ref)
    chunk = 256
    for at in range(0, width, chunk):
        ds = dot_nn(ef, w2[:, at : at + chunk])
        da_ref[:, at : at + chunk] = (ds * d_in[:, at : at + chunk].astype(F32)).astype(BF)
    return dot_nt(da_ref[...], square(w1_ref))


def keep_slab(step, cells, pack_ref, pack_at, own_ref):
    @pl.when(step < 2)
    def _():
        pack_ref[pack_at + step] = cells

    @pl.when(step >= 2)
    def _():
        own_ref[0] = cells


def first_kernel(
    core_ref,
    x_ref,
    w1_ref,
    w2_ref,
    wp_ref,
    vec_ref,
    x1_ref,
    n2_ref,
    pack_ref,
    own_ref,
    d_ref,
    q_ref,
    k_ref,
    v_ref,
    acc_ref,
    s_ref,
):
    step = pl.program_id(0)

    @pl.when(step == 0)
    def _():
        normed, _ = norm_stats(x_ref[...].astype(F32))
        pack_ref[0] = (normed * vec_ref[0:1, :] + vec_ref[1:2, :]).astype(BF)
        acc_ref[...] = jnp.zeros_like(acc_ref)

    @pl.when(step < 4)
    def _():
        acc_ref[...] += forward_slab(pack_ref[0], w1_ref, w2_ref, s_ref, d_ref.at[0])
        keep_slab(step, s_ref[...], pack_ref, 1, own_ref)

    @pl.when(step == 3)
    def _():
        x1 = x_ref[...].astype(F32) + 0.5 * acc_ref[...]
        x1_ref[...] = x1
        normed, _ = norm_stats(x1)
        n2_ref[...] = (normed * vec_ref[2:3, :] + vec_ref[3:4, :]).astype(BF)

    for part, ref in enumerate((q_ref, k_ref, v_ref)):

        @pl.when(step == 4 + part)
        def _():
            projected = dot_nn(n2_ref[...], square(wp_ref))
            if part == 0:
                projected = projected + vec_ref[4:5, :]
            projected = projected.astype(BF)
            for h in range(ref.shape[0]):
                ref[h] = projected[:, h * DH : (h + 1) * DH]


def first_call(core, x, gathered, rows, proj, vectors):
    frames, width = x.shape
    heads = width // DH
    fixed = lambda *shape: pl.BlockSpec(shape, lambda j, c: (0,) * len(shape))
    slabs, slab_blocks = slab_specs(gathered, rows, lambda j: jnp.minimum(j, 3))
    proj_array, proj_block = proj.blocks(lambda j: jnp.clip(j - 4, 0, 2), 3)
    return pl.pallas_call(
        first_kernel,
        grid_spec=pltpu.PrefetchScalarGridSpec(
            num_scalar_prefetch=1,
            grid=(7,),
            in_specs=[fixed(frames, width)] + slab_blocks + [proj_block, fixed(*vectors.shape)],
            out_specs=[
                fixed(frames, width),
                fixed(frames, width),
                fixed(3, frames, width),
                pl.BlockSpec((1, frames, width), lambda j, c: (jnp.clip(j - 2, 0, 1), 0, 0)),
                pl.BlockSpec((1, frames, width), lambda j, c: (jnp.minimum(j, 3), 0, 0)),
                fixed(heads, frames, DH),
                fixed(heads, frames, DH),
                fixed(heads, frames, DH),
            ],
            scratch_shapes=[pltpu.VMEM((frames, width), F32), pltpu.VMEM((frames, width), BF)],
        ),
        out_shape=[
            jax.ShapeDtypeStruct((frames, width), F32),
            jax.ShapeDtypeStruct((frames, width), BF),
            jax.ShapeDtypeStruct((3, frames, width), BF),
            jax.ShapeDtypeStruct((2, frames, width), BF),
            jax.ShapeDtypeStruct((4, frames, width), BF),
            jax.ShapeDtypeStruct((heads, frames, DH), BF),
            jax.ShapeDtypeStruct((heads, frames, DH), BF),
            jax.ShapeDtypeStruct((heads, frames, DH), BF),
        ],
        compiler_params=pltpu.CompilerParams(vmem_limit_bytes=VMEM_BYTES),
        cost_estimate=pl.CostEstimate(
            flops=22 * frames * width * width,
            bytes_accessed=22 * width * width + 40 * frames * width,
            transcendentals=4 * frames * width,
        ),
        name="first_part",
    )(core, x, *slabs, proj_array, vectors)


def gate_kernel(extra, mh_ref, x1_ref, w_ref, vec_ref, cols_ref, *refs):
    mixed_ref, x2_ref, n3_ref, lin_ref, sig_ref, g_ref = refs[extra:]
    step = pl.program_id(0)

    @pl.when(step == 0)
    def _():
        mixed = heads_of(mh_ref, 0, DH)
        mixed_ref[...] = mixed
        x2 = x1_ref[...] + dot_nn(mixed, square(w_ref))
        x2_ref[...] = x2
        normed, _ = norm_stats(x2)
        n3_ref[...] = (normed * vec_ref[0:1, :] + vec_ref[1:2, :]).astype(BF)

    @pl.when(step == 1)
    def _():
        lin_ref[...] = dot_nn(n3_ref[...], square(w_ref))

    @pl.when(step == 2)
    def _():
        sig = jax.nn.sigmoid(dot_nn(n3_ref[...], square(w_ref)))
        sig_ref[...] = sig
        g_ref[...] = (lin_ref[...] * sig * cols_ref[:, KSIZE : KSIZE + 1]).astype(BF)


def gate_call(mixed_heads, x1, weights, vectors, columns, order=()):
    frames, width = x1.shape
    fixed = lambda *shape: pl.BlockSpec(shape, lambda j: (0,) * len(shape))
    array, block = weights.blocks(lambda j: j, 3)
    return pl.pallas_call(
        functools.partial(gate_kernel, len(order)),
        grid=(3,),
        in_specs=[
            fixed(*mixed_heads.shape),
            fixed(frames, width),
            block,
            fixed(*vectors.shape),
            fixed(*columns.shape),
        ]
        + [pl.BlockSpec(memory_space=pl.ANY)] * len(order),
        out_specs=[fixed(frames, width)] * 6,
        out_shape=[jax.ShapeDtypeStruct((frames, width), t) for t in (BF, F32, BF, F32, F32, BF)],
        compiler_params=pltpu.CompilerParams(vmem_limit_bytes=VMEM_BYTES),
        cost_estimate=pl.CostEstimate(
            flops=6 * frames * width * width,
            bytes_accessed=6 * width * width + 24 * frames * width,
            transcendentals=frames * width,
        ),
        name="attention_out_and_gate",
    )(mixed_heads, x1, array, vectors, columns, *order)


PAD = 8


def lay_out(scratch, before, cells, after):
    frames = cells.shape[0]
    scratch[PAD - REACH : PAD, :] = before
    scratch[PAD : PAD + frames, :] = cells
    scratch[PAD + frames : PAD + frames + REACH, :] = after


def conv_kernel(g_ref, before_ref, after_ref, vec_ref, cols_ref, conv_ref, sums_ref, ext):
    frames = g_ref.shape[0]
    lay_out(
        ext, before_ref[...].astype(F32), g_ref[...].astype(F32), after_ref[...].astype(F32)
    )
    conv = jnp.zeros(g_ref.shape, F32)
    for m in range(KSIZE):
        rows = ext[PAD - REACH + m : PAD - REACH + m + frames, :]
        conv = conv + vec_ref[m : m + 1, :] * rows * cols_ref[:, m : m + 1]
    conv_ref[...] = conv
    counted = conv * cols_ref[:, KSIZE : KSIZE + 1]
    sums = jnp.concatenate(
        [jnp.sum(counted, axis=0, keepdims=True), jnp.sum(counted * conv, axis=0, keepdims=True)]
    )
    sums_ref[...] = jnp.broadcast_to(sums[None], sums_ref.shape)


def conv_call(g, before, after, taps, columns, devices):
    frames, width = g.shape
    return pl.pallas_call(
        conv_kernel,
        out_shape=[
            jax.ShapeDtypeStruct((frames, width), F32),
            jax.ShapeDtypeStruct((devices, 2, width), F32),
        ],
        scratch_shapes=[pltpu.VMEM((frames + 2 * PAD, width), F32)],
        compiler_params=pltpu.CompilerParams(vmem_limit_bytes=VMEM_BYTES),
        cost_estimate=pl.CostEstimate(
            flops=20 * frames * width, bytes_accessed=8 * frames * width, transcendentals=0
        ),
        name="depthwise",
    )(g, before, after, taps, columns)


def batch_stats(moments_ref, count):
    sums = jnp.sum(moments_ref[...], axis=0)
    mean = sums[0:1, :] / count
    return mean, lax.rsqrt(sums[1:2, :] / count - mean * mean + EPSILON)


def second_kernel(
    core_ref,
    x2_ref,
    conv_ref,
    mom_ref,
    wc_ref,
    w1_ref,
    w2_ref,
    vec_ref,
    og_ref,
    out_ref,
    swish_ref,
    dx_ref,
    ew_ref,
    dz_ref,
    sums_ref,
    spread_ref,
    pack_ref,
    s_own_ref,
    da_own_ref,
    x3_ref,
    acc_ref,
    d_ref,
    dsilu_ref,
    s_ref,
    dx4_ref,
):
    step = pl.program_id(0)
    count = vec_ref[6:7, :]

    @pl.when(step == 0)
    def _():
        mean, inv = batch_stats(mom_ref, count)
        z = (conv_ref[...] - mean) * inv * vec_ref[0:1, :] + vec_ref[1:2, :]
        sig = jax.nn.sigmoid(z)
        swish = (z * sig).astype(BF)
        swish_ref[...] = swish
        dsilu_ref[...] = sig * (1.0 + z * (1.0 - sig))
        x3 = x2_ref[...] + dot_nn(swish, square(wc_ref))
        x3_ref[...] = x3
        normed, _ = norm_stats(x3)
        pack_ref[0] = (normed * vec_ref[2:3, :] + vec_ref[3:4, :]).astype(BF)
        acc_ref[...] = jnp.zeros_like(acc_ref)

    @pl.when(step < 4)
    def _():
        acc_ref[...] += forward_slab(pack_ref[0], w1_ref, w2_ref, s_ref, d_ref.at[step])
        keep_slab(step, s_ref[...], pack_ref, 1, s_own_ref)

    @pl.when(step == 3)
    def _():
        normed, inv_std = norm_stats(x3_ref[...] + 0.5 * acc_ref[...])
        gain = vec_ref[4:5, :]
        out_ref[...] = (normed * gain + vec_ref[5:6, :]).astype(BF)
        upstream = og_ref[...].astype(F32)
        dx4 = norm_back(upstream, normed, inv_std, gain)
        dx4_ref[...] = dx4
        pack_ref[3] = (0.5 * dx4).astype(BF)
        sums_ref[0:1, :] = jnp.sum(upstream * normed, axis=0, keepdims=True)
        sums_ref[1:2, :] = jnp.sum(upstream, axis=0, keepdims=True)
        acc_ref[...] = jnp.zeros_like(acc_ref)

    @pl.when(step >= 4)
    def _():
        acc_ref[...] += backward_slab(pack_ref[3], w1_ref, w2_ref, d_ref.at[step - 4], s_ref)
        keep_slab(step - 4, s_ref[...], pack_ref, 4, da_own_ref)

    @pl.when(step == 7)
    def _():
        normed, inv_std = norm_stats(x3_ref[...])
        dn = acc_ref[...]
        dx3 = dx4_ref[...] + norm_back(dn, normed, inv_std, vec_ref[2:3, :])
        dx_ref[...] = dx3
        sums_ref[2:3, :] = jnp.sum(dn * normed, axis=0, keepdims=True)
        sums_ref[3:4, :] = jnp.sum(dn, axis=0, keepdims=True)
        ew = dx3.astype(BF)
        ew_ref[...] = ew
        dz = dot_nt(ew, square(wc_ref)) * dsilu_ref[...]
        dz_ref[...] = dz
        mean, inv = batch_stats(mom_ref, count)
        zhat = (conv_ref[...] - mean) * inv
        totals = jnp.concatenate(
            [jnp.sum(dz * zhat, axis=0, keepdims=True), jnp.sum(dz, axis=0, keepdims=True)]
        )
        sums_ref[4:6, :] = totals
        sums_ref[6:8, :] = jnp.zeros((2, dz.shape[1]), F32)
        spread_ref[...] = jnp.broadcast_to(totals[None], spread_ref.shape)


def second_call(core, x2, conv, moments, weights, gathered, rows, vectors, out_grad):
    frames, width = x2.shape
    fixed = lambda *shape: pl.BlockSpec(shape, lambda j, c: (0,) * len(shape))
    slabs, slab_blocks = slab_specs(gathered, rows, lambda j: j % 4)
    array, block = weights.blocks(lambda j: 0, 1)
    whole = fixed(frames, width)
    return pl.pallas_call(
        second_kernel,
        grid_spec=pltpu.PrefetchScalarGridSpec(
            num_scalar_prefetch=1,
            grid=(8,),
            in_specs=[whole, whole, fixed(*moments.shape), block]
            + slab_blocks
            + [fixed(*vectors.shape), whole],
            out_specs=[
                whole,
                whole,
                whole,
                whole,
                whole,
                fixed(8, width),
                fixed(*moments.shape),
                fixed(6, frames, width),
                pl.BlockSpec((1, frames, width), lambda j, c: (jnp.clip(j - 2, 0, 1), 0, 0)),
                pl.BlockSpec((1, frames, width), lambda j, c: (jnp.clip(j - 6, 0, 1), 0, 0)),
            ],
            scratch_shapes=[
                pltpu.VMEM((frames, width), F32),
                pltpu.VMEM((frames, width), F32),
                pltpu.VMEM((4, frames, width), BF),
                pltpu.VMEM((frames, width), F32),
                pltpu.VMEM((frames, width), BF),
                pltpu.VMEM((frames, width), F32),
            ],
        ),
        out_shape=[
            jax.ShapeDtypeStruct((frames, width), BF),
            jax.ShapeDtypeStruct((frames, width), BF),
            jax.ShapeDtypeStruct((frames, width), F32),
            jax.ShapeDtypeStruct((frames, width), BF),
            jax.ShapeDtypeStruct((frames, width), F32),
            jax.ShapeDtypeStruct((8, width), F32),
            jax.ShapeDtypeStruct(moments.shape, F32),
            jax.ShapeDtypeStruct((6, frames, width), BF),
            jax.ShapeDtypeStruct((2, frames, width), BF),
            jax.ShapeDtypeStruct((2, frames, width), BF),
        ],
        compiler_params=pltpu.CompilerParams(vmem_limit_bytes=VMEM_BYTES),
        cost_estimate=pl.CostEstimate(
            flops=36 * frames * width * width,
            bytes_accessed=34 * width * width + 40 * frames * width,
            transcendentals=5 * frames * width,
        ),
        name="second_part",
    )(core, x2, conv, moments, array, *slabs, vectors, out_grad)


def back_kernel(
    extra,
    dz_ref,
    conv_ref,
    edge_before_ref,
    edge_after_ref,
    g_ref,
    g_before_ref,
    g_after_ref,
    mom_ref,
    tot_ref,
    lin_ref,
    sig_ref,
    x2_ref,
    dx3_ref,
    w_ref,
    vec_ref,
    cols_ref,
    *refs,
):
    pg_ref, dx2_ref, ey_ref, do_ref, sums_ref, ext, g_ext, acc_ref, b_ref = refs[extra:]
    step = pl.program_id(0)
    frames, width = dz_ref.shape

    @pl.when(step == 0)
    def _():
        count = vec_ref[8:9, :]
        gain = vec_ref[5:6, :]
        mean, inv = batch_stats(mom_ref, count)
        totals = jnp.sum(tot_ref[...], axis=0) * gain

        def conv_grad(dz, conv, valid):
            zhat = (conv - mean) * inv
            dc = inv * (dz * gain - valid * (totals[1:2, :] + zhat * totals[0:1, :]) / count)
            return dc.astype(BF).astype(F32)

        valid = cols_ref[:, KSIZE : KSIZE + 1]
        dc = conv_grad(dz_ref[...], conv_ref[...], valid)
        edges = []
        for at, ref in ((0, edge_before_ref), (REACH, edge_after_ref)):
            edges.append(
                conv_grad(
                    ref[0:REACH, :],
                    ref[REACH : 2 * REACH, :],
                    cols_ref[at : at + REACH, KSIZE + 1 : KSIZE + 2],
                )
            )
        lay_out(ext, edges[0], dc, edges[1])
        lay_out(
            g_ext,
            g_before_ref[...].astype(F32),
            g_ref[...].astype(F32),
            g_after_ref[...].astype(F32),
        )
        dg = jnp.zeros((frames, width), F32)
        for m in range(KSIZE):
            back = 2 * REACH - m
            rows = ext[PAD - REACH + back : PAD - REACH + back + frames, :]
            dg = dg + vec_ref[m : m + 1, :] * rows * cols_ref[:, back : back + 1]
            there = g_ext[PAD - REACH + m : PAD - REACH + m + frames, :]
            sums_ref[2 + m : 3 + m, :] = jnp.sum(
                dc * there * cols_ref[:, m : m + 1], axis=0, keepdims=True
            )
        sums_ref[7:8, :] = jnp.zeros((1, width), F32)
        de = dg * valid
        sig = sig_ref[...]
        pa = (de * sig).astype(BF)
        pb = (de * lin_ref[...] * sig * (1.0 - sig)).astype(BF)
        pg_ref[:, :width] = pa
        pg_ref[:, width:] = pb
        b_ref[...] = pb
        acc_ref[...] = dot_nt(pa, square(w_ref))

    @pl.when(step == 1)
    def _():
        dn = acc_ref[...] + dot_nt(b_ref[...], square(w_ref))
        normed, inv_std = norm_stats(x2_ref[...])
        dx2 = dx3_ref[...] + norm_back(dn, normed, inv_std, vec_ref[6:7, :])
        dx2_ref[...] = dx2
        ey_ref[...] = dx2.astype(BF)
        sums_ref[0:1, :] = jnp.sum(dn * normed, axis=0, keepdims=True)
        sums_ref[1:2, :] = jnp.sum(dn, axis=0, keepdims=True)

    @pl.when(step == 2)
    def _():
        grads = dot_nt(ey_ref[...], square(w_ref)).astype(BF)
        for h in range(do_ref.shape[0]):
            do_ref[h] = grads[:, h * DH : (h + 1) * DH]


def back_call(dz, conv, edges, g, g_edges, moments, totals, lin, sig, x2, dx3, weights, vectors, columns, order):
    frames, width = dz.shape
    fixed = lambda *shape: pl.BlockSpec(shape, lambda j: (0,) * len(shape))
    array, block = weights.blocks(lambda j: (j + 1) % 3, 3)
    whole = fixed(frames, width)
    return pl.pallas_call(
        functools.partial(back_kernel, len(order)),
        grid=(3,),
        in_specs=[
            whole,
            whole,
            fixed(2 * REACH, width),
            fixed(2 * REACH, width),
            whole,
            fixed(REACH, width),
            fixed(REACH, width),
            fixed(*moments.shape),
            fixed(*totals.shape),
            whole,
            whole,
            whole,
            whole,
            block,
            fixed(*vectors.shape),
            fixed(*columns.shape),
        ]
        + [pl.BlockSpec(memory_space=pl.ANY)] * len(order),
        out_specs=[
            fixed(frames, 2 * width),
            whole,
            whole,
            fixed(width // DH, frames, DH),
            fixed(8, width),
        ],
        out_shape=[
            jax.ShapeDtypeStruct((frames, 2 * width), BF),
            jax.ShapeDtypeStruct((frames, width), F32),
            jax.ShapeDtypeStruct((frames, width), BF),
            jax.ShapeDtypeStruct((width // DH, frames, DH), BF),
            jax.ShapeDtypeStruct((8, width), F32),
        ],
        scratch_shapes=[
            pltpu.VMEM((frames + 2 * PAD, width), F32),
            pltpu.VMEM((frames + 2 * PAD, width), F32),
            pltpu.VMEM((frames, width), F32),
            pltpu.VMEM((frames, width), BF),
        ],
        compiler_params=pltpu.CompilerParams(vmem_limit_bytes=VMEM_BYTES),
        cost_estimate=pl.CostEstimate(
            flops=6 * frames * width * width,
            bytes_accessed=6 * width * width + 34 * frames * width,
            transcendentals=0,
        ),
        name="convolution_backward",
    )(
        dz,
        conv,
        edges[0],
        edges[1],
        g,
        g_edges[0],
        g_edges[1],
        moments,
        totals,
        lin,
        sig,
        x2,
        dx3,
        array,
        vectors,
        columns,
        *order,
    )


def proj_back_kernel(extra, dq_ref, dkv_ref, dx2_ref, x1_ref, wp_ref, vec_ref, *refs):
    dx1_ref, ef_ref, sums_ref, acc_ref = refs[extra:]
    step = pl.program_id(0)

    @pl.when(step == 0)
    def _():
        dq = heads_of(dq_ref, 0, DH)
        acc_ref[...] = dot_nt(dq, square(wp_ref))
        sums_ref[2:3, :] = jnp.sum(dq.astype(F32), axis=0, keepdims=True)
        sums_ref[3:8, :] = jnp.zeros((5, dq.shape[1]), F32)

    @pl.when(step == 1)
    def _():
        acc_ref[...] += dot_nt(heads_of(dkv_ref, 0, DH), square(wp_ref))

    @pl.when(step == 2)
    def _():
        dn = acc_ref[...] + dot_nt(heads_of(dkv_ref, DH, 2 * DH), square(wp_ref))
        normed, inv_std = norm_stats(x1_ref[...])
        dx1 = dx2_ref[...] + norm_back(dn, normed, inv_std, vec_ref[1:2, :])
        dx1_ref[...] = dx1
        ef_ref[0] = (0.5 * dx1).astype(BF)
        sums_ref[0:1, :] = jnp.sum(dn * normed, axis=0, keepdims=True)
        sums_ref[1:2, :] = jnp.sum(dn, axis=0, keepdims=True)


def proj_back_call(dq, dkv, dx2, x1, proj, vectors, order):
    frames, width = x1.shape
    fixed = lambda *shape: pl.BlockSpec(shape, lambda j: (0,) * len(shape))
    array, block = proj.blocks(lambda j: j, 3)
    whole = fixed(frames, width)
    return pl.pallas_call(
        functools.partial(proj_back_kernel, len(order)),
        grid=(3,),
        in_specs=[fixed(*dq.shape), fixed(*dkv.shape), whole, whole, block, fixed(*vectors.shape)]
        + [pl.BlockSpec(memory_space=pl.ANY)] * len(order),
        out_specs=[whole, fixed(1, frames, width), fixed(8, width)],
        out_shape=[
            jax.ShapeDtypeStruct((frames, width), F32),
            jax.ShapeDtypeStruct((1, frames, width), BF),
            jax.ShapeDtypeStruct((8, width), F32),
        ],
        scratch_shapes=[pltpu.VMEM((frames, width), F32)],
        compiler_params=pltpu.CompilerParams(vmem_limit_bytes=VMEM_BYTES),
        cost_estimate=takes(9),
        name="projections_backward",
    )(dq, dkv, dx2, x1, array, vectors, *order)


def last_kernel(extra, core_ref, dx1_ref, ef_ref, x_ref, w1_ref, w2_ref, d_ref, vec_ref, *refs):
    gin_ref, sums_ref, first_ref, second_ref, own_ref, acc_ref, da_ref = refs[extra:]
    step = pl.program_id(0)

    @pl.when(step == 0)
    def _():
        acc_ref[...] = jnp.zeros_like(acc_ref)

    acc_ref[...] += backward_slab(ef_ref[0], w1_ref, w2_ref, d_ref.at[0], da_ref)
    for at, ref in enumerate((first_ref, second_ref)):

        @pl.when(step == at)
        def _():
            ref[0] = da_ref[...]

    @pl.when(step >= 2)
    def _():
        own_ref[0] = da_ref[...]

    @pl.when(step == 3)
    def _():
        normed, inv_std = norm_stats(x_ref[...].astype(F32))
        dn = acc_ref[...]
        dx = dx1_ref[...] + norm_back(dn, normed, inv_std, vec_ref[0:1, :])
        gin_ref[...] = dx.astype(BF)
        sums_ref[0:1, :] = jnp.sum(dn * normed, axis=0, keepdims=True)
        sums_ref[1:2, :] = jnp.sum(dn, axis=0, keepdims=True)
        sums_ref[2:8, :] = jnp.zeros((6, dn.shape[1]), F32)


def last_call(core, dx1, ef, x, gathered, rows, slope, vectors, order):
    frames, width = x.shape
    fixed = lambda *shape: pl.BlockSpec(shape, lambda j, c: (0,) * len(shape))
    slabs, slab_blocks = slab_specs(gathered, rows, lambda j: j)
    whole = fixed(frames, width)
    return pl.pallas_call(
        functools.partial(last_kernel, len(order)),
        grid_spec=pltpu.PrefetchScalarGridSpec(
            num_scalar_prefetch=1,
            grid=(4,),
            in_specs=[whole, fixed(1, frames, width), whole]
            + slab_blocks
            + [pl.BlockSpec((1, frames, width), lambda j, c: (j, 0, 0)), fixed(*vectors.shape)]
            + [pl.BlockSpec(memory_space=pl.ANY)] * len(order),
            out_specs=[
                whole,
                fixed(8, width),
                fixed(1, frames, width),
                fixed(1, frames, width),
                pl.BlockSpec((1, frames, width), lambda j, c: (jnp.clip(j - 2, 0, 1), 0, 0)),
            ],
            scratch_shapes=[pltpu.VMEM((frames, width), F32), pltpu.VMEM((frames, width), BF)],
        ),
        out_shape=[
            jax.ShapeDtypeStruct((frames, width), BF),
            jax.ShapeDtypeStruct((8, width), F32),
            jax.ShapeDtypeStruct((1, frames, width), BF),
            jax.ShapeDtypeStruct((1, frames, width), BF),
            jax.ShapeDtypeStruct((2, frames, width), BF),
        ],
        compiler_params=pltpu.CompilerParams(vmem_limit_bytes=VMEM_BYTES),
        cost_estimate=takes(15),
        name="last_part",
    )(core, dx1, ef, x, *slabs, slope, vectors, *order)


def fill_window(kv_ref, parts):
    for column, refs in ((0, parts[:3]), (DH, parts[3:])):
        at = 0
        for ref in refs:
            kv_ref[at : at + ref.shape[0], column : column + DH] = ref[...]
            at += ref.shape[0]
    kv_ref[at:, :] = jnp.zeros((kv_ref.shape[0] - at, kv_ref.shape[1]), kv_ref.dtype)


def attn_fwd_kernel(
    origin,
    low_ref,
    high_ref,
    c2_ref,
    q_ref,
    *refs,
):
    lo_ref, hi_ref, o_ref, lse_ref, kv_ref = refs[6:]
    block = pl.program_id(0)

    @pl.when(block == 0)
    def _():
        fill_window(kv_ref, refs[:6])

    rows = q_ref.shape[0]
    q = q_ref[...]
    c1 = LOG2E * DH**-0.5
    c2 = c2_ref[0]
    at = lax.broadcasted_iota(jnp.int32, (1, rows), 1) + (origin + block * rows)
    q_pos = at.astype(F32)
    lo_q, hi_q = lo_ref[...], hi_ref[...]
    first = low_ref[block]
    steps = (high_ref[block] - first + (BK - 1)) // BK

    def step(t, carry):
        top, total, mixed = carry
        start = pl.multiple_of(first + t * BK, 128)
        k = kv_ref[pl.ds(start, BK), :DH]
        v = kv_ref[pl.ds(start, BK), DH:]
        k_pos = (lax.broadcasted_iota(jnp.int32, (BK, 1), 0) + start).astype(F32)
        scores = dot_nt(k, q) * c1 - jnp.abs(k_pos - q_pos) * c2
        scores = jnp.where((k_pos >= lo_q) & (k_pos < hi_q), scores, MASKED)
        new_top = jnp.maximum(top, jnp.max(scores, axis=0, keepdims=True))
        expo = jnp.exp2(scores - new_top)
        keep = jnp.exp2(top - new_top)
        total = total * keep + jnp.sum(expo, axis=0, keepdims=True)
        mixed = mixed * keep + dot_tn(v, expo.astype(BF))
        return new_top, total, mixed

    top, total, mixed = lax.fori_loop(
        0,
        steps,
        step,
        (
            jnp.full((1, rows), MASKED, F32),
            jnp.zeros((1, rows), F32),
            jnp.zeros((DH, rows), F32),
        ),
    )
    o_ref[...] = (mixed / total).T.astype(BF)
    lse_ref[...] = top + jnp.log2(total)


def attn_fwd(q, kv, low, high, c2, lo_q, hi_q, origin):
    frames = q.shape[0]
    window = sum(v.shape[0] for v in kv[:3]) + BK
    parts = [pl.BlockSpec(v.shape, lambda i, *_: (0, 0)) for v in kv]
    blocks = frames // BQ
    pairs = frames * 1024 * DH
    grid_spec = pltpu.PrefetchScalarGridSpec(
        num_scalar_prefetch=3,
        grid=(blocks,),
        in_specs=[
            pl.BlockSpec((BQ, DH), lambda i, *_: (i, 0)),
            *parts,
            pl.BlockSpec((1, BQ), lambda i, *_: (0, i)),
            pl.BlockSpec((1, BQ), lambda i, *_: (0, i)),
        ],
        out_specs=[
            pl.BlockSpec((BQ, DH), lambda i, *_: (i, 0)),
            pl.BlockSpec((1, BQ), lambda i, *_: (0, i)),
        ],
        scratch_shapes=[pltpu.VMEM((window, 2 * DH), BF)],
    )

    def kernel(*refs):
        attn_fwd_kernel(origin, *refs)

    return pl.pallas_call(
        kernel,
        grid_spec=grid_spec,
        out_shape=[
            jax.ShapeDtypeStruct((frames, DH), BF),
            jax.ShapeDtypeStruct((1, frames), F32),
        ],
        compiler_params=pltpu.CompilerParams(vmem_limit_bytes=VMEM_BYTES),
        cost_estimate=pl.CostEstimate(
            flops=4 * pairs, bytes_accessed=4 * window * DH, transcendentals=frames * 1024
        ),
        name="attention_forward",
    )(low, high, c2, q, *kv, lo_q, hi_q)


def attn_bwd_kernel(
    origin,
    extra,
    low_ref,
    high_ref,
    c2_ref,
    q_ref,
    o_ref,
    do_ref,
    lse_ref,
    lo_ref,
    hi_ref,
    *refs,
):
    dq_ref, prev_ref, own_ref, next_ref, dk_acc, dv_acc, kv_ref = refs[6 + extra :]
    block = pl.program_id(0)
    rows = q_ref.shape[0]
    frames = own_ref.shape[0]
    scale = DH**-0.5
    c1 = LOG2E * scale

    @pl.when(block == 0)
    def _():
        fill_window(kv_ref, refs[:6])
        dk_acc[...] = jnp.zeros_like(dk_acc)
        dv_acc[...] = jnp.zeros_like(dv_acc)

    q = q_ref[...]
    do = do_ref[...]
    c2 = c2_ref[0]
    delta = jnp.sum((o_ref[...].astype(F32) * do.astype(F32)).T, axis=0, keepdims=True)
    lse = lse_ref[...]
    at = lax.broadcasted_iota(jnp.int32, (1, rows), 1) + (origin + block * rows)
    q_pos = at.astype(F32)
    lo_q, hi_q = lo_ref[...], hi_ref[...]
    first = low_ref[block]
    steps = (high_ref[block] - first + (BK - 1)) // BK

    def step(t, dq):
        start = pl.multiple_of(first + t * BK, 128)
        here = pl.ds(start, BK)
        k = kv_ref[here, :DH]
        v = kv_ref[here, DH:]
        k_pos = (lax.broadcasted_iota(jnp.int32, (BK, 1), 0) + start).astype(F32)
        scores = dot_nt(k, q) * c1 - jnp.abs(k_pos - q_pos) * c2 - lse
        scores = jnp.where((k_pos >= lo_q) & (k_pos < hi_q), scores, MASKED)
        probs = jnp.exp2(scores)
        grads = (probs * (dot_nt(v, do) - delta)).astype(BF)
        dv_acc[here, :] += dot_nn(probs.astype(BF), do)
        dk_acc[here, :] += dot_nn(grads, q)
        return dq + dot_tn(k, grads)

    dq = lax.fori_loop(0, steps, step, jnp.zeros((DH, rows), F32))
    dq_ref[...] = (dq * scale).T.astype(BF)

    @pl.when(block == pl.num_programs(0) - 1)
    def _():
        prev_ref[:, :DH] = (dk_acc[:origin, :] * scale).astype(BF)
        prev_ref[:, DH:] = dv_acc[:origin, :].astype(BF)
        own_ref[:, :DH] = dk_acc[origin : origin + frames, :] * scale
        own_ref[:, DH:] = dv_acc[origin : origin + frames, :]
        next_ref[:, :DH] = (dk_acc[origin + frames : 2 * origin + frames, :] * scale).astype(BF)
        next_ref[:, DH:] = dv_acc[origin + frames : 2 * origin + frames, :].astype(BF)


def attn_bwd(q, o, do, lse, kv, low, high, c2, lo_q, hi_q, origin, order=()):
    frames = q.shape[0]
    blocks = frames // BQ
    pairs = frames * 1024 * DH
    window = sum(v.shape[0] for v in kv[:3]) + BK
    parts = [pl.BlockSpec(v.shape, lambda i, *_: (0, 0)) for v in kv]
    tile = pl.BlockSpec((BQ, DH), lambda i, *_: (i, 0))
    row = pl.BlockSpec((1, BQ), lambda i, *_: (0, i))
    grid_spec = pltpu.PrefetchScalarGridSpec(
        num_scalar_prefetch=3,
        grid=(blocks,),
        in_specs=[
            tile,
            tile,
            tile,
            row,
            row,
            row,
            *parts,
        ]
        + [pl.BlockSpec(memory_space=pl.ANY)] * len(order),
        out_specs=[
            tile,
            pl.BlockSpec((origin, 2 * DH), lambda i, *_: (0, 0)),
            pl.BlockSpec((frames, 2 * DH), lambda i, *_: (0, 0)),
            pl.BlockSpec((origin, 2 * DH), lambda i, *_: (0, 0)),
        ],
        scratch_shapes=[
            pltpu.VMEM((window, DH), F32),
            pltpu.VMEM((window, DH), F32),
            pltpu.VMEM((window, 2 * DH), BF),
        ],
    )

    def kernel(*refs):
        attn_bwd_kernel(origin, len(order), *refs)

    return pl.pallas_call(
        kernel,
        grid_spec=grid_spec,
        out_shape=[
            jax.ShapeDtypeStruct((frames, DH), BF),
            jax.ShapeDtypeStruct((origin, 2 * DH), BF),
            jax.ShapeDtypeStruct((frames, 2 * DH), F32),
            jax.ShapeDtypeStruct((origin, 2 * DH), BF),
        ],
        compiler_params=pltpu.CompilerParams(vmem_limit_bytes=VMEM_BYTES),
        cost_estimate=pl.CostEstimate(
            flops=80 * pairs, bytes_accessed=8 * window * DH, transcendentals=frames * 1024
        ),
        name="attention_backward",
    )(low, high, c2, q, o, do, lse, lo_q, hi_q, *kv, *order)


def pass_on_kernel(extra, *refs):
    count = (len(refs) - extra) // 2
    for a, b in zip(refs[:count], refs[count + extra :]):
        b[...] = a[...]


def pass_on(arrays, order):
    return pl.pallas_call(
        functools.partial(pass_on_kernel, len(order)),
        in_specs=[pl.BlockSpec(v.shape, lambda n=v.ndim: (0,) * n) for v in arrays]
        + [pl.BlockSpec(memory_space=pl.ANY)] * len(order),
        out_specs=[pl.BlockSpec(v.shape, lambda n=v.ndim: (0,) * n) for v in arrays],
        out_shape=[jax.ShapeDtypeStruct(v.shape, v.dtype) for v in arrays],
        compiler_params=pltpu.CompilerParams(vmem_limit_bytes=VMEM_BYTES // 3),
        cost_estimate=pl.CostEstimate(flops=1, bytes_accessed=1024, transcendentals=0),
        name="pass_on",
    )(*arrays, *order)


def join_kernel(extra, own_ref, before_ref, after_ref, *refs):
    out_ref = refs[extra]
    span = before_ref.shape[0]
    rows = own_ref.shape[0]
    out_ref[:span, :] = (own_ref[:span, :] + before_ref[...].astype(F32)).astype(BF)
    if rows > 2 * span:
        out_ref[span : rows - span, :] = own_ref[span : rows - span, :].astype(BF)
    out_ref[rows - span :, :] = (own_ref[rows - span :, :] + after_ref[...].astype(F32)).astype(BF)


def join_edges(own, before, after, order=()):
    return pl.pallas_call(
        functools.partial(join_kernel, len(order)),
        in_specs=[pl.BlockSpec(v.shape, lambda: (0, 0)) for v in (own, before, after)]
        + [pl.BlockSpec(memory_space=pl.ANY)] * len(order),
        out_specs=pl.BlockSpec(own.shape, lambda: (0, 0)),
        out_shape=jax.ShapeDtypeStruct(own.shape, BF),
        compiler_params=pltpu.CompilerParams(vmem_limit_bytes=VMEM_BYTES // 2),
        cost_estimate=pl.CostEstimate(
            flops=own.size, bytes_accessed=8 * own.size, transcendentals=0
        ),
        name="join_edges",
    )(own, before, after, *order)


def stack_kernel(extra, places, arrays, *refs):
    out_ref = refs[arrays + extra]
    rows_ref = refs[arrays + extra + 1]
    for at, (source, row) in enumerate(places):
        rows_ref[at : at + 1, :] = refs[source][row : row + 1, :]
    share = out_ref.shape[2]
    rows = rows_ref[...]
    for i in range(out_ref.shape[0]):
        out_ref[i] = rows[:, i * share : (i + 1) * share]


def stack_rows(arrays, places, devices, order=()):
    width = arrays[0].shape[1]
    share = width // devices
    if share % 32:
        rows = jnp.stack([arrays[source][row] for source, row in places])
        return rows.reshape(len(places), devices, share).transpose(1, 0, 2)
    return pl.pallas_call(
        functools.partial(stack_kernel, len(order), places, len(arrays)),
        in_specs=[pl.BlockSpec(v.shape, lambda: (0, 0)) for v in arrays]
        + [pl.BlockSpec(memory_space=pl.ANY)] * len(order),
        out_specs=pl.BlockSpec((devices, len(places), share), lambda: (0, 0, 0)),
        out_shape=jax.ShapeDtypeStruct((devices, len(places), share), F32),
        scratch_shapes=[pltpu.VMEM((len(places), width), F32)],
        name="stack_rows",
    )(*arrays, *order)


def halve_kernel(extra, sel_ref, kept_a, kept_b, got_a, got_b, *refs):
    send_ref, keep_ref = refs[extra:]
    send_ref[...] = (kept_a[0].astype(F32) + got_a[0].astype(F32)).astype(BF)
    keep_ref[...] = (kept_b[0].astype(F32) + got_b[0].astype(F32)).astype(BF)


def halve(kept, got, mine, order=()):
    count, _, rows, columns = kept.shape
    step = rows
    while step % 32 == 0 and step * columns > 512 * 1024:
        step //= 2
    block = (1, 1, step, columns)
    other = pl.BlockSpec(block, lambda i, j, m: (i, 1 - m[0], j, 0))
    own = pl.BlockSpec(block, lambda i, j, m: (i, m[0], j, 0))
    out = pl.BlockSpec((1, step, columns), lambda i, j, m: (i, j, 0))
    return pl.pallas_call(
        functools.partial(halve_kernel, len(order)),
        grid_spec=pltpu.PrefetchScalarGridSpec(
            num_scalar_prefetch=1,
            grid=(count, rows // step),
            in_specs=[other, own, other, own]
            + [pl.BlockSpec(memory_space=pl.ANY)] * len(order),
            out_specs=[out, out],
        ),
        out_shape=[jax.ShapeDtypeStruct((count, rows, columns), BF)] * 2,
        compiler_params=pltpu.CompilerParams(vmem_limit_bytes=VMEM_BYTES // 3),
        cost_estimate=pl.CostEstimate(flops=1024, bytes_accessed=1024, transcendentals=0),
        name="halve",
    )(mine.astype(jnp.int32)[None], kept, kept, got, got, *order)


def finish_kernel(extra, turned, kept_ref, got_ref, *refs):
    total = kept_ref[...].astype(F32) + got_ref[...].astype(F32)
    refs[extra][...] = total.T if turned else total


def finish(kept, got, turned=False, order=()):
    rows, columns = kept.shape
    fixed = pl.BlockSpec((rows, columns), lambda: (0, 0))
    shape = (columns, rows) if turned else (rows, columns)
    if turned and rows % 128:
        return finish(kept, got, False, order).T
    return pl.pallas_call(
        functools.partial(finish_kernel, len(order), turned),
        in_specs=[fixed, fixed] + [pl.BlockSpec(memory_space=pl.ANY)] * len(order),
        out_specs=pl.BlockSpec(shape, lambda: (0, 0)),
        out_shape=jax.ShapeDtypeStruct(shape, F32),
        compiler_params=pltpu.CompilerParams(vmem_limit_bytes=VMEM_BYTES // 3),
        name="finish",
    )(kept, got, *order)


def halve_both_kernel(extra, sel_ref, *refs):
    send_ref, keep_ref = refs[8 + extra :]
    for i in (0, 1):
        kept_a, kept_b, got_a, got_b = refs[4 * i : 4 * i + 4]
        rows = kept_a.shape[2]
        here = slice(i * rows, (i + 1) * rows)
        send_ref[0, here, :] = (kept_a[0, 0].astype(F32) + got_a[0, 0].astype(F32)).astype(BF)
        keep_ref[0, here, :] = (kept_b[0, 0].astype(F32) + got_b[0, 0].astype(F32)).astype(BF)


def halve_both(first, second, shape, mine, order=()):
    count, _, rows, columns = shape
    block = (1, 1, rows, columns)
    other = pl.BlockSpec(block, lambda i, m: (i, 1 - m[0], 0, 0))
    own = pl.BlockSpec(block, lambda i, m: (i, m[0], 0, 0))
    out = pl.BlockSpec((1, 2 * rows, columns), lambda i, m: (i, 0, 0))
    arrays = []
    for part in (first, second):
        kept, got = part.kept.reshape(shape), part.got.reshape(shape)
        arrays += [kept, kept, got, got]
    return pl.pallas_call(
        functools.partial(halve_both_kernel, len(order)),
        grid_spec=pltpu.PrefetchScalarGridSpec(
            num_scalar_prefetch=1,
            grid=(count,),
            in_specs=[other, own, other, own] * 2
            + [pl.BlockSpec(memory_space=pl.ANY)] * len(order),
            out_specs=[out, out],
        ),
        out_shape=[jax.ShapeDtypeStruct((count, 2 * rows, columns), BF)] * 2,
        compiler_params=pltpu.CompilerParams(vmem_limit_bytes=VMEM_BYTES // 3),
        cost_estimate=pl.CostEstimate(flops=1024, bytes_accessed=1024, transcendentals=0),
        name="halve_both",
    )(mine.astype(jnp.int32)[None], *arrays, *order)


def finish_both_kernel(extra, kept_ref, got_ref, *refs):
    first_ref, second_ref = refs[extra:]
    rows = first_ref.shape[0]
    total = kept_ref[...].astype(F32) + got_ref[...].astype(F32)
    first_ref[...] = total[:rows]
    second_ref[...] = total[rows:].T


def finish_both(total, rows, columns, order=()):
    kept, got = total.kept.reshape(2 * rows, columns), total.got.reshape(2 * rows, columns)
    if rows % 128:
        both = kept.astype(F32) + got.astype(F32)
        return both[:rows], both[rows:].T
    fixed = lambda *shape: pl.BlockSpec(shape, lambda: (0, 0))
    return pl.pallas_call(
        functools.partial(finish_both_kernel, len(order)),
        in_specs=[fixed(2 * rows, columns)] * 2
        + [pl.BlockSpec(memory_space=pl.ANY)] * len(order),
        out_specs=[fixed(rows, columns), fixed(columns, rows)],
        out_shape=[
            jax.ShapeDtypeStruct((rows, columns), F32),
            jax.ShapeDtypeStruct((columns, rows), F32),
        ],
        compiler_params=pltpu.CompilerParams(vmem_limit_bytes=VMEM_BYTES // 3),
        cost_estimate=pl.CostEstimate(flops=1024, bytes_accessed=1024, transcendentals=0),
        name="finish_both",
    )(kept, got, *order)


def total_kernel(extra, parts_ref, *refs):
    total = jnp.sum(parts_ref[...], axis=0)
    at = 0
    for ref in refs[extra:]:
        ref[...] = total[at : at + ref.shape[0]]
        at += ref.shape[0]


def total_of(parts, counts, order=()):
    columns = parts.shape[2]
    return pl.pallas_call(
        functools.partial(total_kernel, len(order)),
        in_specs=[pl.BlockSpec(parts.shape, lambda: (0, 0, 0))]
        + [pl.BlockSpec(memory_space=pl.ANY)] * len(order),
        out_specs=[pl.BlockSpec((n, columns), lambda: (0, 0)) for n in counts],
        out_shape=[jax.ShapeDtypeStruct((n, columns), F32) for n in counts],
        name="total_of",
    )(parts, *order)


class Sum:
    def __init__(self, kept, send, axis, bit):
        self.kept = kept
        self.send = send
        self.got = xor_send(send, axis, bit)

    def step(self, shape, axis, bit=1, order=()):
        mine = (lax.axis_index(axis) // bit) % 2
        send, kept = halve(self.kept.reshape(shape), self.got.reshape(shape), mine, order)
        return Sum(kept, send, axis, bit)

    def finish(self, shape, turned=False, order=()):
        return finish(self.kept.reshape(shape), self.got.reshape(shape), turned, order)


def slab_grad_kernel(split, extra, pair, sel_ref, la_ref, lb_ref, ra_ref, rb_ref, *refs):
    if pair:
        rb_ref = [jnp.where(pl.program_id(0) == 0, rb_ref[0], refs[0][0])]
        refs = refs[1:]
    out_ref = refs[extra]
    if split is None:
        out = dot_tn(la_ref[0], ra_ref[0]) + dot_tn(lb_ref[0], rb_ref[0])
    else:
        zs, rows = split
        take = [pl.ds(pl.multiple_of((z * 2 + sel_ref[0]) * rows, rows), rows) for z in range(zs)]
        left = [jnp.concatenate([ref[0, :, t] for t in take], axis=1) for ref in (la_ref, lb_ref)]
        out = dot_tn(left[0], ra_ref[0]) + dot_tn(left[1], rb_ref[0])
    out_ref[0] = out.astype(BF)


def slab_grad(left, right, x, y, order=(), lasting=0):
    left_a, left_b, left_at = left
    right_a, right_b, right_at = right
    pair = isinstance(right_b, tuple)
    _, frames, width = left_a.shape
    hidden = right_a.shape[2]
    zs = lax.axis_size("z")
    rows = width // (2 * zs)
    half = width // 2
    if x is None:
        split = None
        sel = y
        left_block = pl.BlockSpec((1, frames, half), lambda i, s: (left_at, 0, i))
        right = [
            pl.BlockSpec((1, frames, hidden), lambda i, s: (s[0], 0, 0)),
            pl.BlockSpec((1, frames, hidden), lambda i, s: (s[0] + right_at, 0, 0)),
        ]
    else:
        sel = x
        right = [
            pl.BlockSpec((1, frames, hidden), lambda i, s: (i, 0, 0)),
            pl.BlockSpec((1, frames, hidden), lambda i, s: (i + right_at, 0, 0)),
        ]
        if pair:
            right[1:] = [pl.BlockSpec((1, frames, hidden), lambda i, s: (0, 0, 0))] * 2
        if rows % 128 == 0:
            split = (zs, rows)
            left_block = pl.BlockSpec((1, frames, width), lambda i, s: (left_at, 0, 0))
        else:
            split = None
            left_block = pl.BlockSpec((1, frames, half), lambda i, s: (0, 0, 0))
            left_a, left_b = (
                pick(l[left_at].reshape(frames, zs, 2, rows), x, 2).reshape(1, frames, half)
                for l in (left_a, left_b)
            )
    return pl.pallas_call(
        functools.partial(slab_grad_kernel, split, len(order), pair),
        grid_spec=pltpu.PrefetchScalarGridSpec(
            num_scalar_prefetch=1,
            grid=(2,),
            in_specs=[left_block, left_block]
            + right
            + [pl.BlockSpec(memory_space=pl.ANY)] * len(order),
            out_specs=pl.BlockSpec((1, half, hidden), lambda i, s: (i, 0, 0)),
        ),
        out_shape=jax.ShapeDtypeStruct((2, half, hidden), BF),
        compiler_params=pltpu.CompilerParams(vmem_limit_bytes=VMEM_BYTES),
        cost_estimate=takes(lasting),
        name="slab_grad",
    )(sel.astype(jnp.int32)[None], left_a, left_b, right_a, *(right_b if pair else (right_b,)), *order)


def slab_sum(left, right, first, order=(), kept_order=()):
    place = lax.axis_index(first)
    picks = lambda i: (i, None) if first == "x" else (None, i)
    away = slab_grad(left, right, *picks(1 - place), order)
    return Sum(slab_grad(left, right, *picks(place), (away,) + tuple(kept_order)), away, first, 1)


def slab_second(total, first, order=()):
    zs = lax.axis_size("z")
    _, half, hidden = total.kept.shape
    if first == "x":
        return total.step((1, 2, half, hidden), "y", 1, order)
    return total.step((zs, 2, half // zs, hidden), "x", 1, order)


def z_steps(total, rows, columns, bits=None, order=()):
    zs = lax.axis_size("z")
    for bit in z_bits() if bits is None else bits:
        total = total.step((zs // (2 * bit), 2, rows, columns), "z", bit, order)
    return total


def z_both(first, second, rows, columns, order=()):
    zs = lax.axis_size("z")
    mine = lax.axis_index("z") % 2
    send, kept = halve_both(first, second, (zs // 2, 2, rows, columns), mine, order)
    return Sum(kept, send, "z", 1)


def z_bits():
    bits = []
    while 1 << len(bits) < lax.axis_size("z"):
        bits.append(1 << len(bits))
    return bits


def right_of(ref):
    if len(ref.shape) == 2:
        return ref[...]
    return jnp.concatenate([heads_of(ref, at, at + DH) for at in range(0, ref.shape[2], DH)], axis=1)


def row_grad_kernel(pairs, rows, core_ref, *refs):
    send_ref, keep_ref = refs[-2:]
    at = 0
    for i in range(pairs):
        whole = dot_tn(refs[2 * i][...], right_of(refs[2 * i + 1])).astype(BF)
        columns = whole.shape[1]
        parts = [whole[k * rows : (k + 1) * rows] for k in range(whole.shape[0] // rows)]
        even = jnp.concatenate(parts[0::2], axis=0)
        odd = jnp.concatenate(parts[1::2], axis=0)
        first = core_ref[0] == 0
        keep_ref[:, at : at + columns] = jnp.where(first, even, odd)
        send_ref[:, at : at + columns] = jnp.where(first, odd, even)
        at += columns


def row_grad(core, pairs, order=()):
    frames, width = pairs[0][0].shape
    zs = lax.axis_size("z")
    rows = width // (8 * zs)
    columns = sum(right.size // frames for _, right in pairs)
    if rows % 16:
        whole = jnp.concatenate(
            [dot_tn(left, right_of(right)).astype(BF) for left, right in pairs], axis=1
        )
        whole = whole.reshape(4 * zs, 2, rows, columns)
        flat = lambda v: v.reshape(width // 2, columns)
        return flat(pick(whole, 1 - core[0], 1)), flat(pick(whole, core[0], 1))
    tile = 256
    specs, args = [], []
    for left, right in pairs:
        specs += [
            pl.BlockSpec((frames, tile), lambda i, c: (0, i)),
            pl.BlockSpec(right.shape, lambda i, c, n=right.ndim: (0,) * n),
        ]
        args += [left, right]
    specs += [pl.BlockSpec(memory_space=pl.ANY)] * len(order)
    out = pl.BlockSpec((tile // 2, columns), lambda i, c: (i, 0))
    return pl.pallas_call(
        functools.partial(row_grad_kernel, len(pairs), rows),
        grid_spec=pltpu.PrefetchScalarGridSpec(
            num_scalar_prefetch=1, grid=(width // tile,), in_specs=specs, out_specs=[out, out]
        ),
        out_shape=[jax.ShapeDtypeStruct((width // 2, columns), BF)] * 2,
        compiler_params=pltpu.CompilerParams(vmem_limit_bytes=VMEM_BYTES),
        cost_estimate=takes(10),
        name="row_grad",
    )(core, *args, *order)


def body(
    block_in,
    out_grad,
    utt_ends,
    valid_ends,
    ffn1_in,
    ffn1_out,
    att_qkv,
    att_out,
    content_bias,
    conv_in,
    conv_out,
    ffn2_in,
    ffn2_out,
    conv_depth,
    norm_gain,
    norm_bias,
):
    zs = lax.axis_size("z")
    devices = 8 * zs
    frames, width = block_in.shape
    heads = width // DH
    z, x, y, c = (lax.axis_index(axis) for axis in DEV)
    place = ((z * 2 + x) * 2 + y) * 2 + c
    head = (x * 2 + y) * 2 + c

    small = jnp.concatenate([norm_gain, norm_bias, conv_depth, content_bias[None]], axis=0)
    small = jnp.broadcast_to(small[None], (devices,) + small.shape)
    small = lax.all_to_all(small, DEV, split_axis=0, concat_axis=0, tiled=True)
    small = small.transpose(1, 0, 2).reshape(small.shape[1], width).astype(F32)
    gains, shifts, taps, q_bias = small[:6], small[6:12], small[12 : 12 + KSIZE], small[12 + KSIZE]

    rows, few = ffn1_in.shape[0], att_qkv.shape[0]
    blocks = lambda w: [w[:, i : i + width] for i in range(0, w.shape[1], width)]

    def gather(*parts):
        mine = jnp.concatenate(parts, axis=0)
        return lax.all_gather(mine, DEV, axis=0, tiled=True).reshape(devices, -1, width)

    w_first = gather(pack_ffn(ffn1_in, ffn1_out), *blocks(att_qkv))
    w_mid = gather(att_out, *blocks(conv_in), conv_out)
    w_second = gather(pack_ffn(ffn2_in, ffn2_out, order=(small,)))
    w_proj = Rows(w_first, 2 * rows, few)
    w_conv = Rows(w_mid, 0, few)
    w_cout = Rows(w_mid, 3 * few, few)
    core = c.astype(jnp.int32)[None]

    all_frames = frames * devices
    first_frame = place * frames
    span = 4 * frames
    group = 8 * frames
    origin = span
    group_first = z * group
    starts = jnp.concatenate([jnp.zeros((1,), jnp.int32), utt_ends[:-1]])
    valid_count = jnp.sum((valid_ends - starts).astype(F32))

    def segments(positions):
        seg = jnp.sum((utt_ends[None, :] <= positions[:, None]).astype(jnp.int32), axis=1)
        valid_seg = jnp.sum((valid_ends[None, :] <= positions[:, None]).astype(jnp.int32), axis=1)
        valid = seg == valid_seg
        return jnp.where(positions < 0, -1, jnp.where(positions >= all_frames, -2, seg)), valid

    ext_seg, ext_valid = segments(
        first_frame - REACH + jnp.arange(frames + 2 * REACH, dtype=jnp.int32)
    )
    own_seg = ext_seg[REACH : REACH + frames]
    ext_valid = ext_valid.astype(F32)
    edge_valid = jnp.concatenate([ext_valid[:REACH], ext_valid[-REACH:]])
    edge_valid = jnp.concatenate([edge_valid, jnp.zeros((frames - 2 * REACH,), F32)])
    columns = jnp.stack(
        [(ext_seg[m : m + frames] == own_seg).astype(F32) for m in range(KSIZE)]
        + [ext_valid[REACH : REACH + frames], edge_valid, jnp.zeros((frames,), F32)],
        axis=1,
    )
    group_pos = group_first + jnp.arange(group, dtype=jnp.int32)
    ended = utt_ends[None, :] <= group_pos[:, None]
    group_seg = jnp.sum(ended.astype(jnp.int32), axis=1)
    group_lo = jnp.max(jnp.where(ended, utt_ends[None, :], 0), axis=1)
    slots = jnp.arange(utt_ends.shape[0], dtype=jnp.int32)
    group_hi = jnp.sum(
        jnp.where(group_seg[:, None] == slots[None, :], valid_ends[None, :], 0), axis=1
    )
    window_first = group_first - origin
    lo_q = group_lo - window_first
    hi_q = group_hi - window_first
    low = (lo_q[::BQ] // 128) * 128
    high = hi_q[BQ - 1 :: BQ]
    lo_q = lo_q.astype(F32)[None, :]
    hi_q = hi_q.astype(F32)[None, :]
    c2 = (32.0 * jnp.exp2(-head.astype(F32)) * (LOG2E / span))[None]

    def vectors(*rows):
        rows = jnp.stack(rows)
        return jnp.concatenate([rows, jnp.zeros((-len(rows) % 8, width), F32)], axis=0)

    count_row = jnp.broadcast_to(valid_count, (width,))

    x1, n2, pack1, s1, d1, q_heads, k_heads, v_heads = first_call(
        core,
        block_in,
        w_first,
        rows,
        w_proj,
        vectors(gains[0], shifts[0], gains[1], shifts[1], q_bias),
    )
    pack1_sib = xor_send(pack1, "c", 1)

    def to_heads(cells):
        got = lax.all_to_all(cells, LAYER, split_axis=0, concat_axis=0, tiled=True)
        return got.reshape(group, cells.shape[2])

    def to_frames(cells):
        cells = cells.reshape(heads, frames, cells.shape[1])
        return lax.all_to_all(cells, LAYER, split_axis=0, concat_axis=0, tiled=True)

    up = [(i, i + 1) for i in range(zs - 1)]
    down = [(i + 1, i) for i in range(zs - 1)]

    def with_edges(cells):
        return lax.ppermute(cells[-span:], "z", up), cells, lax.ppermute(cells[:span], "z", down)

    kv = with_edges(to_heads(k_heads)) + with_edges(to_heads(v_heads))
    q_own = to_heads(q_heads)
    o_own, lse = attn_fwd(q_own, kv, low, high, c2, lo_q, hi_q, origin)
    mixed, x2, n3, lin, sig, gated = gate_call(
        to_frames(o_own), x1, w_conv, vectors(gains[2], shifts[2]), columns, (pack1_sib,)
    )
    g_edges = neighbour_rows(gated)
    tap_rows = [taps[m] for m in range(KSIZE)]
    conv, moments = conv_call(gated, *g_edges, vectors(*tap_rows), columns, devices)
    spread = lambda cells: lax.all_to_all(cells, DEV, split_axis=0, concat_axis=0, tiled=True)
    moments = spread(moments)

    final_out, swished, dx3, ew, dz, sums_c, totals, pack2, s2, da2 = second_call(
        core,
        x2,
        conv,
        moments,
        w_cout,
        w_second,
        rows,
        vectors(gains[3], shifts[3], gains[4], shifts[4], gains[5], shifts[5], count_row),
        out_grad,
    )
    totals = spread(totals)
    edges = neighbour_rows(jnp.concatenate([dz[-REACH:], conv[-REACH:]]), jnp.concatenate([dz[:REACH], conv[:REACH]]))
    pack2_sib = xor_send(pack2, "c", 1)
    hidden = pack2.shape[2]
    f2i = slab_sum((pack2, pack2_sib, 0), (da2, pack2_sib, 4), "x")
    f2o = slab_sum((pack2, pack2_sib, 3), (s2, pack2_sib, 1), "y")

    point_grad, dx2, ey, mixed_grad, sums_b = back_call(
        dz,
        conv,
        edges,
        gated,
        g_edges,
        moments,
        totals,
        lin,
        sig,
        x2,
        dx3,
        w_conv,
        vectors(*tap_rows, gains[3], gains[2], gains[2], count_row),
        columns,
        order=(f2i.send, f2o.send),
    )
    do_own = to_heads(mixed_grad)
    send, kept = row_grad(core, [(mixed, ey), (n3, point_grad), (swished, ew)])
    mid = Sum(kept, send, "c", 1)
    dq, dkv_prev, dkv, dkv_next = attn_bwd(
        q_own,
        o_own,
        do_own,
        lse,
        kv,
        low,
        high,
        c2,
        lo_q,
        hi_q,
        origin,
        order=(f2i.kept, f2o.kept, kept),
    )
    dq = to_frames(dq)
    f2i = slab_second(f2i, "x")
    f2o = slab_second(f2o, "y", order=(f2i.send,))
    dkv = join_edges(
        dkv,
        lax.ppermute(dkv_next, "z", up),
        lax.ppermute(dkv_prev, "z", down),
        order=(f2i.send, f2o.send),
    )
    dkv = to_frames(dkv)

    low_z, high_z = z_bits()[:1], z_bits()[1:]
    dx1, ef1, sums_p = proj_back_call(dq, dkv, dx2, x1, w_proj, vectors(gains[0], gains[1]), ())
    ef1_sib = xor_send(ef1, "c", 1)
    send, kept = row_grad(core, [(n2, dq), (n2, dkv)], order=(ef1,))
    qkv = Sum(kept, send, "c", 1)
    f1o_left, f1o_right = (ef1, ef1_sib, 0), (s1, pack1_sib, 1)
    f1o_away = slab_grad(f1o_left, f1o_right, None, 1 - y, (qkv.send,))
    mid = mid.step((zs, 2, 2 * few, 4 * width), "x", order=(f1o_away,))
    f2 = z_both(f2i, f2o, rows, hidden, order=(mid.send,))
    grad_input, sums_a, da_first, da_second, da1 = last_call(
        core,
        dx1,
        ef1,
        block_in,
        w_first,
        rows,
        d1,
        vectors(gains[0]),
        order=(f2.send,),
    )
    da_sib = (xor_send(da_first, "c", 1), xor_send(da_second, "c", 1))
    f2 = z_steps(f2, 2 * rows, hidden, high_z, order=(da1,))
    f1o = Sum(slab_grad(f1o_left, f1o_right, None, y, (f2.send,), 10), f1o_away, "y", 1)
    f1i = slab_sum((pack1, pack1_sib, 0), (da1, da_sib, 0), "x", order=(f1o.kept,))
    grad_f2i, grad_f2o = finish_both(f2, rows, hidden, order=(f1i.kept,))
    qkv = z_steps(qkv, 4 * few, 3 * width, low_z, order=(grad_f2i,))
    f1o = slab_second(f1o, "y", order=(qkv.send,))
    mid = mid.step((zs, 2, few, 4 * width), "y", order=(f1o.send,))
    qkv = qkv.step((zs // 2, 2, 2 * few, 3 * width), "x", order=(mid.send,))
    mid = z_steps(mid, few, 4 * width, low_z, order=(qkv.send,))
    f1i = slab_second(f1i, "x", order=(mid.send,))
    f1o = z_steps(f1o, rows, hidden, low_z, order=(f1i.send,))
    mid = z_steps(mid, few, 4 * width, high_z, order=(f1o.send,))
    f1i = z_steps(f1i, rows, hidden, low_z, order=(mid.send,))
    f1o = z_steps(f1o, rows, hidden, high_z, order=(f1i.send,))
    mid = mid.finish((few, 4 * width), order=(f1o.send,))
    out_att, out_cin, out_cout = mid[:, :width], mid[:, width : 3 * width], mid[:, 3 * width :]
    qkv = qkv.step((zs // 2, 2, few, 3 * width), "y", order=(mid,))
    f1i = z_steps(f1i, rows, hidden, high_z, order=(qkv.send,))
    a, b, c, p = 0, 1, 2, 3
    places = [(a, 0), (p, 0), (b, 0), (c, 4), (c, 2), (c, 0)]
    places += [(a, 1), (p, 1), (b, 1), (c, 5), (c, 3), (c, 1)]
    places += [(b, 2 + m) for m in range(KSIZE)] + [(p, 2)]
    sums = stack_rows([sums_a, sums_b, sums_c, sums_p], places, devices, order=(f1i.send,))
    qkv = z_steps(qkv, few, 3 * width, high_z, order=(sums,))
    grad_f1o = f1o.finish((rows, hidden), True, order=(qkv.send,))
    grad_f1i = f1i.finish((rows, hidden), order=(grad_f1o,))
    out_qkv = qkv.finish((few, 3 * width), order=(grad_f1i,))
    sums = lax.all_to_all(sums, DEV, split_axis=0, concat_axis=0, tiled=True)
    gain_sums, bias_sums, tap_sums, query_sums = total_of(
        sums, (6, 6, KSIZE, 1), order=(out_qkv,)
    )

    return (
        final_out,
        grad_input,
        grad_f1i,
        grad_f1o,
        out_qkv,
        out_att,
        query_sums[0],
        out_cin,
        out_cout,
        grad_f2i,
        grad_f2o,
        tap_sums,
        gain_sums,
        bias_sums,
    )


def solution(mesh):
    seq, heads = mesh.shape["seq"], mesh.shape["head"]
    grid = Mesh(mesh.devices.reshape(seq // 2, 2, heads // 2, 2), DEV)
    both = P(DEV, None)
    inward = P(("z", "x"), ("y", "c"))
    outward = P(("y", "c"), ("z", "x"))
    columns = P(None, DEV)
    return jax.shard_map(
        body,
        mesh=grid,
        in_specs=(
            both,
            both,
            P(),
            P(),
            inward,
            outward,
            both,
            both,
            P(DEV),
            both,
            both,
            inward,
            outward,
            columns,
            columns,
            columns,
        ),
        out_specs=(
            both,
            both,
            inward,
            outward,
            both,
            both,
            P(DEV),
            both,
            both,
            inward,
            outward,
            columns,
            columns,
            columns,
        ),
        check_vma=False,
    )
```

```python
import functools
import math

import jax
import jax.numpy as jnp
from jax import lax
from jax.experimental import pallas as pl
from jax.experimental.pallas import tpu as pltpu
from jax.sharding import Mesh
from jax.sharding import PartitionSpec as P

DH = 128
KSIZE = 5
REACH = (KSIZE - 1) // 2
EPSILON = 1e-05
MASKED = -1e30
LOG2E = math.log2(math.e)
DEV = ("z", "x", "y", "c")
LAYER = ("x", "y", "c")
BQ = 512
BK = 1024
BF = jnp.bfloat16
F32 = jnp.float32
VMEM_BYTES = 56 * 1024 * 1024


def takes(microseconds):
    return pl.CostEstimate(
        flops=1024, bytes_accessed=1024 + int(microseconds * 3.7e6), transcendentals=0
    )


def pick(cells, index, dim):
    return lax.dynamic_index_in_dim(cells, index, dim, keepdims=False)


def xor_send(cells, axis, bit):
    count = lax.axis_size(axis)
    return lax.ppermute(cells, axis, [(i, i ^ bit) for i in range(count)])


def neighbour_rows(tail, head=None):
    if head is None:
        tail, head = tail[-REACH:], tail[:REACH]
    count = 1
    for axis in DEV:
        count *= lax.axis_size(axis)
    before = lax.ppermute(tail, DEV, [(i, i + 1) for i in range(count - 1)])
    after = lax.ppermute(head, DEV, [(i + 1, i) for i in range(count - 1)])
    return before, after


def dot_nn(a, b):
    return lax.dot_general(a, b, (((1,), (0,)), ((), ())), preferred_element_type=F32)


def dot_nt(a, b):
    return lax.dot_general(a, b, (((1,), (1,)), ((), ())), preferred_element_type=F32)


def dot_tn(a, b):
    return lax.dot_general(a, b, (((0,), (0,)), ((), ())), preferred_element_type=F32)


def norm_stats(values):
    centred = values - jnp.mean(values, axis=-1, keepdims=True)
    inv_std = lax.rsqrt(jnp.mean(centred * centred, axis=-1, keepdims=True) + EPSILON)
    return centred * inv_std, inv_std


def norm_back(upstream, normed, inv_std, gain):
    scaled = upstream * gain
    inner = (
        scaled
        - jnp.mean(scaled, axis=-1, keepdims=True)
        - normed * jnp.mean(scaled * normed, axis=-1, keepdims=True)
    )
    return inv_std * inner


def pack_kernel(extra, in_ref, out_ref, *refs):
    rows = in_ref.shape[0]
    refs[extra][:rows] = in_ref[...]
    refs[extra][rows:] = out_ref[...].T


def pack_ffn(w_in, w_out, order=()):
    rows, width = w_in.shape
    whole = lambda v: pl.BlockSpec(v.shape, lambda: (0, 0))
    if rows % 128:
        return jnp.concatenate([w_in, w_out.T], axis=0)
    return pl.pallas_call(
        functools.partial(pack_kernel, len(order)),
        in_specs=[whole(w_in), whole(w_out)] + [pl.BlockSpec(memory_space=pl.ANY)] * len(order),
        out_specs=pl.BlockSpec((2 * rows, width), lambda: (0, 0)),
        out_shape=jax.ShapeDtypeStruct((2 * rows, width), BF),
        name="pack_ffn",
    )(w_in, w_out, *order)


class Rows:
    def __init__(self, gathered, first, count):
        self.stepped = count % 16 == 0 and first % count == 0
        devices, _, width = gathered.shape
        self.count = count
        if self.stepped:
            self.at = first // count
            self.array = gathered
            self.block = (devices, count, width)
        else:
            self.first = first
            self.gathered = gathered
            self.width = width

    def blocks(self, pick_block, total):
        if self.stepped:
            at = self.at
            return self.array, pl.BlockSpec(self.block, lambda j, *_: (0, at + pick_block(j), 0))
        cut = [
            self.gathered[:, self.first + i * self.count : self.first + (i + 1) * self.count]
            for i in range(total)
        ]
        cut = jnp.stack([v.reshape(-1, self.width) for v in cut])
        return cut, pl.BlockSpec((1,) + cut.shape[1:], lambda j, *_: (pick_block(j), 0, 0))


def square(ref):
    return ref[...].reshape(-1, ref.shape[-1])


def slab_of(step, core):
    return (step % 2) * 2 + jnp.where(step < 2, 1 - core, core)


def slab_specs(gathered, rows, step_of):
    devices, total, width = gathered.shape
    array = gathered.reshape(devices // 4, 4, total, width)
    block = (devices // 4, 1, rows, width)
    specs = [
        pl.BlockSpec(block, lambda j, c, i=i: (0, slab_of(step_of(j), c[0]), i, 0)) for i in (0, 1)
    ]
    return [array, array], specs


def heads_of(ref, lo, hi):
    return jnp.concatenate([ref[h, :, lo:hi] for h in range(ref.shape[0])], axis=1)


def forward_slab(n, w1_ref, w2_ref, s_ref, d_out):
    width = n.shape[1]
    w1 = square(w1_ref)
    chunk = 256
    for at in range(0, width, chunk):
        a = dot_nn(n, w1[:, at : at + chunk])
        sig = jax.nn.sigmoid(a)
        s_ref[:, at : at + chunk] = (a * sig).astype(BF)
        d_out[:, at : at + chunk] = (sig * (1.0 + a * (1.0 - sig))).astype(BF)
    return dot_nt(s_ref[...], square(w2_ref))


def backward_slab(ef, w1_ref, w2_ref, d_in, da_ref):
    width = ef.shape[1]
    w2 = square(w2_ref)
    chunk = 256
    for at in range(0, width, chunk):
        ds = dot_nn(ef, w2[:, at : at + chunk])
        da_ref[:, at : at + chunk] = (ds * d_in[:, at : at + chunk].astype(F32)).astype(BF)
    return dot_nt(da_ref[...], square(w1_ref))


def keep_slab(step, cells, pack_ref, pack_at, own_ref):
    @pl.when(step < 2)
    def _():
        pack_ref[pack_at + step] = cells

    @pl.when(step >= 2)
    def _():
        own_ref[0] = cells


def first_kernel(
    core_ref,
    x_ref,
    w1_ref,
    w2_ref,
    wp_ref,
    vec_ref,
    x1_ref,
    n2_ref,
    pack_ref,
    own_ref,
    d_ref,
    q_ref,
    k_ref,
    v_ref,
    acc_ref,
    s_ref,
):
    step = pl.program_id(0)

    @pl.when(step == 0)
    def _():
        normed, _ = norm_stats(x_ref[...].astype(F32))
        pack_ref[0] = (normed * vec_ref[0:1, :] + vec_ref[1:2, :]).astype(BF)
        acc_ref[...] = jnp.zeros_like(acc_ref)

    @pl.when(step < 4)
    def _():
        acc_ref[...] += forward_slab(pack_ref[0], w1_ref, w2_ref, s_ref, d_ref.at[0])
        keep_slab(step, s_ref[...], pack_ref, 1, own_ref)

    @pl.when(step == 3)
    def _():
        x1 = x_ref[...].astype(F32) + 0.5 * acc_ref[...]
        x1_ref[...] = x1
        normed, _ = norm_stats(x1)
        n2_ref[...] = (normed * vec_ref[2:3, :] + vec_ref[3:4, :]).astype(BF)

    for part, ref in enumerate((q_ref, k_ref, v_ref)):

        @pl.when(step == 4 + part)
        def _():
            projected = dot_nn(n2_ref[...], square(wp_ref))
            if part == 0:
                projected = projected + vec_ref[4:5, :]
            projected = projected.astype(BF)
            for h in range(ref.shape[0]):
                ref[h] = projected[:, h * DH : (h + 1) * DH]


def first_call(core, x, gathered, rows, proj, vectors):
    frames, width = x.shape
    heads = width // DH
    fixed = lambda *shape: pl.BlockSpec(shape, lambda j, c: (0,) * len(shape))
    slabs, slab_blocks = slab_specs(gathered, rows, lambda j: jnp.minimum(j, 3))
    proj_array, proj_block = proj.blocks(lambda j: jnp.clip(j - 4, 0, 2), 3)
    return pl.pallas_call(
        first_kernel,
        grid_spec=pltpu.PrefetchScalarGridSpec(
            num_scalar_prefetch=1,
            grid=(7,),
            in_specs=[fixed(frames, width)] + slab_blocks + [proj_block, fixed(*vectors.shape)],
            out_specs=[
                fixed(frames, width),
                fixed(frames, width),
                fixed(3, frames, width),
                pl.BlockSpec((1, frames, width), lambda j, c: (jnp.clip(j - 2, 0, 1), 0, 0)),
                pl.BlockSpec((1, frames, width), lambda j, c: (jnp.minimum(j, 3), 0, 0)),
                fixed(heads, frames, DH),
                fixed(heads, frames, DH),
                fixed(heads, frames, DH),
            ],
            scratch_shapes=[pltpu.VMEM((frames, width), F32), pltpu.VMEM((frames, width), BF)],
        ),
        out_shape=[
            jax.ShapeDtypeStruct((frames, width), F32),
            jax.ShapeDtypeStruct((frames, width), BF),
            jax.ShapeDtypeStruct((3, frames, width), BF),
            jax.ShapeDtypeStruct((2, frames, width), BF),
            jax.ShapeDtypeStruct((4, frames, width), BF),
            jax.ShapeDtypeStruct((heads, frames, DH), BF),
            jax.ShapeDtypeStruct((heads, frames, DH), BF),
            jax.ShapeDtypeStruct((heads, frames, DH), BF),
        ],
        compiler_params=pltpu.CompilerParams(vmem_limit_bytes=VMEM_BYTES),
        cost_estimate=pl.CostEstimate(
            flops=22 * frames * width * width,
            bytes_accessed=22 * width * width + 40 * frames * width,
            transcendentals=4 * frames * width,
        ),
        name="first_part",
    )(core, x, *slabs, proj_array, vectors)


def gate_kernel(extra, mh_ref, x1_ref, w_ref, vec_ref, cols_ref, *refs):
    mixed_ref, x2_ref, n3_ref, lin_ref, sig_ref, g_ref = refs[extra:]
    step = pl.program_id(0)

    @pl.when(step == 0)
    def _():
        mixed = heads_of(mh_ref, 0, DH)
        mixed_ref[...] = mixed
        x2 = x1_ref[...] + dot_nn(mixed, square(w_ref))
        x2_ref[...] = x2
        normed, _ = norm_stats(x2)
        n3_ref[...] = (normed * vec_ref[0:1, :] + vec_ref[1:2, :]).astype(BF)

    @pl.when(step == 1)
    def _():
        lin_ref[...] = dot_nn(n3_ref[...], square(w_ref))

    @pl.when(step == 2)
    def _():
        sig = jax.nn.sigmoid(dot_nn(n3_ref[...], square(w_ref)))
        sig_ref[...] = sig
        g_ref[...] = (lin_ref[...] * sig * cols_ref[:, KSIZE : KSIZE + 1]).astype(BF)


def gate_call(mixed_heads, x1, weights, vectors, columns, order=()):
    frames, width = x1.shape
    fixed = lambda *shape: pl.BlockSpec(shape, lambda j: (0,) * len(shape))
    array, block = weights.blocks(lambda j: j, 3)
    return pl.pallas_call(
        functools.partial(gate_kernel, len(order)),
        grid=(3,),
        in_specs=[
            fixed(*mixed_heads.shape),
            fixed(frames, width),
            block,
            fixed(*vectors.shape),
            fixed(*columns.shape),
        ]
        + [pl.BlockSpec(memory_space=pl.ANY)] * len(order),
        out_specs=[fixed(frames, width)] * 6,
        out_shape=[jax.ShapeDtypeStruct((frames, width), t) for t in (BF, F32, BF, F32, F32, BF)],
        compiler_params=pltpu.CompilerParams(vmem_limit_bytes=VMEM_BYTES),
        cost_estimate=pl.CostEstimate(
            flops=6 * frames * width * width,
            bytes_accessed=6 * width * width + 24 * frames * width,
            transcendentals=frames * width,
        ),
        name="attention_out_and_gate",
    )(mixed_heads, x1, array, vectors, columns, *order)


PAD = 8


def lay_out(scratch, before, cells, after):
    frames = cells.shape[0]
    scratch[PAD - REACH : PAD, :] = before
    scratch[PAD : PAD + frames, :] = cells
    scratch[PAD + frames : PAD + frames + REACH, :] = after


def conv_kernel(g_ref, before_ref, after_ref, vec_ref, cols_ref, conv_ref, sums_ref, ext):
    frames = g_ref.shape[0]
    lay_out(
        ext, before_ref[...].astype(F32), g_ref[...].astype(F32), after_ref[...].astype(F32)
    )
    conv = jnp.zeros(g_ref.shape, F32)
    for m in range(KSIZE):
        rows = ext[PAD - REACH + m : PAD - REACH + m + frames, :]
        conv = conv + vec_ref[m : m + 1, :] * rows * cols_ref[:, m : m + 1]
    conv_ref[...] = conv
    counted = conv * cols_ref[:, KSIZE : KSIZE + 1]
    sums = jnp.concatenate(
        [jnp.sum(counted, axis=0, keepdims=True), jnp.sum(counted * conv, axis=0, keepdims=True)]
    )
    sums_ref[...] = jnp.broadcast_to(sums[None], sums_ref.shape)


def conv_call(g, before, after, taps, columns, devices):
    frames, width = g.shape
    return pl.pallas_call(
        conv_kernel,
        out_shape=[
            jax.ShapeDtypeStruct((frames, width), F32),
            jax.ShapeDtypeStruct((devices, 2, width), F32),
        ],
        scratch_shapes=[pltpu.VMEM((frames + 2 * PAD, width), F32)],
        compiler_params=pltpu.CompilerParams(vmem_limit_bytes=VMEM_BYTES),
        cost_estimate=pl.CostEstimate(
            flops=20 * frames * width, bytes_accessed=8 * frames * width, transcendentals=0
        ),
        name="depthwise",
    )(g, before, after, taps, columns)


def batch_stats(moments_ref, count):
    sums = jnp.sum(moments_ref[...], axis=0)
    mean = sums[0:1, :] / count
    return mean, lax.rsqrt(sums[1:2, :] / count - mean * mean + EPSILON)


def second_kernel(
    core_ref,
    x2_ref,
    conv_ref,
    mom_ref,
    wc_ref,
    w1_ref,
    w2_ref,
    vec_ref,
    og_ref,
    out_ref,
    swish_ref,
    dx_ref,
    ew_ref,
    dz_ref,
    sums_ref,
    spread_ref,
    pack_ref,
    s_own_ref,
    da_own_ref,
    x3_ref,
    acc_ref,
    d_ref,
    dsilu_ref,
    s_ref,
    dx4_ref,
):
    step = pl.program_id(0)
    count = vec_ref[6:7, :]

    @pl.when(step == 0)
    def _():
        mean, inv = batch_stats(mom_ref, count)
        z = (conv_ref[...] - mean) * inv * vec_ref[0:1, :] + vec_ref[1:2, :]
        sig = jax.nn.sigmoid(z)
        swish = (z * sig).astype(BF)
        swish_ref[...] = swish
        dsilu_ref[...] = sig * (1.0 + z * (1.0 - sig))
        x3 = x2_ref[...] + dot_nn(swish, square(wc_ref))
        x3_ref[...] = x3
        normed, _ = norm_stats(x3)
        pack_ref[0] = (normed * vec_ref[2:3, :] + vec_ref[3:4, :]).astype(BF)
        acc_ref[...] = jnp.zeros_like(acc_ref)

    @pl.when(step < 4)
    def _():
        acc_ref[...] += forward_slab(pack_ref[0], w1_ref, w2_ref, s_ref, d_ref.at[step])
        keep_slab(step, s_ref[...], pack_ref, 1, s_own_ref)

    @pl.when(step == 3)
    def _():
        normed, inv_std = norm_stats(x3_ref[...] + 0.5 * acc_ref[...])
        gain = vec_ref[4:5, :]
        out_ref[...] = (normed * gain + vec_ref[5:6, :]).astype(BF)
        upstream = og_ref[...].astype(F32)
        dx4 = norm_back(upstream, normed, inv_std, gain)
        dx4_ref[...] = dx4
        pack_ref[3] = (0.5 * dx4).astype(BF)
        sums_ref[0:1, :] = jnp.sum(upstream * normed, axis=0, keepdims=True)
        sums_ref[1:2, :] = jnp.sum(upstream, axis=0, keepdims=True)
        acc_ref[...] = jnp.zeros_like(acc_ref)

    @pl.when(step >= 4)
    def _():
        acc_ref[...] += backward_slab(pack_ref[3], w1_ref, w2_ref, d_ref.at[step - 4], s_ref)
        keep_slab(step - 4, s_ref[...], pack_ref, 4, da_own_ref)

    @pl.when(step == 7)
    def _():
        normed, inv_std = norm_stats(x3_ref[...])
        dn = acc_ref[...]
        dx3 = dx4_ref[...] + norm_back(dn, normed, inv_std, vec_ref[2:3, :])
        dx_ref[...] = dx3
        sums_ref[2:3, :] = jnp.sum(dn * normed, axis=0, keepdims=True)
        sums_ref[3:4, :] = jnp.sum(dn, axis=0, keepdims=True)
        ew = dx3.astype(BF)
        ew_ref[...] = ew
        dz = dot_nt(ew, square(wc_ref)) * dsilu_ref[...]
        dz_ref[...] = dz
        mean, inv = batch_stats(mom_ref, count)
        zhat = (conv_ref[...] - mean) * inv
        totals = jnp.concatenate(
            [jnp.sum(dz * zhat, axis=0, keepdims=True), jnp.sum(dz, axis=0, keepdims=True)]
        )
        sums_ref[4:6, :] = totals
        sums_ref[6:8, :] = jnp.zeros((2, dz.shape[1]), F32)
        spread_ref[...] = jnp.broadcast_to(totals[None], spread_ref.shape)


def second_call(core, x2, conv, moments, weights, gathered, rows, vectors, out_grad):
    frames, width = x2.shape
    fixed = lambda *shape: pl.BlockSpec(shape, lambda j, c: (0,) * len(shape))
    slabs, slab_blocks = slab_specs(gathered, rows, lambda j: j % 4)
    array, block = weights.blocks(lambda j: 0, 1)
    whole = fixed(frames, width)
    return pl.pallas_call(
        second_kernel,
        grid_spec=pltpu.PrefetchScalarGridSpec(
            num_scalar_prefetch=1,
            grid=(8,),
            in_specs=[whole, whole, fixed(*moments.shape), block]
            + slab_blocks
            + [fixed(*vectors.shape), whole],
            out_specs=[
                whole,
                whole,
                whole,
                whole,
                whole,
                fixed(8, width),
                fixed(*moments.shape),
                fixed(6, frames, width),
                pl.BlockSpec((1, frames, width), lambda j, c: (jnp.clip(j - 2, 0, 1), 0, 0)),
                pl.BlockSpec((1, frames, width), lambda j, c: (jnp.clip(j - 6, 0, 1), 0, 0)),
            ],
            scratch_shapes=[
                pltpu.VMEM((frames, width), F32),
                pltpu.VMEM((frames, width), F32),
                pltpu.VMEM((4, frames, width), BF),
                pltpu.VMEM((frames, width), F32),
                pltpu.VMEM((frames, width), BF),
                pltpu.VMEM((frames, width), F32),
            ],
        ),
        out_shape=[
            jax.ShapeDtypeStruct((frames, width), BF),
            jax.ShapeDtypeStruct((frames, width), BF),
            jax.ShapeDtypeStruct((frames, width), F32),
            jax.ShapeDtypeStruct((frames, width), BF),
            jax.ShapeDtypeStruct((frames, width), F32),
            jax.ShapeDtypeStruct((8, width), F32),
            jax.ShapeDtypeStruct(moments.shape, F32),
            jax.ShapeDtypeStruct((6, frames, width), BF),
            jax.ShapeDtypeStruct((2, frames, width), BF),
            jax.ShapeDtypeStruct((2, frames, width), BF),
        ],
        compiler_params=pltpu.CompilerParams(vmem_limit_bytes=VMEM_BYTES),
        cost_estimate=pl.CostEstimate(
            flops=36 * frames * width * width,
            bytes_accessed=34 * width * width + 40 * frames * width,
            transcendentals=5 * frames * width,
        ),
        name="second_part",
    )(core, x2, conv, moments, array, *slabs, vectors, out_grad)


def back_kernel(
    extra,
    dz_ref,
    conv_ref,
    edge_before_ref,
    edge_after_ref,
    g_ref,
    g_before_ref,
    g_after_ref,
    mom_ref,
    tot_ref,
    lin_ref,
    sig_ref,
    x2_ref,
    dx3_ref,
    w_ref,
    vec_ref,
    cols_ref,
    *refs,
):
    pg_ref, dx2_ref, ey_ref, do_ref, sums_ref, ext, g_ext, acc_ref, b_ref = refs[extra:]
    step = pl.program_id(0)
    frames, width = dz_ref.shape

    @pl.when(step == 0)
    def _():
        count = vec_ref[8:9, :]
        gain = vec_ref[5:6, :]
        mean, inv = batch_stats(mom_ref, count)
        totals = jnp.sum(tot_ref[...], axis=0) * gain

        def conv_grad(dz, conv, valid):
            zhat = (conv - mean) * inv
            dc = inv * (dz * gain - valid * (totals[1:2, :] + zhat * totals[0:1, :]) / count)
            return dc.astype(BF).astype(F32)

        valid = cols_ref[:, KSIZE : KSIZE + 1]
        dc = conv_grad(dz_ref[...], conv_ref[...], valid)
        edges = []
        for at, ref in ((0, edge_before_ref), (REACH, edge_after_ref)):
            edges.append(
                conv_grad(
                    ref[0:REACH, :],
                    ref[REACH : 2 * REACH, :],
                    cols_ref[at : at + REACH, KSIZE + 1 : KSIZE + 2],
                )
            )
        lay_out(ext, edges[0], dc, edges[1])
        lay_out(
            g_ext,
            g_before_ref[...].astype(F32),
            g_ref[...].astype(F32),
            g_after_ref[...].astype(F32),
        )
        dg = jnp.zeros((frames, width), F32)
        for m in range(KSIZE):
            back = 2 * REACH - m
            rows = ext[PAD - REACH + back : PAD - REACH + back + frames, :]
            dg = dg + vec_ref[m : m + 1, :] * rows * cols_ref[:, back : back + 1]
            there = g_ext[PAD - REACH + m : PAD - REACH + m + frames, :]
            sums_ref[2 + m : 3 + m, :] = jnp.sum(
                dc * there * cols_ref[:, m : m + 1], axis=0, keepdims=True
            )
        sums_ref[7:8, :] = jnp.zeros((1, width), F32)
        de = dg * valid
        sig = sig_ref[...]
        pa = (de * sig).astype(BF)
        pb = (de * lin_ref[...] * sig * (1.0 - sig)).astype(BF)
        pg_ref[:, :width] = pa
        pg_ref[:, width:] = pb
        b_ref[...] = pb
        acc_ref[...] = dot_nt(pa, square(w_ref))

    @pl.when(step == 1)
    def _():
        dn = acc_ref[...] + dot_nt(b_ref[...], square(w_ref))
        normed, inv_std = norm_stats(x2_ref[...])
        dx2 = dx3_ref[...] + norm_back(dn, normed, inv_std, vec_ref[6:7, :])
        dx2_ref[...] = dx2
        ey_ref[...] = dx2.astype(BF)
        sums_ref[0:1, :] = jnp.sum(dn * normed, axis=0, keepdims=True)
        sums_ref[1:2, :] = jnp.sum(dn, axis=0, keepdims=True)

    @pl.when(step == 2)
    def _():
        grads = dot_nt(ey_ref[...], square(w_ref)).astype(BF)
        for h in range(do_ref.shape[0]):
            do_ref[h] = grads[:, h * DH : (h + 1) * DH]


def back_call(dz, conv, edges, g, g_edges, moments, totals, lin, sig, x2, dx3, weights, vectors, columns, order):
    frames, width = dz.shape
    fixed = lambda *shape: pl.BlockSpec(shape, lambda j: (0,) * len(shape))
    array, block = weights.blocks(lambda j: (j + 1) % 3, 3)
    whole = fixed(frames, width)
    return pl.pallas_call(
        functools.partial(back_kernel, len(order)),
        grid=(3,),
        in_specs=[
            whole,
            whole,
            fixed(2 * REACH, width),
            fixed(2 * REACH, width),
            whole,
            fixed(REACH, width),
            fixed(REACH, width),
            fixed(*moments.shape),
            fixed(*totals.shape),
            whole,
            whole,
            whole,
            whole,
            block,
            fixed(*vectors.shape),
            fixed(*columns.shape),
        ]
        + [pl.BlockSpec(memory_space=pl.ANY)] * len(order),
        out_specs=[
            fixed(frames, 2 * width),
            whole,
            whole,
            fixed(width // DH, frames, DH),
            fixed(8, width),
        ],
        out_shape=[
            jax.ShapeDtypeStruct((frames, 2 * width), BF),
            jax.ShapeDtypeStruct((frames, width), F32),
            jax.ShapeDtypeStruct((frames, width), BF),
            jax.ShapeDtypeStruct((width // DH, frames, DH), BF),
            jax.ShapeDtypeStruct((8, width), F32),
        ],
        scratch_shapes=[
            pltpu.VMEM((frames + 2 * PAD, width), F32),
            pltpu.VMEM((frames + 2 * PAD, width), F32),
            pltpu.VMEM((frames, width), F32),
            pltpu.VMEM((frames, width), BF),
        ],
        compiler_params=pltpu.CompilerParams(vmem_limit_bytes=VMEM_BYTES),
        cost_estimate=pl.CostEstimate(
            flops=6 * frames * width * width,
            bytes_accessed=6 * width * width + 34 * frames * width,
            transcendentals=0,
        ),
        name="convolution_backward",
    )(
        dz,
        conv,
        edges[0],
        edges[1],
        g,
        g_edges[0],
        g_edges[1],
        moments,
        totals,
        lin,
        sig,
        x2,
        dx3,
        array,
        vectors,
        columns,
        *order,
    )


def proj_back_kernel(extra, dq_ref, dkv_ref, dx2_ref, x1_ref, wp_ref, vec_ref, *refs):
    dx1_ref, ef_ref, sums_ref, acc_ref = refs[extra:]
    step = pl.program_id(0)

    @pl.when(step == 0)
    def _():
        dq = heads_of(dq_ref, 0, DH)
        acc_ref[...] = dot_nt(dq, square(wp_ref))
        sums_ref[2:3, :] = jnp.sum(dq.astype(F32), axis=0, keepdims=True)
        sums_ref[3:8, :] = jnp.zeros((5, dq.shape[1]), F32)

    @pl.when(step == 1)
    def _():
        acc_ref[...] += dot_nt(heads_of(dkv_ref, 0, DH), square(wp_ref))

    @pl.when(step == 2)
    def _():
        dn = acc_ref[...] + dot_nt(heads_of(dkv_ref, DH, 2 * DH), square(wp_ref))
        normed, inv_std = norm_stats(x1_ref[...])
        dx1 = dx2_ref[...] + norm_back(dn, normed, inv_std, vec_ref[1:2, :])
        dx1_ref[...] = dx1
        ef_ref[0] = (0.5 * dx1).astype(BF)
        sums_ref[0:1, :] = jnp.sum(dn * normed, axis=0, keepdims=True)
        sums_ref[1:2, :] = jnp.sum(dn, axis=0, keepdims=True)


def proj_back_call(dq, dkv, dx2, x1, proj, vectors, order):
    frames, width = x1.shape
    fixed = lambda *shape: pl.BlockSpec(shape, lambda j: (0,) * len(shape))
    array, block = proj.blocks(lambda j: j, 3)
    whole = fixed(frames, width)
    return pl.pallas_call(
        functools.partial(proj_back_kernel, len(order)),
        grid=(3,),
        in_specs=[fixed(*dq.shape), fixed(*dkv.shape), whole, whole, block, fixed(*vectors.shape)]
        + [pl.BlockSpec(memory_space=pl.ANY)] * len(order),
        out_specs=[whole, fixed(1, frames, width), fixed(8, width)],
        out_shape=[
            jax.ShapeDtypeStruct((frames, width), F32),
            jax.ShapeDtypeStruct((1, frames, width), BF),
            jax.ShapeDtypeStruct((8, width), F32),
        ],
        scratch_shapes=[pltpu.VMEM((frames, width), F32)],
        compiler_params=pltpu.CompilerParams(vmem_limit_bytes=VMEM_BYTES),
        cost_estimate=takes(9),
        name="projections_backward",
    )(dq, dkv, dx2, x1, array, vectors, *order)


def last_kernel(extra, core_ref, dx1_ref, ef_ref, x_ref, w1_ref, w2_ref, d_ref, vec_ref, *refs):
    gin_ref, sums_ref, first_ref, second_ref, own_ref, acc_ref, da_ref = refs[extra:]
    step = pl.program_id(0)

    @pl.when(step == 0)
    def _():
        acc_ref[...] = jnp.zeros_like(acc_ref)

    acc_ref[...] += backward_slab(ef_ref[0], w1_ref, w2_ref, d_ref.at[0], da_ref)
    for at, ref in enumerate((first_ref, second_ref)):

        @pl.when(step == at)
        def _():
            ref[0] = da_ref[...]

    @pl.when(step >= 2)
    def _():
        own_ref[0] = da_ref[...]

    @pl.when(step == 3)
    def _():
        normed, inv_std = norm_stats(x_ref[...].astype(F32))
        dn = acc_ref[...]
        dx = dx1_ref[...] + norm_back(dn, normed, inv_std, vec_ref[0:1, :])
        gin_ref[...] = dx.astype(BF)
        sums_ref[0:1, :] = jnp.sum(dn * normed, axis=0, keepdims=True)
        sums_ref[1:2, :] = jnp.sum(dn, axis=0, keepdims=True)
        sums_ref[2:8, :] = jnp.zeros((6, dn.shape[1]), F32)


def last_call(core, dx1, ef, x, gathered, rows, slope, vectors, order):
    frames, width = x.shape
    fixed = lambda *shape: pl.BlockSpec(shape, lambda j, c: (0,) * len(shape))
    slabs, slab_blocks = slab_specs(gathered, rows, lambda j: j)
    whole = fixed(frames, width)
    return pl.pallas_call(
        functools.partial(last_kernel, len(order)),
        grid_spec=pltpu.PrefetchScalarGridSpec(
            num_scalar_prefetch=1,
            grid=(4,),
            in_specs=[whole, fixed(1, frames, width), whole]
            + slab_blocks
            + [pl.BlockSpec((1, frames, width), lambda j, c: (j, 0, 0)), fixed(*vectors.shape)]
            + [pl.BlockSpec(memory_space=pl.ANY)] * len(order),
            out_specs=[
                whole,
                fixed(8, width),
                fixed(1, frames, width),
                fixed(1, frames, width),
                pl.BlockSpec((1, frames, width), lambda j, c: (jnp.clip(j - 2, 0, 1), 0, 0)),
            ],
            scratch_shapes=[pltpu.VMEM((frames, width), F32), pltpu.VMEM((frames, width), BF)],
        ),
        out_shape=[
            jax.ShapeDtypeStruct((frames, width), BF),
            jax.ShapeDtypeStruct((8, width), F32),
            jax.ShapeDtypeStruct((1, frames, width), BF),
            jax.ShapeDtypeStruct((1, frames, width), BF),
            jax.ShapeDtypeStruct((2, frames, width), BF),
        ],
        compiler_params=pltpu.CompilerParams(vmem_limit_bytes=VMEM_BYTES),
        cost_estimate=takes(15),
        name="last_part",
    )(core, dx1, ef, x, *slabs, slope, vectors, *order)


def fill_window(kv_ref, parts):
    for column, refs in ((0, parts[:3]), (DH, parts[3:])):
        at = 0
        for ref in refs:
            kv_ref[at : at + ref.shape[0], column : column + DH] = ref[...]
            at += ref.shape[0]
    kv_ref[at:, :] = jnp.zeros((kv_ref.shape[0] - at, kv_ref.shape[1]), kv_ref.dtype)


def attn_fwd_kernel(
    origin,
    low_ref,
    high_ref,
    c2_ref,
    q_ref,
    *refs,
):
    lo_ref, hi_ref, o_ref, lse_ref, kv_ref = refs[6:]
    block = pl.program_id(0)

    @pl.when(block == 0)
    def _():
        fill_window(kv_ref, refs[:6])

    rows = q_ref.shape[0]
    q = q_ref[...]
    c1 = LOG2E * DH**-0.5
    c2 = c2_ref[0]
    at = lax.broadcasted_iota(jnp.int32, (1, rows), 1) + (origin + block * rows)
    q_pos = at.astype(F32)
    lo_q, hi_q = lo_ref[...], hi_ref[...]
    first = low_ref[block]
    steps = (high_ref[block] - first + (BK - 1)) // BK

    def step(t, carry):
        top, total, mixed = carry
        start = pl.multiple_of(first + t * BK, 128)
        k = kv_ref[pl.ds(start, BK), :DH]
        v = kv_ref[pl.ds(start, BK), DH:]
        k_pos = (lax.broadcasted_iota(jnp.int32, (BK, 1), 0) + start).astype(F32)
        scores = dot_nt(k, q) * c1 - jnp.abs(k_pos - q_pos) * c2
        scores = jnp.where((k_pos >= lo_q) & (k_pos < hi_q), scores, MASKED)
        new_top = jnp.maximum(top, jnp.max(scores, axis=0, keepdims=True))
        expo = jnp.exp2(scores - new_top)
        keep = jnp.exp2(top - new_top)
        total = total * keep + jnp.sum(expo, axis=0, keepdims=True)
        mixed = mixed * keep + dot_tn(v, expo.astype(BF))
        return new_top, total, mixed

    top, total, mixed = lax.fori_loop(
        0,
        steps,
        step,
        (
            jnp.full((1, rows), MASKED, F32),
            jnp.zeros((1, rows), F32),
            jnp.zeros((DH, rows), F32),
        ),
    )
    o_ref[...] = (mixed / total).T.astype(BF)
    lse_ref[...] = top + jnp.log2(total)


def attn_fwd(q, kv, low, high, c2, lo_q, hi_q, origin):
    frames = q.shape[0]
    window = sum(v.shape[0] for v in kv[:3]) + BK
    parts = [pl.BlockSpec(v.shape, lambda i, *_: (0, 0)) for v in kv]
    blocks = frames // BQ
    pairs = frames * 1024 * DH
    grid_spec = pltpu.PrefetchScalarGridSpec(
        num_scalar_prefetch=3,
        grid=(blocks,),
        in_specs=[
            pl.BlockSpec((BQ, DH), lambda i, *_: (i, 0)),
            *parts,
            pl.BlockSpec((1, BQ), lambda i, *_: (0, i)),
            pl.BlockSpec((1, BQ), lambda i, *_: (0, i)),
        ],
        out_specs=[
            pl.BlockSpec((BQ, DH), lambda i, *_: (i, 0)),
            pl.BlockSpec((1, BQ), lambda i, *_: (0, i)),
        ],
        scratch_shapes=[pltpu.VMEM((window, 2 * DH), BF)],
    )

    def kernel(*refs):
        attn_fwd_kernel(origin, *refs)

    return pl.pallas_call(
        kernel,
        grid_spec=grid_spec,
        out_shape=[
            jax.ShapeDtypeStruct((frames, DH), BF),
            jax.ShapeDtypeStruct((1, frames), F32),
        ],
        compiler_params=pltpu.CompilerParams(vmem_limit_bytes=VMEM_BYTES),
        cost_estimate=pl.CostEstimate(
            flops=4 * pairs, bytes_accessed=4 * window * DH, transcendentals=frames * 1024
        ),
        name="attention_forward",
    )(low, high, c2, q, *kv, lo_q, hi_q)


def attn_bwd_kernel(
    origin,
    extra,
    low_ref,
    high_ref,
    c2_ref,
    q_ref,
    o_ref,
    do_ref,
    lse_ref,
    lo_ref,
    hi_ref,
    *refs,
):
    dq_ref, prev_ref, own_ref, next_ref, dk_acc, dv_acc, kv_ref = refs[6 + extra :]
    block = pl.program_id(0)
    rows = q_ref.shape[0]
    frames = own_ref.shape[0]
    scale = DH**-0.5
    c1 = LOG2E * scale

    @pl.when(block == 0)
    def _():
        fill_window(kv_ref, refs[:6])
        dk_acc[...] = jnp.zeros_like(dk_acc)
        dv_acc[...] = jnp.zeros_like(dv_acc)

    q = q_ref[...]
    do = do_ref[...]
    c2 = c2_ref[0]
    delta = jnp.sum((o_ref[...].astype(F32) * do.astype(F32)).T, axis=0, keepdims=True)
    lse = lse_ref[...]
    at = lax.broadcasted_iota(jnp.int32, (1, rows), 1) + (origin + block * rows)
    q_pos = at.astype(F32)
    lo_q, hi_q = lo_ref[...], hi_ref[...]
    first = low_ref[block]
    steps = (high_ref[block] - first + (BK - 1)) // BK

    def step(t, dq):
        start = pl.multiple_of(first + t * BK, 128)
        here = pl.ds(start, BK)
        k = kv_ref[here, :DH]
        v = kv_ref[here, DH:]
        k_pos = (lax.broadcasted_iota(jnp.int32, (BK, 1), 0) + start).astype(F32)
        scores = dot_nt(k, q) * c1 - jnp.abs(k_pos - q_pos) * c2 - lse
        scores = jnp.where((k_pos >= lo_q) & (k_pos < hi_q), scores, MASKED)
        probs = jnp.exp2(scores)
        grads = (probs * (dot_nt(v, do) - delta)).astype(BF)
        dv_acc[here, :] += dot_nn(probs.astype(BF), do)
        dk_acc[here, :] += dot_nn(grads, q)
        return dq + dot_tn(k, grads)

    dq = lax.fori_loop(0, steps, step, jnp.zeros((DH, rows), F32))
    dq_ref[...] = (dq * scale).T.astype(BF)

    @pl.when(block == pl.num_programs(0) - 1)
    def _():
        prev_ref[:, :DH] = (dk_acc[:origin, :] * scale).astype(BF)
        prev_ref[:, DH:] = dv_acc[:origin, :].astype(BF)
        own_ref[:, :DH] = dk_acc[origin : origin + frames, :] * scale
        own_ref[:, DH:] = dv_acc[origin : origin + frames, :]
        next_ref[:, :DH] = (dk_acc[origin + frames : 2 * origin + frames, :] * scale).astype(BF)
        next_ref[:, DH:] = dv_acc[origin + frames : 2 * origin + frames, :].astype(BF)


def attn_bwd(q, o, do, lse, kv, low, high, c2, lo_q, hi_q, origin, order=()):
    frames = q.shape[0]
    blocks = frames // BQ
    pairs = frames * 1024 * DH
    window = sum(v.shape[0] for v in kv[:3]) + BK
    parts = [pl.BlockSpec(v.shape, lambda i, *_: (0, 0)) for v in kv]
    tile = pl.BlockSpec((BQ, DH), lambda i, *_: (i, 0))
    row = pl.BlockSpec((1, BQ), lambda i, *_: (0, i))
    grid_spec = pltpu.PrefetchScalarGridSpec(
        num_scalar_prefetch=3,
        grid=(blocks,),
        in_specs=[
            tile,
            tile,
            tile,
            row,
            row,
            row,
            *parts,
        ]
        + [pl.BlockSpec(memory_space=pl.ANY)] * len(order),
        out_specs=[
            tile,
            pl.BlockSpec((origin, 2 * DH), lambda i, *_: (0, 0)),
            pl.BlockSpec((frames, 2 * DH), lambda i, *_: (0, 0)),
            pl.BlockSpec((origin, 2 * DH), lambda i, *_: (0, 0)),
        ],
        scratch_shapes=[
            pltpu.VMEM((window, DH), F32),
            pltpu.VMEM((window, DH), F32),
            pltpu.VMEM((window, 2 * DH), BF),
        ],
    )

    def kernel(*refs):
        attn_bwd_kernel(origin, len(order), *refs)

    return pl.pallas_call(
        kernel,
        grid_spec=grid_spec,
        out_shape=[
            jax.ShapeDtypeStruct((frames, DH), BF),
            jax.ShapeDtypeStruct((origin, 2 * DH), BF),
            jax.ShapeDtypeStruct((frames, 2 * DH), F32),
            jax.ShapeDtypeStruct((origin, 2 * DH), BF),
        ],
        compiler_params=pltpu.CompilerParams(vmem_limit_bytes=VMEM_BYTES),
        cost_estimate=pl.CostEstimate(
            flops=80 * pairs, bytes_accessed=8 * window * DH, transcendentals=frames * 1024
        ),
        name="attention_backward",
    )(low, high, c2, q, o, do, lse, lo_q, hi_q, *kv, *order)


def pass_on_kernel(extra, *refs):
    count = (len(refs) - extra) // 2
    for a, b in zip(refs[:count], refs[count + extra :]):
        b[...] = a[...]


def pass_on(arrays, order):
    return pl.pallas_call(
        functools.partial(pass_on_kernel, len(order)),
        in_specs=[pl.BlockSpec(v.shape, lambda n=v.ndim: (0,) * n) for v in arrays]
        + [pl.BlockSpec(memory_space=pl.ANY)] * len(order),
        out_specs=[pl.BlockSpec(v.shape, lambda n=v.ndim: (0,) * n) for v in arrays],
        out_shape=[jax.ShapeDtypeStruct(v.shape, v.dtype) for v in arrays],
        compiler_params=pltpu.CompilerParams(vmem_limit_bytes=VMEM_BYTES // 3),
        cost_estimate=pl.CostEstimate(flops=1, bytes_accessed=1024, transcendentals=0),
        name="pass_on",
    )(*arrays, *order)


def join_kernel(extra, own_ref, before_ref, after_ref, *refs):
    out_ref = refs[extra]
    span = before_ref.shape[0]
    rows = own_ref.shape[0]
    out_ref[:span, :] = (own_ref[:span, :] + before_ref[...].astype(F32)).astype(BF)
    if rows > 2 * span:
        out_ref[span : rows - span, :] = own_ref[span : rows - span, :].astype(BF)
    out_ref[rows - span :, :] = (own_ref[rows - span :, :] + after_ref[...].astype(F32)).astype(BF)


def join_edges(own, before, after, order=()):
    return pl.pallas_call(
        functools.partial(join_kernel, len(order)),
        in_specs=[pl.BlockSpec(v.shape, lambda: (0, 0)) for v in (own, before, after)]
        + [pl.BlockSpec(memory_space=pl.ANY)] * len(order),
        out_specs=pl.BlockSpec(own.shape, lambda: (0, 0)),
        out_shape=jax.ShapeDtypeStruct(own.shape, BF),
        compiler_params=pltpu.CompilerParams(vmem_limit_bytes=VMEM_BYTES // 2),
        cost_estimate=pl.CostEstimate(
            flops=own.size, bytes_accessed=8 * own.size, transcendentals=0
        ),
        name="join_edges",
    )(own, before, after, *order)


def stack_kernel(extra, places, arrays, *refs):
    out_ref = refs[arrays + extra]
    rows_ref = refs[arrays + extra + 1]
    for at, (source, row) in enumerate(places):
        rows_ref[at : at + 1, :] = refs[source][row : row + 1, :]
    share = out_ref.shape[2]
    rows = rows_ref[...]
    for i in range(out_ref.shape[0]):
        out_ref[i] = rows[:, i * share : (i + 1) * share]


def stack_rows(arrays, places, devices, order=()):
    width = arrays[0].shape[1]
    share = width // devices
    if share % 32:
        rows = jnp.stack([arrays[source][row] for source, row in places])
        return rows.reshape(len(places), devices, share).transpose(1, 0, 2)
    return pl.pallas_call(
        functools.partial(stack_kernel, len(order), places, len(arrays)),
        in_specs=[pl.BlockSpec(v.shape, lambda: (0, 0)) for v in arrays]
        + [pl.BlockSpec(memory_space=pl.ANY)] * len(order),
        out_specs=pl.BlockSpec((devices, len(places), share), lambda: (0, 0, 0)),
        out_shape=jax.ShapeDtypeStruct((devices, len(places), share), F32),
        scratch_shapes=[pltpu.VMEM((len(places), width), F32)],
        name="stack_rows",
    )(*arrays, *order)


def halve_kernel(extra, sel_ref, kept_a, kept_b, got_a, got_b, *refs):
    send_ref, keep_ref = refs[extra:]
    send_ref[...] = (kept_a[0].astype(F32) + got_a[0].astype(F32)).astype(BF)
    keep_ref[...] = (kept_b[0].astype(F32) + got_b[0].astype(F32)).astype(BF)


def halve(kept, got, mine, order=()):
    count, _, rows, columns = kept.shape
    step = rows
    while step % 32 == 0 and step * columns > 512 * 1024:
        step //= 2
    block = (1, 1, step, columns)
    other = pl.BlockSpec(block, lambda i, j, m: (i, 1 - m[0], j, 0))
    own = pl.BlockSpec(block, lambda i, j, m: (i, m[0], j, 0))
    out = pl.BlockSpec((1, step, columns), lambda i, j, m: (i, j, 0))
    return pl.pallas_call(
        functools.partial(halve_kernel, len(order)),
        grid_spec=pltpu.PrefetchScalarGridSpec(
            num_scalar_prefetch=1,
            grid=(count, rows // step),
            in_specs=[other, own, other, own]
            + [pl.BlockSpec(memory_space=pl.ANY)] * len(order),
            out_specs=[out, out],
        ),
        out_shape=[jax.ShapeDtypeStruct((count, rows, columns), BF)] * 2,
        compiler_params=pltpu.CompilerParams(vmem_limit_bytes=VMEM_BYTES // 3),
        cost_estimate=pl.CostEstimate(flops=1024, bytes_accessed=1024, transcendentals=0),
        name="halve",
    )(mine.astype(jnp.int32)[None], kept, kept, got, got, *order)


def finish_kernel(extra, turned, kept_ref, got_ref, *refs):
    total = kept_ref[...].astype(F32) + got_ref[...].astype(F32)
    refs[extra][...] = total.T if turned else total


def finish(kept, got, turned=False, order=()):
    rows, columns = kept.shape
    fixed = pl.BlockSpec((rows, columns), lambda: (0, 0))
    shape = (columns, rows) if turned else (rows, columns)
    if turned and rows % 128:
        return finish(kept, got, False, order).T
    return pl.pallas_call(
        functools.partial(finish_kernel, len(order), turned),
        in_specs=[fixed, fixed] + [pl.BlockSpec(memory_space=pl.ANY)] * len(order),
        out_specs=pl.BlockSpec(shape, lambda: (0, 0)),
        out_shape=jax.ShapeDtypeStruct(shape, F32),
        compiler_params=pltpu.CompilerParams(vmem_limit_bytes=VMEM_BYTES // 3),
        name="finish",
    )(kept, got, *order)


def halve_both_kernel(extra, sel_ref, *refs):
    send_ref, keep_ref = refs[8 + extra :]
    for i in (0, 1):
        kept_a, kept_b, got_a, got_b = refs[4 * i : 4 * i + 4]
        rows = kept_a.shape[2]
        here = slice(i * rows, (i + 1) * rows)
        send_ref[0, here, :] = (kept_a[0, 0].astype(F32) + got_a[0, 0].astype(F32)).astype(BF)
        keep_ref[0, here, :] = (kept_b[0, 0].astype(F32) + got_b[0, 0].astype(F32)).astype(BF)


def halve_both(first, second, shape, mine, order=()):
    count, _, rows, columns = shape
    block = (1, 1, rows, columns)
    other = pl.BlockSpec(block, lambda i, m: (i, 1 - m[0], 0, 0))
    own = pl.BlockSpec(block, lambda i, m: (i, m[0], 0, 0))
    out = pl.BlockSpec((1, 2 * rows, columns), lambda i, m: (i, 0, 0))
    arrays = []
    for part in (first, second):
        kept, got = part.kept.reshape(shape), part.got.reshape(shape)
        arrays += [kept, kept, got, got]
    return pl.pallas_call(
        functools.partial(halve_both_kernel, len(order)),
        grid_spec=pltpu.PrefetchScalarGridSpec(
            num_scalar_prefetch=1,
            grid=(count,),
            in_specs=[other, own, other, own] * 2
            + [pl.BlockSpec(memory_space=pl.ANY)] * len(order),
            out_specs=[out, out],
        ),
        out_shape=[jax.ShapeDtypeStruct((count, 2 * rows, columns), BF)] * 2,
        compiler_params=pltpu.CompilerParams(vmem_limit_bytes=VMEM_BYTES // 3),
        cost_estimate=pl.CostEstimate(flops=1024, bytes_accessed=1024, transcendentals=0),
        name="halve_both",
    )(mine.astype(jnp.int32)[None], *arrays, *order)


def finish_both_kernel(extra, kept_ref, got_ref, *refs):
    first_ref, second_ref = refs[extra:]
    rows = first_ref.shape[0]
    total = kept_ref[...].astype(F32) + got_ref[...].astype(F32)
    first_ref[...] = total[:rows]
    second_ref[...] = total[rows:].T


def finish_both(total, rows, columns, order=()):
    kept, got = total.kept.reshape(2 * rows, columns), total.got.reshape(2 * rows, columns)
    if rows % 128:
        both = kept.astype(F32) + got.astype(F32)
        return both[:rows], both[rows:].T
    fixed = lambda *shape: pl.BlockSpec(shape, lambda: (0, 0))
    return pl.pallas_call(
        functools.partial(finish_both_kernel, len(order)),
        in_specs=[fixed(2 * rows, columns)] * 2
        + [pl.BlockSpec(memory_space=pl.ANY)] * len(order),
        out_specs=[fixed(rows, columns), fixed(columns, rows)],
        out_shape=[
            jax.ShapeDtypeStruct((rows, columns), F32),
            jax.ShapeDtypeStruct((columns, rows), F32),
        ],
        compiler_params=pltpu.CompilerParams(vmem_limit_bytes=VMEM_BYTES // 3),
        cost_estimate=pl.CostEstimate(flops=1024, bytes_accessed=1024, transcendentals=0),
        name="finish_both",
    )(kept, got, *order)


def total_kernel(extra, parts_ref, *refs):
    total = jnp.sum(parts_ref[...], axis=0)
    at = 0
    for ref in refs[extra:]:
        ref[...] = total[at : at + ref.shape[0]]
        at += ref.shape[0]


def total_of(parts, counts, order=()):
    columns = parts.shape[2]
    return pl.pallas_call(
        functools.partial(total_kernel, len(order)),
        in_specs=[pl.BlockSpec(parts.shape, lambda: (0, 0, 0))]
        + [pl.BlockSpec(memory_space=pl.ANY)] * len(order),
        out_specs=[pl.BlockSpec((n, columns), lambda: (0, 0)) for n in counts],
        out_shape=[jax.ShapeDtypeStruct((n, columns), F32) for n in counts],
        name="total_of",
    )(parts, *order)


class Sum:
    def __init__(self, kept, send, axis, bit):
        self.kept = kept
        self.send = send
        self.got = xor_send(send, axis, bit)

    def step(self, shape, axis, bit=1, order=()):
        mine = (lax.axis_index(axis) // bit) % 2
        send, kept = halve(self.kept.reshape(shape), self.got.reshape(shape), mine, order)
        return Sum(kept, send, axis, bit)

    def finish(self, shape, turned=False, order=()):
        return finish(self.kept.reshape(shape), self.got.reshape(shape), turned, order)


def slab_grad_kernel(split, extra, pair, sel_ref, la_ref, lb_ref, ra_ref, rb_ref, *refs):
    if pair:
        rb_ref = [jnp.where(pl.program_id(0) == 0, rb_ref[0], refs[0][0])]
        refs = refs[1:]
    out_ref = refs[extra]
    if split is None:
        out = dot_tn(la_ref[0], ra_ref[0]) + dot_tn(lb_ref[0], rb_ref[0])
    else:
        zs, rows = split
        take = [pl.ds(pl.multiple_of((z * 2 + sel_ref[0]) * rows, rows), rows) for z in range(zs)]
        left = [jnp.concatenate([ref[0, :, t] for t in take], axis=1) for ref in (la_ref, lb_ref)]
        out = dot_tn(left[0], ra_ref[0]) + dot_tn(left[1], rb_ref[0])
    out_ref[0] = out.astype(BF)


def slab_grad(left, right, x, y, order=(), lasting=0):
    left_a, left_b, left_at = left
    right_a, right_b, right_at = right
    pair = isinstance(right_b, tuple)
    _, frames, width = left_a.shape
    hidden = right_a.shape[2]
    zs = lax.axis_size("z")
    rows = width // (2 * zs)
    half = width // 2
    if x is None:
        split = None
        sel = y
        left_block = pl.BlockSpec((1, frames, half), lambda i, s: (left_at, 0, i))
        right = [
            pl.BlockSpec((1, frames, hidden), lambda i, s: (s[0], 0, 0)),
            pl.BlockSpec((1, frames, hidden), lambda i, s: (s[0] + right_at, 0, 0)),
        ]
    else:
        sel = x
        right = [
            pl.BlockSpec((1, frames, hidden), lambda i, s: (i, 0, 0)),
            pl.BlockSpec((1, frames, hidden), lambda i, s: (i + right_at, 0, 0)),
        ]
        if pair:
            right[1:] = [pl.BlockSpec((1, frames, hidden), lambda i, s: (0, 0, 0))] * 2
        if rows % 128 == 0:
            split = (zs, rows)
            left_block = pl.BlockSpec((1, frames, width), lambda i, s: (left_at, 0, 0))
        else:
            split = None
            left_block = pl.BlockSpec((1, frames, half), lambda i, s: (0, 0, 0))
            left_a, left_b = (
                pick(l[left_at].reshape(frames, zs, 2, rows), x, 2).reshape(1, frames, half)
                for l in (left_a, left_b)
            )
    return pl.pallas_call(
        functools.partial(slab_grad_kernel, split, len(order), pair),
        grid_spec=pltpu.PrefetchScalarGridSpec(
            num_scalar_prefetch=1,
            grid=(2,),
            in_specs=[left_block, left_block]
            + right
            + [pl.BlockSpec(memory_space=pl.ANY)] * len(order),
            out_specs=pl.BlockSpec((1, half, hidden), lambda i, s: (i, 0, 0)),
        ),
        out_shape=jax.ShapeDtypeStruct((2, half, hidden), BF),
        compiler_params=pltpu.CompilerParams(vmem_limit_bytes=VMEM_BYTES),
        cost_estimate=takes(lasting),
        name="slab_grad",
    )(sel.astype(jnp.int32)[None], left_a, left_b, right_a, *(right_b if pair else (right_b,)), *order)


def slab_sum(left, right, first, order=(), kept_order=()):
    place = lax.axis_index(first)
    picks = lambda i: (i, None) if first == "x" else (None, i)
    away = slab_grad(left, right, *picks(1 - place), order)
    return Sum(slab_grad(left, right, *picks(place), (away,) + tuple(kept_order)), away, first, 1)


def slab_second(total, first, order=()):
    zs = lax.axis_size("z")
    _, half, hidden = total.kept.shape
    if first == "x":
        return total.step((1, 2, half, hidden), "y", 1, order)
    return total.step((zs, 2, half // zs, hidden), "x", 1, order)


def z_steps(total, rows, columns, bits=None, order=()):
    zs = lax.axis_size("z")
    for bit in z_bits() if bits is None else bits:
        total = total.step((zs // (2 * bit), 2, rows, columns), "z", bit, order)
    return total


def z_both(first, second, rows, columns, order=()):
    zs = lax.axis_size("z")
    mine = lax.axis_index("z") % 2
    send, kept = halve_both(first, second, (zs // 2, 2, rows, columns), mine, order)
    return Sum(kept, send, "z", 1)


def z_bits():
    bits = []
    while 1 << len(bits) < lax.axis_size("z"):
        bits.append(1 << len(bits))
    return bits


def right_of(ref):
    if len(ref.shape) == 2:
        return ref[...]
    return jnp.concatenate([heads_of(ref, at, at + DH) for at in range(0, ref.shape[2], DH)], axis=1)


def row_grad_kernel(pairs, rows, core_ref, *refs):
    send_ref, keep_ref = refs[-2:]
    at = 0
    for i in range(pairs):
        whole = dot_tn(refs[2 * i][...], right_of(refs[2 * i + 1])).astype(BF)
        columns = whole.shape[1]
        parts = [whole[k * rows : (k + 1) * rows] for k in range(whole.shape[0] // rows)]
        even = jnp.concatenate(parts[0::2], axis=0)
        odd = jnp.concatenate(parts[1::2], axis=0)
        first = core_ref[0] == 0
        keep_ref[:, at : at + columns] = jnp.where(first, even, odd)
        send_ref[:, at : at + columns] = jnp.where(first, odd, even)
        at += columns


def row_grad(core, pairs, order=()):
    frames, width = pairs[0][0].shape
    zs = lax.axis_size("z")
    rows = width // (8 * zs)
    columns = sum(right.size // frames for _, right in pairs)
    if rows % 16:
        whole = jnp.concatenate(
            [dot_tn(left, right_of(right)).astype(BF) for left, right in pairs], axis=1
        )
        whole = whole.reshape(4 * zs, 2, rows, columns)
        flat = lambda v: v.reshape(width // 2, columns)
        return flat(pick(whole, 1 - core[0], 1)), flat(pick(whole, core[0], 1))
    tile = 256
    specs, args = [], []
    for left, right in pairs:
        specs += [
            pl.BlockSpec((frames, tile), lambda i, c: (0, i)),
            pl.BlockSpec(right.shape, lambda i, c, n=right.ndim: (0,) * n),
        ]
        args += [left, right]
    specs += [pl.BlockSpec(memory_space=pl.ANY)] * len(order)
    out = pl.BlockSpec((tile // 2, columns), lambda i, c: (i, 0))
    return pl.pallas_call(
        functools.partial(row_grad_kernel, len(pairs), rows),
        grid_spec=pltpu.PrefetchScalarGridSpec(
            num_scalar_prefetch=1, grid=(width // tile,), in_specs=specs, out_specs=[out, out]
        ),
        out_shape=[jax.ShapeDtypeStruct((width // 2, columns), BF)] * 2,
        compiler_params=pltpu.CompilerParams(vmem_limit_bytes=VMEM_BYTES),
        cost_estimate=takes(10),
        name="row_grad",
    )(core, *args, *order)


def body(
    block_in,
    out_grad,
    utt_ends,
    valid_ends,
    ffn1_in,
    ffn1_out,
    att_qkv,
    att_out,
    content_bias,
    conv_in,
    conv_out,
    ffn2_in,
    ffn2_out,
    conv_depth,
    norm_gain,
    norm_bias,
):
    zs = lax.axis_size("z")
    devices = 8 * zs
    frames, width = block_in.shape
    heads = width // DH
    z, x, y, c = (lax.axis_index(axis) for axis in DEV)
    place = ((z * 2 + x) * 2 + y) * 2 + c
    head = (x * 2 + y) * 2 + c

    small = jnp.concatenate([norm_gain, norm_bias, conv_depth, content_bias[None]], axis=0)
    small = jnp.broadcast_to(small[None], (devices,) + small.shape)
    small = lax.all_to_all(small, DEV, split_axis=0, concat_axis=0, tiled=True)
    small = small.transpose(1, 0, 2).reshape(small.shape[1], width).astype(F32)
    gains, shifts, taps, q_bias = small[:6], small[6:12], small[12 : 12 + KSIZE], small[12 + KSIZE]

    rows, few = ffn1_in.shape[0], att_qkv.shape[0]
    blocks = lambda w: [w[:, i : i + width] for i in range(0, w.shape[1], width)]

    def gather(*parts):
        mine = jnp.concatenate(parts, axis=0)
        return lax.all_gather(mine, DEV, axis=0, tiled=True).reshape(devices, -1, width)

    w_first = gather(pack_ffn(ffn1_in, ffn1_out), *blocks(att_qkv))
    w_mid = gather(att_out, *blocks(conv_in), conv_out)
    w_second = gather(pack_ffn(ffn2_in, ffn2_out, order=(small,)))
    w_proj = Rows(w_first, 2 * rows, few)
    w_conv = Rows(w_mid, 0, few)
    w_cout = Rows(w_mid, 3 * few, few)
    core = c.astype(jnp.int32)[None]

    all_frames = frames * devices
    first_frame = place * frames
    span = 4 * frames
    group = 8 * frames
    origin = span
    group_first = z * group
    starts = jnp.concatenate([jnp.zeros((1,), jnp.int32), utt_ends[:-1]])
    valid_count = jnp.sum((valid_ends - starts).astype(F32))

    def segments(positions):
        seg = jnp.sum((utt_ends[None, :] <= positions[:, None]).astype(jnp.int32), axis=1)
        valid_seg = jnp.sum((valid_ends[None, :] <= positions[:, None]).astype(jnp.int32), axis=1)
        valid = seg == valid_seg
        return jnp.where(positions < 0, -1, jnp.where(positions >= all_frames, -2, seg)), valid

    ext_seg, ext_valid = segments(
        first_frame - REACH + jnp.arange(frames + 2 * REACH, dtype=jnp.int32)
    )
    own_seg = ext_seg[REACH : REACH + frames]
    ext_valid = ext_valid.astype(F32)
    edge_valid = jnp.concatenate([ext_valid[:REACH], ext_valid[-REACH:]])
    edge_valid = jnp.concatenate([edge_valid, jnp.zeros((frames - 2 * REACH,), F32)])
    columns = jnp.stack(
        [(ext_seg[m : m + frames] == own_seg).astype(F32) for m in range(KSIZE)]
        + [ext_valid[REACH : REACH + frames], edge_valid, jnp.zeros((frames,), F32)],
        axis=1,
    )
    group_pos = group_first + jnp.arange(group, dtype=jnp.int32)
    ended = utt_ends[None, :] <= group_pos[:, None]
    group_seg = jnp.sum(ended.astype(jnp.int32), axis=1)
    group_lo = jnp.max(jnp.where(ended, utt_ends[None, :], 0), axis=1)
    slots = jnp.arange(utt_ends.shape[0], dtype=jnp.int32)
    group_hi = jnp.sum(
        jnp.where(group_seg[:, None] == slots[None, :], valid_ends[None, :], 0), axis=1
    )
    window_first = group_first - origin
    lo_q = group_lo - window_first
    hi_q = group_hi - window_first
    low = (lo_q[::BQ] // 128) * 128
    high = hi_q[BQ - 1 :: BQ]
    lo_q = lo_q.astype(F32)[None, :]
    hi_q = hi_q.astype(F32)[None, :]
    c2 = (32.0 * jnp.exp2(-head.astype(F32)) * (LOG2E / span))[None]

    def vectors(*rows):
        rows = jnp.stack(rows)
        return jnp.concatenate([rows, jnp.zeros((-len(rows) % 8, width), F32)], axis=0)

    count_row = jnp.broadcast_to(valid_count, (width,))

    x1, n2, pack1, s1, d1, q_heads, k_heads, v_heads = first_call(
        core,
        block_in,
        w_first,
        rows,
        w_proj,
        vectors(gains[0], shifts[0], gains[1], shifts[1], q_bias),
    )
    pack1_sib = xor_send(pack1, "c", 1)

    def to_heads(cells):
        got = lax.all_to_all(cells, LAYER, split_axis=0, concat_axis=0, tiled=True)
        return got.reshape(group, cells.shape[2])

    def to_frames(cells):
        cells = cells.reshape(heads, frames, cells.shape[1])
        return lax.all_to_all(cells, LAYER, split_axis=0, concat_axis=0, tiled=True)

    up = [(i, i + 1) for i in range(zs - 1)]
    down = [(i + 1, i) for i in range(zs - 1)]

    def with_edges(cells):
        return lax.ppermute(cells[-span:], "z", up), cells, lax.ppermute(cells[:span], "z", down)

    kv = with_edges(to_heads(k_heads)) + with_edges(to_heads(v_heads))
    q_own = to_heads(q_heads)
    o_own, lse = attn_fwd(q_own, kv, low, high, c2, lo_q, hi_q, origin)
    mixed, x2, n3, lin, sig, gated = gate_call(
        to_frames(o_own), x1, w_conv, vectors(gains[2], shifts[2]), columns, (pack1_sib,)
    )
    g_edges = neighbour_rows(gated)
    tap_rows = [taps[m] for m in range(KSIZE)]
    conv, moments = conv_call(gated, *g_edges, vectors(*tap_rows), columns, devices)
    spread = lambda cells: lax.all_to_all(cells, DEV, split_axis=0, concat_axis=0, tiled=True)
    moments = spread(moments)

    final_out, swished, dx3, ew, dz, sums_c, totals, pack2, s2, da2 = second_call(
        core,
        x2,
        conv,
        moments,
        w_cout,
        w_second,
        rows,
        vectors(gains[3], shifts[3], gains[4], shifts[4], gains[5], shifts[5], count_row),
        out_grad,
    )
    totals = spread(totals)
    edges = neighbour_rows(jnp.concatenate([dz[-REACH:], conv[-REACH:]]), jnp.concatenate([dz[:REACH], conv[:REACH]]))
    pack2_sib = xor_send(pack2, "c", 1)
    hidden = pack2.shape[2]
    f2i = slab_sum((pack2, pack2_sib, 0), (da2, pack2_sib, 4), "x")
    f2o = slab_sum((pack2, pack2_sib, 3), (s2, pack2_sib, 1), "y")

    point_grad, dx2, ey, mixed_grad, sums_b = back_call(
        dz,
        conv,
        edges,
        gated,
        g_edges,
        moments,
        totals,
        lin,
        sig,
        x2,
        dx3,
        w_conv,
        vectors(*tap_rows, gains[3], gains[2], gains[2], count_row),
        columns,
        order=(f2i.send, f2o.send),
    )
    do_own = to_heads(mixed_grad)
    send, kept = row_grad(core, [(mixed, ey), (n3, point_grad), (swished, ew)])
    mid = Sum(kept, send, "c", 1)
    dq, dkv_prev, dkv, dkv_next = attn_bwd(
        q_own,
        o_own,
        do_own,
        lse,
        kv,
        low,
        high,
        c2,
        lo_q,
        hi_q,
        origin,
        order=(f2i.kept, f2o.kept, kept),
    )
    dq = to_frames(dq)
    f2i = slab_second(f2i, "x")
    f2o = slab_second(f2o, "y", order=(f2i.send,))
    dkv = join_edges(
        dkv,
        lax.ppermute(dkv_next, "z", up),
        lax.ppermute(dkv_prev, "z", down),
        order=(f2i.send, f2o.send),
    )
    dkv = to_frames(dkv)

    low_z, high_z = z_bits()[:1], z_bits()[1:]
    dx1, ef1, sums_p = proj_back_call(dq, dkv, dx2, x1, w_proj, vectors(gains[0], gains[1]), ())
    ef1_sib = xor_send(ef1, "c", 1)
    send, kept = row_grad(core, [(n2, dq), (n2, dkv)], order=(ef1,))
    qkv = Sum(kept, send, "c", 1)
    f1o_left, f1o_right = (ef1, ef1_sib, 0), (s1, pack1_sib, 1)
    f1o_away = slab_grad(f1o_left, f1o_right, None, 1 - y, (qkv.send,))
    mid = mid.step((zs, 2, 2 * few, 4 * width), "x", order=(f1o_away,))
    f2 = z_both(f2i, f2o, rows, hidden, order=(mid.send,))
    grad_input, sums_a, da_first, da_second, da1 = last_call(
        core,
        dx1,
        ef1,
        block_in,
        w_first,
        rows,
        d1,
        vectors(gains[0]),
        order=(f2.send,),
    )
    da_sib = (xor_send(da_first, "c", 1), xor_send(da_second, "c", 1))
    f2 = z_steps(f2, 2 * rows, hidden, high_z, order=(da1,))
    f1o = Sum(slab_grad(f1o_left, f1o_right, None, y, (f2.send,), 10), f1o_away, "y", 1)
    f1i = slab_sum((pack1, pack1_sib, 0), (da1, da_sib, 0), "x", order=(f1o.kept,))
    grad_f2i, grad_f2o = finish_both(f2, rows, hidden, order=(f1i.kept,))
    qkv = z_steps(qkv, 4 * few, 3 * width, low_z, order=(grad_f2i,))
    f1o = slab_second(f1o, "y", order=(qkv.send,))
    mid = mid.step((zs, 2, few, 4 * width), "y", order=(f1o.send,))
    qkv = qkv.step((zs // 2, 2, 2 * few, 3 * width), "x", order=(mid.send,))
    mid = z_steps(mid, few, 4 * width, low_z, order=(qkv.send,))
    f1i = slab_second(f1i, "x", order=(mid.send,))
    f1o = z_steps(f1o, rows, hidden, low_z, order=(f1i.send,))
    mid = z_steps(mid, few, 4 * width, high_z, order=(f1o.send,))
    f1i = z_steps(f1i, rows, hidden, low_z, order=(mid.send,))
    f1o = z_steps(f1o, rows, hidden, high_z, order=(f1i.send,))
    mid = mid.finish((few, 4 * width), order=(f1o.send,))
    out_att, out_cin, out_cout = mid[:, :width], mid[:, width : 3 * width], mid[:, 3 * width :]
    qkv = qkv.step((zs // 2, 2, few, 3 * width), "y", order=(mid,))
    f1i = z_steps(f1i, rows, hidden, high_z, order=(qkv.send,))
    a, b, c, p = 0, 1, 2, 3
    places = [(a, 0), (p, 0), (b, 0), (c, 4), (c, 2), (c, 0)]
    places += [(a, 1), (p, 1), (b, 1), (c, 5), (c, 3), (c, 1)]
    places += [(b, 2 + m) for m in range(KSIZE)] + [(p, 2)]
    sums = stack_rows([sums_a, sums_b, sums_c, sums_p], places, devices, order=(f1i.send,))
    qkv = z_steps(qkv, few, 3 * width, high_z, order=(sums,))
    grad_f1o = f1o.finish((rows, hidden), True, order=(qkv.send,))
    grad_f1i = f1i.finish((rows, hidden), order=(grad_f1o,))
    out_qkv = qkv.finish((few, 3 * width), order=(grad_f1i,))
    sums = lax.all_to_all(sums, DEV, split_axis=0, concat_axis=0, tiled=True)
    gain_sums, bias_sums, tap_sums, query_sums = total_of(
        sums, (6, 6, KSIZE, 1), order=(out_qkv,)
    )

    return (
        final_out,
        grad_input,
        grad_f1i,
        grad_f1o,
        out_qkv,
        out_att,
        query_sums[0],
        out_cin,
        out_cout,
        grad_f2i,
        grad_f2o,
        tap_sums,
        gain_sums,
        bias_sums,
    )


def solution(mesh):
    seq, heads = mesh.shape["seq"], mesh.shape["head"]
    grid = Mesh(mesh.devices.reshape(seq // 2, 2, heads // 2, 2), DEV)
    both = P(DEV, None)
    inward = P(("z", "x"), ("y", "c"))
    outward = P(("y", "c"), ("z", "x"))
    columns = P(None, DEV)
    return jax.shard_map(
        body,
        mesh=grid,
        in_specs=(
            both,
            both,
            P(),
            P(),
            inward,
            outward,
            both,
            both,
            P(DEV),
            both,
            both,
            inward,
            outward,
            columns,
            columns,
            columns,
        ),
        out_specs=(
            both,
            both,
            inward,
            outward,
            both,
            both,
            P(DEV),
            both,
            both,
            inward,
            outward,
            columns,
            columns,
            columns,
        ),
        check_vma=False,
    )
```
